512 devices in a mesh: lat: 16 (over x_hi, z), lon: 32 (over y, x_lo, core).
Axes of the slice: x: 4 (x_hi: 2, x_lo: 2; x = x_hi * 2 + x_lo), y: 8, z: 8, core: 2. Of those that a mesh axis runs over, the one named last changes fastest.
Arguments:
- fields: bfloat16 [192, 2, 512, 512], P('lat', None, 'lon'), may hold values from -6 to 6
- land_ids: int32 [192, 512], P('lat', 'lon'), may hold values from 0 to 2
- surface_table: bfloat16 [3, 512], replicated, may hold values from -6 to 6
- level_table: bfloat16 [2, 512], replicated, may hold values from -6 to 6
- norm_first: float32 [512], replicated, may hold values from 0.5 to 1.5
- qkv_first: bfloat16 [3, 512, 512], replicated, may hold values from -2 to 2
- out_first: bfloat16 [512, 512], P('lat'), may hold values from -0.25 to 0.25
- norm_merge2: float32 [2048], replicated, may hold values from 0.5 to 1.5
- merge_second: bfloat16 [2048, 1024], P('lat'), may hold values from -0.125 to 0.125
- norm_merge3: float32 [4096], replicated, may hold values from 0.5 to 1.5
- merge_third: bfloat16 [4096, 2048], P(None, 'lat'), may hold values from -0.09375 to 0.09375
- norm_third: float32 [2048], replicated, may hold values from 0.5 to 1.5
- qkv_third: bfloat16 [3, 2048, 1024], P(None, None, 'lat'), may hold values from -2 to 2
- out_third: bfloat16 [1024, 2048], P('lat'), may hold values from -0.1875 to 0.1875
- up_third: bfloat16 [2048, 1024], P('lat'), may hold values from -0.125 to 0.125
- up_second: bfloat16 [1024, 512], P('lat'), may hold values from -0.1875 to 0.1875
Outputs:
- decoded: bfloat16 [192, 2, 512, 512], P('lat', None, 'lon')
The draws below stay inside these ranges and needn't reach their ends.
All inputs are finite; a program needn't handle non-finite values.
Results may differ from the reference program's by a relative error of at most 0.02.
Values may be sent and summed in bfloat16 or wider, within the bound.
No kernel may reach another device: no remote copies, remote signals or barrier semaphores. Data moves between devices by JAX's collectives and lax.ppermute only.
A program may use at most 64 MiB of HBM per device.

```python
import jax
import jax.numpy as jnp
from jax import lax

C1 = 512
C2 = 1024
C3 = 2048
HD = 64
NH3 = 16
Z = 2
NLAT = 192
NLON = 512
HF = 1024
N_LAT = 16


def projection_table(key, fan_in, out_dim):
    key_one, key_two, key_three = jax.random.split(key, 3)
    scale = fan_in ** (-0.5)
    query_part = jax.random.normal(key_one, (fan_in, out_dim), jnp.float32) * scale
    key_own = jax.random.normal(key_two, (fan_in, out_dim), jnp.float32) * scale
    value_part = jax.random.normal(key_three, (fan_in, out_dim), jnp.float32) * scale
    key_part = key_own
    table = jnp.stack([query_part, key_part, value_part])
    return jnp.clip(table, -2.0, 2.0).astype(jnp.bfloat16)


def draw_qkv_first(key, part):
    key = jax.random.fold_in(key, 7)
    return projection_table(key, C1, C1)


def draw_qkv_third(key, part):
    key = jax.random.fold_in(key, 13)
    return projection_table(key, C3, NH3 * HD)


def with_ends(result, stream_key, least, high):
    longest = result.shape.index(max(result.shape))
    spots = []
    for shift in (0, 1):
        where = [jax.random.randint(jax.random.fold_in(stream_key, axis), (), 0, length) for axis, length in enumerate(result.shape)]
        where[longest] = (where[longest] + shift) % result.shape[longest]
        spots.append(tuple(where))
    return result.at[spots[0]].set(least).at[spots[1]].set(high)


def steps_of(stream_key, shape, pieces, low, high):
    level, own = 1.0, jax.random.fold_in(stream_key, 6)
    for axis_at, parts in pieces:
        steps = jnp.exp(jax.random.uniform(jax.random.fold_in(own, axis_at), (parts,), jnp.float32, low / len(pieces), high / len(pieces)))
        level = level * jnp.repeat(steps, shape[axis_at] // parts).reshape([-1 if axis == axis_at else 1 for axis in range(len(shape))])
    return level


def bell_draw(own_key, dims, deviation, limit, cuts=(), kind=jnp.bfloat16):
    level = steps_of(own_key, dims, cuts, -0.22, 0.18) if cuts else 1.0
    drawn = jax.random.normal(own_key, dims, jnp.float32) * deviation * level
    return jnp.minimum(jnp.maximum(drawn, -limit), limit).astype(kind)


def setup_inputs(seed: int = 0) -> dict:
    arg_keys = jax.random.split(jax.random.key(seed), 17)
    return {
        "fields": bell_draw(arg_keys[0], (NLAT, Z, NLON, C1), 1.0, 6.0, ((0, 16), (2, 32))),
        "land_ids": with_ends(jax.random.randint(arg_keys[1], (NLAT, NLON), 0, 3), jax.random.fold_in(arg_keys[1], 1), 0, 2).astype(jnp.int32),
        "surface_table": bell_draw(arg_keys[2], (3, C1), 1.0, 6.0),
        "level_table": bell_draw(arg_keys[3], (Z, C1), 1.0, 6.0),
        "norm_first": jnp.clip(1.0 + 0.1 * jax.random.normal(arg_keys[4], (C1,), jnp.float32), 0.5, 1.5),
        "qkv_first": draw_qkv_first(jax.random.fold_in(arg_keys[16], 71), 0),
        "out_first": bell_draw(arg_keys[6], (C1, C1), C1 ** -0.5, 0.25, ((0, 16),)),
        "norm_merge2": jnp.clip(1.0 + 0.1 * jax.random.normal(arg_keys[7], (4 * C1,), jnp.float32), 0.5, 1.5),
        "merge_second": bell_draw(arg_keys[8], (4 * C1, C2), (4 * C1) ** -0.5, 0.125, ((0, 16),)),
        "norm_merge3": jnp.clip(1.0 + 0.1 * jax.random.normal(arg_keys[9], (4 * C2,), jnp.float32), 0.5, 1.5),
        "merge_third": bell_draw(arg_keys[10], (4 * C2, C3), (4 * C2) ** -0.5, 0.09375, ((1, 16),)),
        "norm_third": jnp.clip(1.0 + 0.1 * jax.random.normal(arg_keys[11], (C3,), jnp.float32), 0.5, 1.5),
        "qkv_third": draw_qkv_third(jax.random.fold_in(arg_keys[16], 71), 0),
        "out_third": bell_draw(arg_keys[13], (HF, C3), HF ** -0.5, 0.1875, ((0, 16),)),
        "up_third": bell_draw(arg_keys[14], (C3, C2), C3 ** -0.5, 0.125, ((0, 16),)),
        "up_second": bell_draw(arg_keys[15], (C2, C1), C2 ** -0.5, 0.1875, ((0, 16),)),
    }


def norm_rows(values, gain):
    row_mean = lax.optimization_barrier(jnp.mean(values, axis=-1, keepdims=True))
    centred = values - row_mean
    spread = lax.optimization_barrier(jnp.mean(centred * centred, axis=-1, keepdims=True))
    return centred * lax.rsqrt(spread + 1e-05) * gain

def split_quads(cell_grid):
    lat_count, levels, lon_count, feat_dim = cell_grid.shape
    blocks = cell_grid.reshape(lat_count // 2, 2, levels, lon_count // 2, 2, feat_dim)
    return blocks.transpose(0, 2, 3, 1, 4, 5).reshape(lat_count // 2, levels, lon_count // 2, 4 * feat_dim)

def spread_quads(cell_grid):
    lat_count, levels, lon_count, feat_dim = cell_grid.shape
    widened = jnp.broadcast_to(cell_grid[:, None, :, :, None, :], (lat_count, 2, levels, lon_count, 2, feat_dim))
    return widened.reshape(2 * lat_count, levels, 2 * lon_count, feat_dim)

def to_windows(cell_grid):
    lat_count, levels, lon_count, feat_dim = cell_grid.shape
    blocks = cell_grid.reshape(lat_count // 4, 4, levels, lon_count // 4, 4, feat_dim).transpose(0, 3, 1, 2, 4, 5)
    return blocks.reshape(lat_count // 4 * (lon_count // 4), 16 * levels, feat_dim)

def from_windows(windows, lat_count, levels, lon_count):
    feat_dim = windows.shape[-1]
    blocks = windows.reshape(lat_count // 4, lon_count // 4, 4, levels, 4, feat_dim).transpose(0, 2, 3, 1, 4, 5)
    return blocks.reshape(lat_count, levels, lon_count, feat_dim)

def attend(query_in, key_in, value_in, head_count, key_mask):
    win_count, win_tokens, feat_dim = query_in.shape
    head_width = feat_dim // head_count
    query_heads = query_in.astype(jnp.float32).reshape(win_count, win_tokens, head_count, head_width)
    key_heads = key_in.astype(jnp.float32).reshape(win_count, win_tokens, head_count, head_width)
    value_heads = value_in.astype(jnp.float32).reshape(win_count, win_tokens, head_count, head_width)
    scores = jnp.einsum('wqhd,wkhd->whqk', query_heads, key_heads) * head_width ** (-0.5)
    if key_mask is not None:
        scores = jnp.where(key_mask[:, None, None, :], scores, -1e+30)
    row_peak = lax.optimization_barrier(jnp.max(scores, axis=-1, keepdims=True))
    weights = jnp.exp(scores - row_peak)
    prob_bf = (weights / lax.optimization_barrier(jnp.sum(weights, axis=-1, keepdims=True))).astype(jnp.bfloat16)
    mixed_out = jnp.einsum('whqk,wkhd->wqhd', prob_bf.astype(jnp.float32), value_heads)
    return mixed_out.astype(jnp.bfloat16).reshape(win_count, win_tokens, feat_dim)

def project(flat_rows, matrix):
    return jnp.dot(flat_rows, matrix, preferred_element_type=jnp.float32)

def reference(fields, land_ids, surface_table, level_table, norm_first, qkv_first, out_first, norm_merge2, merge_second, norm_merge3, merge_third, norm_third, qkv_third, out_third, up_third, up_second):
    lat_cells, levels, lon_cells, feat_dim = fields.shape
    picks = (land_ids[:, :, None] == jnp.arange(3, dtype=jnp.int32)).astype(jnp.float32)
    surface = jnp.einsum('ijs,sc->ijc', picks, surface_table.astype(jnp.float32))
    hidden = (fields.astype(jnp.float32) + surface[:, None, :, :] + level_table.astype(jnp.float32)[None, :, None, :]).astype(jnp.bfloat16)
    normed = norm_rows(hidden.astype(jnp.float32), norm_first).astype(jnp.bfloat16).reshape(-1, feat_dim)
    triple = jnp.stack([project(normed, qkv_first[component]).astype(jnp.bfloat16) for component in range(3)])
    triple = triple.reshape(3, lat_cells, levels, lon_cells, feat_dim)
    padded = jnp.pad(triple, ((0, 0), (2, 2), (0, 0), (0, 0), (0, 0)))
    rolled = jnp.roll(padded, 2, axis=3)
    ext_rows = lat_cells + 4
    row_index = jnp.arange(ext_rows)
    valid_rows = (row_index >= 2) & (row_index < lat_cells + 2)
    mask_grid = jnp.broadcast_to(valid_rows[:, None, None, None], (ext_rows, levels, lon_cells, 1))
    key_mask = to_windows(mask_grid)[:, :, 0]
    window_parts = [to_windows(rolled[component]) for component in range(3)]
    mixed_out = attend(window_parts[0], window_parts[1], window_parts[2], feat_dim // HD, key_mask)
    attended = jnp.roll(from_windows(mixed_out, ext_rows, levels, lon_cells), -2, axis=2)[2:lat_cells + 2]
    projected = project(attended.reshape(-1, feat_dim), out_first).reshape(hidden.shape)
    skip_first = (hidden.astype(jnp.float32) + projected).astype(jnp.bfloat16)
    quads = split_quads(skip_first)
    merged_in = norm_rows(quads.astype(jnp.float32), norm_merge2).astype(jnp.bfloat16)
    second_grid = project(merged_in.reshape(-1, quads.shape[-1]), merge_second).astype(jnp.bfloat16)
    second_grid = second_grid.reshape(lat_cells // 2, levels, lon_cells // 2, -1)
    quads_coarse = split_quads(second_grid)
    coarse_in = norm_rows(quads_coarse.astype(jnp.float32), norm_merge3).astype(jnp.bfloat16).reshape(-1, quads_coarse.shape[-1])
    coarse_full = project(coarse_in, merge_third).astype(jnp.bfloat16)
    normed_coarse = norm_rows(coarse_full.astype(jnp.float32), norm_third).astype(jnp.bfloat16)
    head_feats = qkv_third.shape[2]
    triple_coarse = jnp.stack([project(normed_coarse, qkv_third[component]).astype(jnp.bfloat16) for component in range(3)])
    triple_coarse = triple_coarse.reshape(3, lat_cells // 4, levels, lon_cells // 4, head_feats)
    coarse_parts = [to_windows(triple_coarse[component]) for component in range(3)]
    mixed_coarse = attend(coarse_parts[0], coarse_parts[1], coarse_parts[2], head_feats // HD, None)
    heads_out = from_windows(mixed_coarse, lat_cells // 4, levels, lon_cells // 4).reshape(-1, head_feats)
    block_width = head_feats // N_LAT
    running = coarse_full.astype(jnp.float32)
    for block_index in range(N_LAT):
        first = block_index * block_width
        head_part = project(heads_out[:, first:first + block_width], out_third[first:first + block_width]).astype(jnp.bfloat16)
        head_part = lax.optimization_barrier(head_part)
        running = running + head_part.astype(jnp.float32)
    level_three = running.astype(jnp.bfloat16)
    lift_three = project(level_three, up_third).reshape(lat_cells // 4, levels, lon_cells // 4, -1)
    level_two = (second_grid.astype(jnp.float32) + spread_quads(lift_three)).astype(jnp.bfloat16)
    lift_two = project(level_two.reshape(-1, level_two.shape[-1]), up_second).reshape(lat_cells // 2, levels, lon_cells // 2, -1)
    return (skip_first.astype(jnp.float32) + spread_quads(lift_two)).astype(jnp.bfloat16)
```

```python
import jax
import jax.numpy as jnp
from jax import lax
from jax.sharding import PartitionSpec as P

HD = 64


def with_halo(cells, sides, width):
    for axis, dim in sides:
        count = lax.axis_size(axis)
        head = lax.slice_in_dim(cells, 0, width, axis=dim)
        tail = lax.slice_in_dim(cells, cells.shape[dim] - width, cells.shape[dim], axis=dim)
        cells = jnp.concatenate(
            [
                lax.ppermute(tail, axis, [(i, (i + 1) % count) for i in range(count)]),
                cells,
                lax.ppermute(head, axis, [((i + 1) % count, i) for i in range(count)]),
            ],
            axis=dim,
        )
    return cells


def norm_rows(values, gain):
    row_mean = jnp.mean(values, axis=-1, keepdims=True)
    centred = values - row_mean
    spread = jnp.mean(centred * centred, axis=-1, keepdims=True)
    return centred * lax.rsqrt(spread + 1e-05) * gain


def split_quads(cell_grid):
    lat_count, levels, lon_count, feat_dim = cell_grid.shape
    blocks = cell_grid.reshape(lat_count // 2, 2, levels, lon_count // 2, 2, feat_dim)
    return blocks.transpose(0, 2, 3, 1, 4, 5).reshape(
        lat_count // 2, levels, lon_count // 2, 4 * feat_dim
    )


def spread_quads(cell_grid):
    lat_count, levels, lon_count, feat_dim = cell_grid.shape
    widened = jnp.broadcast_to(
        cell_grid[:, None, :, :, None, :], (lat_count, 2, levels, lon_count, 2, feat_dim)
    )
    return widened.reshape(2 * lat_count, levels, 2 * lon_count, feat_dim)


def to_windows(cell_grid):
    lat_count, levels, lon_count, feat_dim = cell_grid.shape
    blocks = cell_grid.reshape(lat_count // 4, 4, levels, lon_count // 4, 4, feat_dim).transpose(
        0, 3, 1, 2, 4, 5
    )
    return blocks.reshape(lat_count // 4 * (lon_count // 4), 16 * levels, feat_dim)


def from_windows(windows, lat_count, levels, lon_count):
    feat_dim = windows.shape[-1]
    blocks = windows.reshape(lat_count // 4, lon_count // 4, 4, levels, 4, feat_dim).transpose(
        0, 2, 3, 1, 4, 5
    )
    return blocks.reshape(lat_count, levels, lon_count, feat_dim)


def attend(query_in, key_in, value_in, head_count, key_mask):
    win_count, win_tokens, feat_dim = query_in.shape
    head_width = feat_dim // head_count
    query_heads = query_in.reshape(win_count, win_tokens, head_count, head_width)
    key_heads = key_in.reshape(win_count, win_tokens, head_count, head_width)
    value_heads = value_in.reshape(win_count, win_tokens, head_count, head_width)
    scores = jnp.einsum(
        "wqhd,wkhd->whqk", query_heads, key_heads, preferred_element_type=jnp.float32
    ) * head_width ** (-0.5)
    if key_mask is not None:
        scores = jnp.where(key_mask[:, None, None, :], scores, -1e30)
    row_peak = jnp.max(scores, axis=-1, keepdims=True)
    weights = jnp.exp(scores - row_peak)
    prob_bf = (weights / jnp.sum(weights, axis=-1, keepdims=True)).astype(jnp.bfloat16)
    mixed_out = jnp.einsum(
        "whqk,wkhd->wqhd", prob_bf, value_heads, preferred_element_type=jnp.float32
    )
    return mixed_out.astype(jnp.bfloat16).reshape(win_count, win_tokens, feat_dim)


def project_three(normed_rows, tables):
    return jnp.stack(
        [
            jnp.dot(normed_rows, tables[component], preferred_element_type=jnp.float32).astype(
                jnp.bfloat16
            )
            for component in range(3)
        ]
    )


Z_RING = 8
RINGS = [[ring * Z_RING + place for place in range(Z_RING)] for ring in range(2)]


def swap_cores(values):
    count = lax.axis_size("lon")
    return lax.ppermute(values, "lon", [(i, i ^ 1) for i in range(count)])


def swap_rings(values):
    count = lax.axis_size("lat")
    return lax.ppermute(values, "lat", [(i, (i + Z_RING) % count) for i in range(count)])


def swap_shards(values):
    lon_count = lax.axis_size("lon")
    pairs = []
    for lat in range(lax.axis_size("lat")):
        for lon in range(lon_count):
            ring, place = divmod(lat, Z_RING)
            target = (lat, lon)
            if ring != lon % 2:
                target = ((1 - ring) * Z_RING + place, lon ^ 1)
            pairs.append((lat * lon_count + lon, target[0] * lon_count + target[1]))
    return lax.ppermute(values, ("lat", "lon"), pairs)


def ring_scatter(blocks):
    return lax.all_to_all(blocks, "lat", 0, 0, axis_index_groups=RINGS, tiled=True)


def ring_gather(values):
    return ring_scatter(jnp.broadcast_to(values[None], (Z_RING,) + values.shape))


def in_order(flag, own, other, axis):
    return jnp.where(
        flag == 0,
        jnp.concatenate([own, other], axis=axis),
        jnp.concatenate([other, own], axis=axis),
    )


def gather_weights(wide, narrow, ring, core):
    wide_rows, columns = wide.shape[0], wide.shape[1] // 2
    narrow_rows = narrow.shape[0] // 2
    own = jnp.concatenate(
        [
            lax.dynamic_slice_in_dim(wide, core * columns, columns, 1),
            lax.dynamic_slice_in_dim(narrow, core * narrow_rows, narrow_rows, 0),
        ],
        axis=0,
    )[None]
    both = in_order(ring, own, swap_rings(own), 0)
    mine = lax.all_gather(both, "lat", axis=1, axis_index_groups=RINGS, tiled=True)
    other = swap_cores(mine)
    split = [
        half.reshape(2, Z_RING, wide_rows + narrow_rows, columns) for half in (mine, other)
    ]
    wides = [half[:, :, :wide_rows].reshape(-1, columns) for half in split]
    narrows = [half[:, :, None, wide_rows:] for half in split]
    narrow_all = in_order(core, narrows[0], narrows[1], 2).reshape(-1, columns)
    return wides, narrow_all


def dot_halves(rows, halves, core):
    parts = [jnp.dot(rows, half, preferred_element_type=jnp.float32) for half in halves]
    return in_order(core, parts[0], parts[1], 1)


def on_device(
    fields,
    land_ids,
    surface_table,
    level_table,
    norm_first,
    qkv_first,
    out_first,
    norm_merge2,
    merge_second,
    norm_merge3,
    merge_third,
    norm_third,
    qkv_third,
    out_third,
    up_third,
    up_second,
):
    tile_rows, levels, tile_cols, feat_dim = fields.shape
    lat_count = lax.axis_size("lat")
    ring = lax.axis_index("lat") // Z_RING
    core = lax.axis_index("lon") % 2
    merge_second_halves, out_first_all = gather_weights(merge_second, out_first, ring, core)
    up_third_halves, up_second_all = gather_weights(up_third, up_second, ring, core)
    merge_third = swap_shards(merge_third)
    qkv_third = swap_shards(qkv_third)
    out_third = swap_shards(out_third)
    picks = (land_ids[:, :, None] == jnp.arange(3, dtype=jnp.int32)).astype(jnp.float32)
    surface = jnp.einsum("ijs,sc->ijc", picks, surface_table.astype(jnp.float32))
    hidden = (
        fields.astype(jnp.float32)
        + surface[:, None, :, :]
        + level_table.astype(jnp.float32)[None, :, None, :]
    ).astype(jnp.bfloat16)
    ext_rows = tile_rows + 4
    ext_cols = tile_cols + 4
    grown = with_halo(hidden, (("lat", 0), ("lon", 2)), 2)
    normed = (
        norm_rows(grown.astype(jnp.float32), norm_first).astype(jnp.bfloat16).reshape(-1, feat_dim)
    )
    triple = project_three(normed, qkv_first).reshape(3, ext_rows, levels, ext_cols, feat_dim)
    lat_place = lax.axis_index("lat") * tile_rows + jnp.arange(ext_rows) - 2
    valid_rows = (lat_place >= 0) & (lat_place < tile_rows * lat_count)
    mask_grid = jnp.broadcast_to(valid_rows[:, None, None, None], (ext_rows, levels, ext_cols, 1))
    key_mask = to_windows(mask_grid)[:, :, 0]
    window_parts = [to_windows(triple[component]) for component in range(3)]
    mixed_out = attend(window_parts[0], window_parts[1], window_parts[2], feat_dim // HD, key_mask)
    attended = from_windows(mixed_out, ext_rows, levels, ext_cols)[
        2 : tile_rows + 2, :, 2 : tile_cols + 2, :
    ]
    projected = jnp.dot(
        attended.reshape(-1, feat_dim), out_first_all, preferred_element_type=jnp.float32
    ).reshape(hidden.shape)
    skip_first = (hidden.astype(jnp.float32) + projected).astype(jnp.bfloat16)
    quads = split_quads(skip_first)
    merged_in = norm_rows(quads.astype(jnp.float32), norm_merge2).astype(jnp.bfloat16)
    second_grid = dot_halves(
        merged_in.reshape(-1, quads.shape[-1]), merge_second_halves, core
    ).astype(jnp.bfloat16)
    second_grid = second_grid.reshape(tile_rows // 2, levels, tile_cols // 2, -1)
    quads_coarse = split_quads(second_grid)
    coarse_in = (
        norm_rows(quads_coarse.astype(jnp.float32), norm_merge3)
        .astype(jnp.bfloat16)
        .reshape(-1, quads_coarse.shape[-1])
    )
    own_count = coarse_in.shape[0]
    line = Z_RING * own_count

    ring_tokens = ring_gather(coarse_in).reshape(line, -1)
    column_block = jnp.stack(
        [
            jnp.dot(tokens, merge_third, preferred_element_type=jnp.float32).astype(jnp.bfloat16)
            for tokens in (ring_tokens, swap_cores(ring_tokens))
        ]
    )
    own_columns = ring_gather(column_block).transpose(1, 2, 0, 3).reshape(2, line, -1)
    other_columns = swap_cores(own_columns)[::-1]
    coarse_full = jnp.concatenate([own_columns, other_columns], axis=-1)
    half = own_columns.shape[-1]
    gain_third = in_order(core, norm_third[:half], norm_third[half:], 0)
    qkv_rolled = in_order(core, qkv_third[:, :half], qkv_third[:, half:], 1)
    normed_coarse = norm_rows(coarse_full.astype(jnp.float32), gain_third).astype(jnp.bfloat16)
    head_feats = qkv_third.shape[2]
    triple_coarse = project_three(normed_coarse.reshape(2 * line, -1), qkv_rolled)
    coarse_parts = triple_coarse.reshape(3, -1, 16 * levels, head_feats)
    heads_out = attend(
        coarse_parts[0], coarse_parts[1], coarse_parts[2], head_feats // HD, None
    ).reshape(2, line, head_feats)
    head_part = jnp.dot(heads_out, out_third, preferred_element_type=jnp.float32)
    chip_part = head_part[0] + swap_cores(head_part[1].astype(jnp.bfloat16)).astype(jnp.float32)
    update = jnp.sum(
        ring_scatter(chip_part.astype(jnp.bfloat16).reshape(Z_RING, own_count, -1)).astype(
            jnp.float32
        ),
        axis=0,
    )
    place = lax.axis_index("lat") % Z_RING
    own_coarse = lax.dynamic_slice_in_dim(coarse_full[0], place * own_count, own_count, 0)
    own_coarse = in_order(core, own_coarse[:, :half], own_coarse[:, half:], 1)
    level_three = (own_coarse.astype(jnp.float32) + update).astype(jnp.bfloat16)
    lift_three = dot_halves(level_three, up_third_halves, core).reshape(
        tile_rows // 4, levels, tile_cols // 4, -1
    )
    level_two = (second_grid.astype(jnp.float32) + spread_quads(lift_three)).astype(jnp.bfloat16)
    lift_two = jnp.dot(
        level_two.reshape(-1, level_two.shape[-1]),
        up_second_all,
        preferred_element_type=jnp.float32,
    ).reshape(tile_rows // 2, levels, tile_cols // 2, -1)
    return (skip_first.astype(jnp.float32) + spread_quads(lift_two)).astype(jnp.bfloat16)


def solution(mesh):
    in_specs = (
        P("lat", None, "lon", None),
        P("lat", "lon"),
        P(),
        P(),
        P(),
        P(),
        P("lat", None),
        P(),
        P("lat", None),
        P(),
        P(None, "lat"),
        P(),
        P(None, None, "lat"),
        P("lat", None),
        P("lat", None),
        P("lat", None),
    )
    out_specs = P("lat", None, "lon", None)
    return jax.shard_map(
        on_device, mesh=mesh, in_specs=in_specs, out_specs=out_specs, check_vma=False
    )
```

```python
import jax
import jax.numpy as jnp
from jax import lax
from jax.sharding import PartitionSpec as P

HD = 64


def with_halo(cells, sides, width):
    for axis, dim in sides:
        count = lax.axis_size(axis)
        head = lax.slice_in_dim(cells, 0, width, axis=dim)
        tail = lax.slice_in_dim(cells, cells.shape[dim] - width, cells.shape[dim], axis=dim)
        cells = jnp.concatenate(
            [
                lax.ppermute(tail, axis, [(i, (i + 1) % count) for i in range(count)]),
                cells,
                lax.ppermute(head, axis, [((i + 1) % count, i) for i in range(count)]),
            ],
            axis=dim,
        )
    return cells


def norm_rows(values, gain):
    row_mean = jnp.mean(values, axis=-1, keepdims=True)
    centred = values - row_mean
    spread = jnp.mean(centred * centred, axis=-1, keepdims=True)
    return centred * lax.rsqrt(spread + 1e-05) * gain


def split_quads(cell_grid):
    lat_count, levels, lon_count, feat_dim = cell_grid.shape
    blocks = cell_grid.reshape(lat_count // 2, 2, levels, lon_count // 2, 2, feat_dim)
    return blocks.transpose(0, 2, 3, 1, 4, 5).reshape(
        lat_count // 2, levels, lon_count // 2, 4 * feat_dim
    )


def spread_quads(cell_grid):
    lat_count, levels, lon_count, feat_dim = cell_grid.shape
    widened = jnp.broadcast_to(
        cell_grid[:, None, :, :, None, :], (lat_count, 2, levels, lon_count, 2, feat_dim)
    )
    return widened.reshape(2 * lat_count, levels, 2 * lon_count, feat_dim)


def to_windows(cell_grid):
    lat_count, levels, lon_count, feat_dim = cell_grid.shape
    blocks = cell_grid.reshape(lat_count // 4, 4, levels, lon_count // 4, 4, feat_dim).transpose(
        0, 3, 1, 2, 4, 5
    )
    return blocks.reshape(lat_count // 4 * (lon_count // 4), 16 * levels, feat_dim)


def from_windows(windows, lat_count, levels, lon_count):
    feat_dim = windows.shape[-1]
    blocks = windows.reshape(lat_count // 4, lon_count // 4, 4, levels, 4, feat_dim).transpose(
        0, 2, 3, 1, 4, 5
    )
    return blocks.reshape(lat_count, levels, lon_count, feat_dim)


def attend(query_in, key_in, value_in, head_count, key_mask):
    win_count, win_tokens, feat_dim = query_in.shape
    head_width = feat_dim // head_count
    query_heads = query_in.reshape(win_count, win_tokens, head_count, head_width)
    key_heads = key_in.reshape(win_count, win_tokens, head_count, head_width)
    value_heads = value_in.reshape(win_count, win_tokens, head_count, head_width)
    scores = jnp.einsum(
        "wqhd,wkhd->whqk", query_heads, key_heads, preferred_element_type=jnp.float32
    ) * head_width ** (-0.5)
    if key_mask is not None:
        scores = jnp.where(key_mask[:, None, None, :], scores, -1e30)
    row_peak = jnp.max(scores, axis=-1, keepdims=True)
    weights = jnp.exp(scores - row_peak)
    prob_bf = (weights / jnp.sum(weights, axis=-1, keepdims=True)).astype(jnp.bfloat16)
    mixed_out = jnp.einsum(
        "whqk,wkhd->wqhd", prob_bf, value_heads, preferred_element_type=jnp.float32
    )
    return mixed_out.astype(jnp.bfloat16).reshape(win_count, win_tokens, feat_dim)


def project_three(normed_rows, tables):
    return jnp.stack(
        [
            jnp.dot(normed_rows, tables[component], preferred_element_type=jnp.float32).astype(
                jnp.bfloat16
            )
            for component in range(3)
        ]
    )


Z_RING = 8
RINGS = [[ring * Z_RING + place for place in range(Z_RING)] for ring in range(2)]


def swap_cores(values):
    count = lax.axis_size("lon")
    return lax.ppermute(values, "lon", [(i, i ^ 1) for i in range(count)])


def swap_rings(values):
    count = lax.axis_size("lat")
    return lax.ppermute(values, "lat", [(i, (i + Z_RING) % count) for i in range(count)])


def swap_shards(values):
    lon_count = lax.axis_size("lon")
    pairs = []
    for lat in range(lax.axis_size("lat")):
        for lon in range(lon_count):
            ring, place = divmod(lat, Z_RING)
            target = (lat, lon)
            if ring != lon % 2:
                target = ((1 - ring) * Z_RING + place, lon ^ 1)
            pairs.append((lat * lon_count + lon, target[0] * lon_count + target[1]))
    return lax.ppermute(values, ("lat", "lon"), pairs)


def ring_scatter(blocks):
    return lax.all_to_all(blocks, "lat", 0, 0, axis_index_groups=RINGS, tiled=True)


def ring_gather(values):
    return ring_scatter(jnp.broadcast_to(values[None], (Z_RING,) + values.shape))


def in_order(flag, own, other, axis):
    return jnp.where(
        flag == 0,
        jnp.concatenate([own, other], axis=axis),
        jnp.concatenate([other, own], axis=axis),
    )


def dot_halves(rows, halves, core):
    parts = [jnp.dot(rows, half, preferred_element_type=jnp.float32) for half in halves]
    return in_order(core, parts[0], parts[1], 1)


def cut(values, row, rows, column, columns):
    return lax.dynamic_slice(values, (row, column), (rows, columns))


def after(values, *before):
    return lax.optimization_barrier((values,) + before)[0]


def column_gather(values):
    groups = [[4 * y + x for y in range(8)] for x in range(4)]
    return lax.all_to_all(
        jnp.broadcast_to(values[None], (8,) + values.shape),
        "lon",
        0,
        0,
        axis_index_groups=groups,
        tiled=True,
    )


def on_device(
    fields,
    land_ids,
    surface_table,
    level_table,
    norm_first,
    qkv_first,
    out_first,
    norm_merge2,
    merge_second,
    norm_merge3,
    merge_third,
    norm_third,
    qkv_third,
    out_third,
    up_third,
    up_second,
):
    tile_rows, levels, tile_cols, feat_dim = fields.shape
    lat_count = lax.axis_size("lat")
    ring = lax.axis_index("lat") // Z_RING
    core = lax.axis_index("lon") % 2
    column = lax.axis_index("lon") // 4

    own_merge = lax.dynamic_slice_in_dim(merge_second, core * 512, 512, 1)[None]
    merge_half = lax.all_gather(
        in_order(ring, own_merge, swap_rings(own_merge), 0),
        "lat",
        axis=1,
        axis_index_groups=RINGS,
        tiled=True,
    ).reshape(-1, 512)

    own_rest = jnp.concatenate(
        [
            cut(out_first, column // 4 * 16, 16, column % 4 * 128, 128),
            cut(up_third, column * 16, 16, core * 512, 512),
            cut(up_second, column // 2 * 16, 16, core * 256 + column % 2 * 128, 128),
        ],
        axis=1,
    )[None]
    both_rest = in_order(ring, own_rest, swap_rings(own_rest), 0)
    out_first_tiles = column_gather(ring_gather(both_rest[:, :, :128]))
    out_first_all = (
        out_first_tiles.reshape(2, 4, Z_RING, 2, 16, 128)
        .transpose(3, 2, 0, 4, 1, 5)
        .reshape(feat_dim, feat_dim)
    )
    merge_third = swap_shards(merge_third)
    qkv_third = swap_shards(qkv_third)
    out_third = swap_shards(out_third)

    picks = (land_ids[:, :, None] == jnp.arange(3, dtype=jnp.int32)).astype(jnp.float32)
    surface = jnp.einsum("ijs,sc->ijc", picks, surface_table.astype(jnp.float32))
    hidden = (
        fields.astype(jnp.float32)
        + surface[:, None, :, :]
        + level_table.astype(jnp.float32)[None, :, None, :]
    ).astype(jnp.bfloat16)
    ext_rows = tile_rows + 4
    ext_cols = tile_cols + 4
    grown = with_halo(hidden, (("lat", 0), ("lon", 2)), 2)
    normed = (
        norm_rows(grown.astype(jnp.float32), norm_first).astype(jnp.bfloat16).reshape(-1, feat_dim)
    )
    triple = project_three(normed, qkv_first).reshape(3, ext_rows, levels, ext_cols, feat_dim)
    lat_place = lax.axis_index("lat") * tile_rows + jnp.arange(ext_rows) - 2
    valid_rows = (lat_place >= 0) & (lat_place < tile_rows * lat_count)
    mask_grid = jnp.broadcast_to(valid_rows[:, None, None, None], (ext_rows, levels, ext_cols, 1))
    key_mask = to_windows(mask_grid)[:, :, 0]
    window_parts = [to_windows(triple[component]) for component in range(3)]
    mixed_out = attend(window_parts[0], window_parts[1], window_parts[2], feat_dim // HD, key_mask)
    attended = from_windows(mixed_out, ext_rows, levels, ext_cols)[
        2 : tile_rows + 2, :, 2 : tile_cols + 2, :
    ]
    attended = after(attended, merge_third, qkv_third, out_third, out_first_all, both_rest)
    projected = jnp.dot(
        attended.reshape(-1, feat_dim), out_first_all, preferred_element_type=jnp.float32
    ).reshape(hidden.shape)
    skip_first = (hidden.astype(jnp.float32) + projected).astype(jnp.bfloat16)
    quads = split_quads(skip_first)
    merged_in = norm_rows(quads.astype(jnp.float32), norm_merge2).astype(jnp.bfloat16)
    merged_in = merged_in.reshape(-1, quads.shape[-1])
    merged_pair = jnp.concatenate([merged_in, swap_cores(merged_in)], axis=0)
    merge_half = after(merge_half, merged_pair)
    second_half = jnp.dot(merged_pair, merge_half, preferred_element_type=jnp.float32).astype(
        jnp.bfloat16
    )
    own_rows = merged_in.shape[0]
    second_grid = in_order(core, second_half[:own_rows], swap_cores(second_half[own_rows:]), 1)

    late = jnp.concatenate(
        [
            both_rest[0, :, 128:],
            both_rest[1, :, 128:],
            cut(out_third, column // 2 * 16, 16, column % 2 * 1024, 1024),
        ],
        axis=1,
    )
    late = ring_gather(after(late, merge_half))
    late = lax.all_gather(
        late,
        "lon",
        axis=0,
        axis_index_groups=[[4 * y + x for y in range(8)] for x in range(4)],
        tiled=True,
    ).reshape(8, Z_RING, 16, -1)

    second_grid = second_grid.reshape(tile_rows // 2, levels, tile_cols // 2, -1)
    quads_coarse = split_quads(second_grid)
    coarse_in = (
        norm_rows(quads_coarse.astype(jnp.float32), norm_merge3)
        .astype(jnp.bfloat16)
        .reshape(-1, quads_coarse.shape[-1])
    )
    own_count = coarse_in.shape[0]
    line = Z_RING * own_count

    ring_tokens = ring_gather(coarse_in).reshape(line, -1)
    column_block = jnp.stack(
        [
            jnp.dot(tokens, merge_third, preferred_element_type=jnp.float32).astype(jnp.bfloat16)
            for tokens in (ring_tokens, swap_cores(ring_tokens))
        ]
    )
    own_columns = ring_gather(column_block).transpose(1, 2, 0, 3).reshape(2, line, -1)
    other_columns = swap_cores(own_columns)[::-1]
    coarse_full = jnp.concatenate([own_columns, other_columns], axis=-1)
    half = own_columns.shape[-1]
    gain_third = in_order(core, norm_third[:half], norm_third[half:], 0)
    qkv_rolled = in_order(core, qkv_third[:, :half], qkv_third[:, half:], 1)
    normed_coarse = norm_rows(coarse_full.astype(jnp.float32), gain_third).astype(jnp.bfloat16)
    head_feats = qkv_third.shape[2]
    triple_coarse = project_three(normed_coarse.reshape(2 * line, -1), qkv_rolled)
    coarse_parts = triple_coarse.reshape(3, -1, 16 * levels, head_feats)
    heads_out = attend(
        coarse_parts[0], coarse_parts[1], coarse_parts[2], head_feats // HD, None
    ).reshape(2, Z_RING, own_count, head_feats)

    chip_heads = ring_scatter(heads_out.transpose(1, 0, 2, 3)).transpose(1, 2, 0, 3)
    chip_heads = chip_heads.reshape(2 * own_count, -1)
    out_third_half = (
        late[..., 1280:].reshape(4, 2, Z_RING, 16, 1024).transpose(2, 0, 3, 1, 4).reshape(512, 2048)
    )
    head_part = jnp.dot(chip_heads, out_third_half, preferred_element_type=jnp.float32)
    update = head_part[:own_count] + swap_cores(
        head_part[own_count:].astype(jnp.bfloat16)
    ).astype(jnp.float32)
    place = lax.axis_index("lat") % Z_RING
    own_coarse = lax.dynamic_slice_in_dim(coarse_full[0], place * own_count, own_count, 0)
    own_coarse = in_order(core, own_coarse[:, :half], own_coarse[:, half:], 1)
    level_three = (own_coarse.astype(jnp.float32) + update).astype(jnp.bfloat16)

    own_late = late[..., :1280].reshape(8, Z_RING, 16, 2, 640)
    other_late = swap_cores(own_late)
    up_third_halves = [
        tiles[..., :512].transpose(3, 1, 0, 2, 4).reshape(2048, 512)
        for tiles in (own_late, other_late)
    ]
    up_second_halves = [
        tiles[..., 512:]
        .reshape(4, 2, Z_RING, 16, 2, 128)
        .transpose(4, 2, 0, 3, 1, 5)
        .reshape(1024, 256)
        for tiles in (own_late, other_late)
    ]
    lift_three = dot_halves(level_three, up_third_halves, core).reshape(
        tile_rows // 4, levels, tile_cols // 4, -1
    )
    level_two = (second_grid.astype(jnp.float32) + spread_quads(lift_three)).astype(jnp.bfloat16)
    lift_two = dot_halves(
        level_two.reshape(-1, level_two.shape[-1]), up_second_halves, core
    ).reshape(tile_rows // 2, levels, tile_cols // 2, -1)
    return (skip_first.astype(jnp.float32) + spread_quads(lift_two)).astype(jnp.bfloat16)


def solution(mesh):
    in_specs = (
        P("lat", None, "lon", None),
        P("lat", "lon"),
        P(),
        P(),
        P(),
        P(),
        P("lat", None),
        P(),
        P("lat", None),
        P(),
        P(None, "lat"),
        P(),
        P(None, None, "lat"),
        P("lat", None),
        P("lat", None),
        P("lat", None),
    )
    out_specs = P("lat", None, "lon", None)
    return jax.shard_map(
        on_device, mesh=mesh, in_specs=in_specs, out_specs=out_specs, check_vma=False
    )
```

```python
import jax
import jax.numpy as jnp
from jax import lax
from jax.experimental import pallas as pl
from jax.experimental.pallas import tpu as pltpu
from jax.sharding import PartitionSpec as P

HD = 64


def with_halo(cells, sides, width, ties):
    for (axis, dim), tie in zip(sides, ties):
        cells = after(cells, *tie)
        count = lax.axis_size(axis)
        head = lax.slice_in_dim(cells, 0, width, axis=dim)
        tail = lax.slice_in_dim(cells, cells.shape[dim] - width, cells.shape[dim], axis=dim)
        cells = jnp.concatenate(
            [
                lax.ppermute(tail, axis, [(i, (i + 1) % count) for i in range(count)]),
                cells,
                lax.ppermute(head, axis, [((i + 1) % count, i) for i in range(count)]),
            ],
            axis=dim,
        )
    return cells


def norm_rows(values, gain):
    row_mean = jnp.mean(values, axis=-1, keepdims=True)
    centred = values - row_mean
    spread = jnp.mean(centred * centred, axis=-1, keepdims=True)
    return centred * lax.rsqrt(spread + 1e-05) * gain


def split_quads(cell_grid):
    lat_count, levels, lon_count, feat_dim = cell_grid.shape
    blocks = cell_grid.reshape(lat_count // 2, 2, levels, lon_count // 2, 2, feat_dim)
    return blocks.transpose(0, 2, 3, 1, 4, 5).reshape(
        lat_count // 2, levels, lon_count // 2, 4 * feat_dim
    )


def spread_quads(cell_grid):
    lat_count, levels, lon_count, feat_dim = cell_grid.shape
    widened = jnp.broadcast_to(
        cell_grid[:, None, :, :, None, :], (lat_count, 2, levels, lon_count, 2, feat_dim)
    )
    return widened.reshape(2 * lat_count, levels, 2 * lon_count, feat_dim)


def call_kernel(body, out_shape, operands, scratch=(), flops=0):
    smem = [operand.dtype == jnp.int32 for operand in operands]
    return pl.pallas_call(
        body,
        out_shape=out_shape,
        in_specs=[
            pl.BlockSpec(memory_space=pltpu.SMEM if scalar else pltpu.VMEM) for scalar in smem
        ],
        out_specs=jax.tree.map(lambda _: pl.BlockSpec(memory_space=pltpu.VMEM), out_shape),
        scratch_shapes=list(scratch),
        compiler_params=pltpu.CompilerParams(vmem_limit_bytes=48 * 1024 * 1024),
        cost_estimate=pl.CostEstimate(
            flops=flops,
            bytes_accessed=sum(operand.size * operand.dtype.itemsize for operand in operands),
            transcendentals=0,
        ),
    )(*operands)


def dot_rows(left, right):
    return lax.dot_general(left, right, (((1,), (0,)), ((), ())), preferred_element_type=jnp.float32)


def softmax_rows(scores, keep):
    scores = jnp.where(keep, scores, -1e30)
    weights = jnp.exp(scores - jnp.max(scores, axis=-1, keepdims=True))
    total = jnp.sum(weights, axis=-1, keepdims=True)
    return (weights / total).astype(jnp.bfloat16)


def first_kernel(x_ref, gain_ref, qkv_ref, window_ref, lat_ref, out_ref):
    steps = lat_ref.shape[0]
    group = x_ref.shape[0] // steps
    lane = lax.broadcasted_iota(jnp.int32, (group, 128), 1)
    gain = gain_ref[...]
    for step in range(steps):
        mine = pl.ds(step * group, group)
        normed = norm_rows(x_ref[mine, :].astype(jnp.float32), gain).astype(jnp.bfloat16)
        query = (dot_rows(normed, qkv_ref[0]).astype(jnp.bfloat16) * 0.125).astype(jnp.bfloat16)
        key = dot_rows(normed, qkv_ref[1]).astype(jnp.bfloat16)
        value = dot_rows(normed, qkv_ref[2]).astype(jnp.bfloat16)
        keep = window_ref[...] * lat_ref[step] > 0.0
        for pair in range(query.shape[1] // 128):
            here = slice(pair * 128, pair * 128 + 128)
            parts = []
            for side in range(2):
                picked = (lane < HD) if side == 0 else (lane >= HD)
                key_side = jnp.where(picked, key[:, here], jnp.zeros_like(key[:, here]))
                scores = lax.dot_general(
                    query[:, here],
                    key_side,
                    (((1,), (1,)), ((), ())),
                    preferred_element_type=jnp.float32,
                )
                parts.append(dot_rows(softmax_rows(scores, keep), value[:, here]))
            out_ref[mine, here] = jnp.where(lane < HD, parts[0], parts[1]).astype(jnp.bfloat16)


def third_kernel(core_ref, own_ref, other_ref, gain_ref, qkv_ref, out_ref, normed_ref):
    blocks, sides, line, width = own_ref.shape
    core = core_ref[0]
    half = blocks * width
    count = 1.0 / (2 * half)
    rows = 32
    for side in range(sides):
        for start in range(0, line, rows):
            mine = slice(start, start + rows)
            tiles = [own_ref[z, side, mine, :].astype(jnp.float32) for z in range(blocks)]
            tiles += [other_ref[z, 1 - side, mine, :].astype(jnp.float32) for z in range(blocks)]
            row_mean = jnp.sum(sum(tiles), axis=-1, keepdims=True) * count
            tiles = [tile - row_mean for tile in tiles]
            spread = jnp.sum(sum(tile * tile for tile in tiles), axis=-1, keepdims=True)
            scale = lax.rsqrt(spread * count + 1e-05)
            for place, tile in enumerate(tiles):
                origin = core if place < blocks else 1 - core
                gain = gain_ref[origin * blocks + place % blocks]
                normed_ref[
                    side * line + start : side * line + start + rows,
                    place * width : (place + 1) * width,
                ] = (tile * scale * gain).astype(jnp.bfloat16)
    own_rows = pl.multiple_of(core * half, half)
    other_rows = pl.multiple_of((1 - core) * half, half)
    triple = (
        dot_rows(normed_ref[:, :half], qkv_ref[pl.ds(own_rows, half), :])
        + dot_rows(normed_ref[:, half:], qkv_ref[pl.ds(other_rows, half), :])
    ).astype(jnp.bfloat16)
    query = (triple[:, :HD] * 0.125).astype(jnp.bfloat16)
    key = triple[:, HD : 2 * HD]
    value = triple[:, 2 * HD :]
    token = lax.broadcasted_iota(jnp.int32, (128, 128), 0)
    other = lax.broadcasted_iota(jnp.int32, (128, 128), 1)
    keep = jnp.right_shift(token, 5) == jnp.right_shift(other, 5)
    mixed = []
    for group in range(sides * line // 128):
        mine = slice(group * 128, group * 128 + 128)
        scores = lax.dot_general(
            query[mine], key[mine], (((1,), (1,)), ((), ())), preferred_element_type=jnp.float32
        )
        mixed.append(dot_rows(softmax_rows(scores, keep), value[mine]))
    mixed = jnp.concatenate(mixed, axis=0)
    count = line // blocks
    for z in range(blocks):
        for side in range(sides):
            start = side * line + z * count
            out_ref[z, side] = mixed[start : start + count].astype(jnp.bfloat16)


def heads_kernel(heads_ref, late_ref, own_ref, send_ref):
    total = [None, None]
    for z in range(heads_ref.shape[0]):
        left = jnp.concatenate(
            [heads_ref[z, 0].astype(jnp.float32), heads_ref[z, 1].astype(jnp.float32)], axis=0
        ).astype(jnp.bfloat16)
        for part in range(2):
            right = jnp.concatenate(
                [late_ref[(2 * row + part) * 8 + z, :, 1280:2304] for row in range(4)], axis=0
            )
            product = dot_rows(left, right)
            total[part] = product if z == 0 else total[part] + product
    count = heads_ref.shape[2]
    for part in range(2):
        here = slice(part * 1024, part * 1024 + 1024)
        own_ref[:, here] = total[part][:count]
        send_ref[:, here] = total[part][count:].astype(jnp.bfloat16)


def spread_matrix(lat_count, lon_count):
    fine = (2 * lat_count * lon_count, lat_count * lon_count // 2)
    row = lax.broadcasted_iota(jnp.int32, fine, 0)
    column = lax.broadcasted_iota(jnp.int32, fine, 1)
    bits = lon_count.bit_length() - 1
    lat = jnp.right_shift(row, bits + 2)
    level = jnp.right_shift(row, bits) & 1
    lon = jnp.right_shift(row & (lon_count - 1), 1)
    source = (lat * 2 + level) * (lon_count // 2) + lon
    return jnp.where(source == column, 1.0, 0.0).astype(jnp.float32)


def spread_rows(values, lat_count, lon_count):
    return lax.dot_general(
        spread_matrix(lat_count, lon_count),
        values,
        (((1,), (0,)), ((), ())),
        precision=lax.Precision.HIGHEST,
        preferred_element_type=jnp.float32,
    )


def up_kernel(
    core_ref, own_coarse_ref, other_coarse_ref, part_ref, recv_ref, late_ref, swapped_ref,
    second_ref, skip_ref, out_ref, coarse_ref, lift_ref, level_ref, small_ref,
):
    core = core_ref[0]
    blocks, count, width = own_coarse_ref.shape
    half = blocks * width
    for z in range(blocks):
        for ref, origin in ((own_coarse_ref, core), (other_coarse_ref, 1 - core)):
            coarse_ref[origin * blocks + z] = ref[z].astype(jnp.float32)
    level_three = []
    for place in range(2 * blocks):
        here = slice(place * width, place * width + width)
        level_three.append(
            (coarse_ref[place] + (part_ref[:, here] + recv_ref[:, here].astype(jnp.float32))).astype(
                jnp.bfloat16
            )
        )
    for weights_ref, origin in ((late_ref, core), (swapped_ref, 1 - core)):
        total = None
        for ring in range(2):
            for z in range(8):
                right = jnp.concatenate(
                    [weights_ref[y * 8 + z, :, ring * 640 : ring * 640 + 512] for y in range(8)],
                    axis=0,
                )
                product = dot_rows(level_three[ring * 8 + z], right)
                total = product if total is None else total + product
        lift_ref[origin] = total
    lat_count, lon_count = 6, 8
    for side in range(2):
        here = slice(side * 512, side * 512 + 512)
        level_ref[:, here] = (
            second_ref[:, here].astype(jnp.float32)
            + spread_rows(lift_ref[side], lat_count, lon_count)
        ).astype(jnp.bfloat16)
    for weights_ref, origin in ((late_ref, core), (swapped_ref, 1 - core)):
        total = None
        for ring in range(2):
            for z in range(0, 8, 2):
                right = jnp.concatenate(
                    [
                        jnp.concatenate(
                            [
                                weights_ref[
                                    (2 * row + part) * 8 + zz, :, ring * 640 + 512 : ring * 640 + 640
                                ]
                                for zz in (z, z + 1)
                                for row in range(4)
                            ],
                            axis=0,
                        )
                        for part in range(2)
                    ],
                    axis=1,
                )
                start = (ring * 8 + z) * 64
                product = dot_rows(level_ref[:, start : start + 128], right)
                total = product if total is None else total + product
        small_ref[origin] = total
    for side in range(2):
        here = slice(side * 256, side * 256 + 256)
        out_ref[:, here] = (
            skip_ref[:, here].astype(jnp.float32)
            + spread_rows(small_ref[side], 2 * lat_count, 2 * lon_count)
        ).astype(jnp.bfloat16)


Z_RING = 8
RINGS = [[ring * Z_RING + place for place in range(Z_RING)] for ring in range(2)]


def swap_cores(values):
    count = lax.axis_size("lon")
    return lax.ppermute(values, "lon", [(i, i ^ 1) for i in range(count)])


def swap_rings(values):
    count = lax.axis_size("lat")
    return lax.ppermute(values, "lat", [(i, (i + Z_RING) % count) for i in range(count)])


def swap_shards(values):
    lon_count = lax.axis_size("lon")
    pairs = []
    for lat in range(lax.axis_size("lat")):
        for lon in range(lon_count):
            ring, place = divmod(lat, Z_RING)
            target = (lat, lon)
            if ring != lon % 2:
                target = ((1 - ring) * Z_RING + place, lon ^ 1)
            pairs.append((lat * lon_count + lon, target[0] * lon_count + target[1]))
    return lax.ppermute(values, ("lat", "lon"), pairs)


def ring_scatter(blocks):
    return lax.all_to_all(blocks, "lat", 0, 0, axis_index_groups=RINGS, tiled=True)


def ring_gather(values):
    return ring_scatter(jnp.broadcast_to(values[None], (Z_RING,) + values.shape))


def in_order(flag, own, other, axis):
    return jnp.where(
        flag == 0,
        jnp.concatenate([own, other], axis=axis),
        jnp.concatenate([other, own], axis=axis),
    )


def cut(values, row, rows, column, columns):
    return lax.dynamic_slice(values, (row, column), (rows, columns))


def after(values, *before):
    return lax.optimization_barrier((values,) + before)[0]


def column_gather(values):
    groups = [[4 * y + x for y in range(8)] for x in range(4)]
    return lax.all_to_all(
        jnp.broadcast_to(values[None], (8,) + values.shape),
        "lon",
        0,
        0,
        axis_index_groups=groups,
        tiled=True,
    )


def on_device(
    fields,
    land_ids,
    surface_table,
    level_table,
    norm_first,
    qkv_first,
    out_first,
    norm_merge2,
    merge_second,
    norm_merge3,
    merge_third,
    norm_third,
    qkv_third,
    out_third,
    up_third,
    up_second,
):
    tile_rows, levels, tile_cols, feat_dim = fields.shape
    lat_count = lax.axis_size("lat")
    ring = lax.axis_index("lat") // Z_RING
    core = lax.axis_index("lon") % 2
    column = lax.axis_index("lon") // 4

    own_merge = lax.dynamic_slice_in_dim(merge_second, core * 512, 512, 1)[None]
    both_merge = in_order(ring, own_merge, swap_rings(own_merge), 0)
    merge_half = lax.all_gather(
        both_merge,
        "lat",
        axis=1,
        axis_index_groups=RINGS,
        tiled=True,
    ).reshape(-1, 512)

    own_rest = jnp.concatenate(
        [
            cut(out_first, column // 4 * 16, 16, column % 4 * 128, 128),
            cut(up_third, column * 16, 16, core * 512, 512),
            cut(up_second, column // 2 * 16, 16, core * 256 + column % 2 * 128, 128),
        ],
        axis=1,
    )[None]
    both_rest = in_order(ring, own_rest, swap_rings(own_rest), 0)
    out_first_rows = ring_gather(both_rest[:, :, :128])
    out_first_tiles = column_gather(out_first_rows)
    out_first_all = (
        out_first_tiles.reshape(2, 4, Z_RING, 2, 16, 128)
        .transpose(3, 2, 0, 4, 1, 5)
        .reshape(feat_dim, feat_dim)
    )
    out_third = swap_shards(out_third)

    picks = (land_ids[:, :, None] == jnp.arange(3, dtype=jnp.int32)).astype(jnp.float32)
    surface = jnp.einsum("ijs,sc->ijc", picks, surface_table.astype(jnp.float32))
    hidden = (
        fields.astype(jnp.float32)
        + surface[:, None, :, :]
        + level_table.astype(jnp.float32)[None, :, None, :]
    ).astype(jnp.bfloat16)
    ext_rows = tile_rows + 4
    ext_cols = tile_cols + 4
    grown = with_halo(
        hidden, (("lat", 0), ("lon", 2)), 2, ((both_merge,), (out_first_rows, out_third))
    )
    group = 8 * ext_cols
    token_col = jnp.arange(group) % ext_cols // 4
    same_window = (token_col[:, None] == token_col[None, :]).astype(jnp.float32)
    lat_place = lax.axis_index("lat") * tile_rows + jnp.arange(ext_rows) - 2
    valid_rows = ((lat_place >= 0) & (lat_place < tile_rows * lat_count)).astype(jnp.float32)
    valid_rows = jnp.repeat(valid_rows, 2 * ext_cols).reshape(ext_rows // 4, 1, group)
    attended = call_kernel(
        first_kernel,
        jax.ShapeDtypeStruct((ext_rows * levels * ext_cols, feat_dim), jnp.bfloat16),
        (
            grown.reshape(-1, feat_dim),
            norm_first[None],
            qkv_first,
            same_window,
            valid_rows,
        ),
        flops=2 * 640 * 512 * 1536,
    )
    merge_third = swap_shards(after(merge_third, grown))
    qkv_third = swap_shards(after(qkv_third, grown))
    late = jnp.concatenate(
        [
            both_rest[0, :, 128:],
            both_rest[1, :, 128:],
            cut(out_third, column // 2 * 16, 16, column % 2 * 1024, 1024),
        ],
        axis=1,
    )
    late_rows = ring_gather(after(late, attended))
    attended = attended.reshape(ext_rows, levels, ext_cols, feat_dim)[
        2 : tile_rows + 2, :, 2 : tile_cols + 2, :
    ]
    projected = jnp.dot(
        attended.reshape(-1, feat_dim), out_first_all, preferred_element_type=jnp.float32
    ).reshape(hidden.shape)
    skip_first = (hidden.astype(jnp.float32) + projected).astype(jnp.bfloat16)
    quads = split_quads(skip_first)
    merged_in = norm_rows(quads.astype(jnp.float32), norm_merge2).astype(jnp.bfloat16)
    merged_in = merged_in.reshape(-1, quads.shape[-1])
    merged_pair = jnp.concatenate([merged_in, swap_cores(merged_in)], axis=0)
    second_half = jnp.dot(merged_pair, merge_half, preferred_element_type=jnp.float32).astype(
        jnp.bfloat16
    )
    own_rows = merged_in.shape[0]
    second_grid = in_order(core, second_half[:own_rows], swap_cores(second_half[own_rows:]), 1)

    late = lax.all_gather(
        late_rows,
        "lon",
        axis=0,
        axis_index_groups=[[4 * y + x for y in range(8)] for x in range(4)],
        tiled=True,
    )

    second_cells = second_grid
    second_grid = second_grid.reshape(tile_rows // 2, levels, tile_cols // 2, -1)
    quads_coarse = split_quads(second_grid)
    coarse_in = (
        norm_rows(quads_coarse.astype(jnp.float32), norm_merge3)
        .astype(jnp.bfloat16)
        .reshape(-1, quads_coarse.shape[-1])
    )
    coarse_in = after(coarse_in, late_rows, merge_third, qkv_third)
    own_count = coarse_in.shape[0]
    line = Z_RING * own_count

    ring_tokens = ring_gather(coarse_in).reshape(line, -1)
    column_block = jnp.stack(
        [
            jnp.dot(tokens, merge_third, preferred_element_type=jnp.float32).astype(jnp.bfloat16)
            for tokens in (ring_tokens, swap_cores(ring_tokens))
        ]
    )
    own_columns = ring_gather(column_block)
    other_columns = swap_cores(own_columns)
    blocks, _, _, width = own_columns.shape
    head_feats = qkv_third.shape[2]
    core_id = core.astype(jnp.int32).reshape(1)
    heads_out = call_kernel(
        third_kernel,
        jax.ShapeDtypeStruct((Z_RING, 2, own_count, head_feats), jnp.bfloat16),
        (
            core_id,
            own_columns,
            other_columns,
            norm_third.reshape(2 * blocks, 1, width),
            jnp.concatenate([qkv_third[0], qkv_third[1], qkv_third[2]], axis=1),
        ),
        (pltpu.VMEM((2 * line, 2 * blocks * width), jnp.bfloat16),),
        flops=2 * 384 * 2048 * 192,
    )

    chip_heads = ring_scatter(heads_out)
    own_part, send_part = call_kernel(
        heads_kernel,
        (
            jax.ShapeDtypeStruct((own_count, 2048), jnp.float32),
            jax.ShapeDtypeStruct((own_count, 2048), jnp.bfloat16),
        ),
        (chip_heads, late),
        flops=2 * 48 * 512 * 2048,
    )
    place = lax.axis_index("lat") % Z_RING
    own_coarse, other_coarse = [
        lax.dynamic_slice_in_dim(columns[:, side], place * own_count, own_count, 1)
        for side, columns in enumerate((own_columns, other_columns))
    ]
    decoded = call_kernel(
        up_kernel,
        jax.ShapeDtypeStruct((tile_rows * levels * tile_cols, feat_dim), jnp.bfloat16),
        (
            core_id,
            own_coarse,
            other_coarse,
            own_part,
            swap_cores(send_part),
            late,
            swap_cores(late[:, :, :1280]),
            second_cells,
            skip_first.reshape(-1, feat_dim),
        ),
        (
            pltpu.VMEM((2 * blocks, own_count, width), jnp.float32),
            pltpu.VMEM((2, own_count, 512), jnp.float32),
            pltpu.VMEM((second_cells.shape[0], 1024), jnp.bfloat16),
            pltpu.VMEM((2, second_cells.shape[0], 256), jnp.float32),
        ),
        flops=2 * (24 * 2048 * 1024 + 96 * 1024 * 512),
    )
    return decoded.reshape(fields.shape)


def solution(mesh):
    in_specs = (
        P("lat", None, "lon", None),
        P("lat", "lon"),
        P(),
        P(),
        P(),
        P(),
        P("lat", None),
        P(),
        P("lat", None),
        P(),
        P(None, "lat"),
        P(),
        P(None, None, "lat"),
        P("lat", None),
        P("lat", None),
        P("lat", None),
    )
    out_specs = P("lat", None, "lon", None)
    return jax.shard_map(
        on_device, mesh=mesh, in_specs=in_specs, out_specs=out_specs, check_vma=False
    )
```

```python
import jax
import jax.numpy as jnp
from jax import lax
from jax.experimental import pallas as pl
from jax.experimental.pallas import tpu as pltpu
from jax.sharding import PartitionSpec as P

HD = 64


def norm_rows(values, gain):
    row_mean = jnp.mean(values, axis=-1, keepdims=True)
    centred = values - row_mean
    spread = jnp.mean(centred * centred, axis=-1, keepdims=True)
    return centred * lax.rsqrt(spread + 1e-05) * gain


def call_kernel(body, out_shape, operands, scratch=(), flops=0):
    smem = [operand.dtype == jnp.int32 for operand in operands]
    return pl.pallas_call(
        body,
        out_shape=out_shape,
        in_specs=[
            pl.BlockSpec(memory_space=pltpu.SMEM if scalar else pltpu.VMEM) for scalar in smem
        ],
        out_specs=jax.tree.map(lambda _: pl.BlockSpec(memory_space=pltpu.VMEM), out_shape),
        scratch_shapes=list(scratch),
        compiler_params=pltpu.CompilerParams(vmem_limit_bytes=48 * 1024 * 1024),
        cost_estimate=pl.CostEstimate(
            flops=flops,
            bytes_accessed=sum(operand.size * operand.dtype.itemsize for operand in operands),
            transcendentals=0,
        ),
    )(*operands)


def dot_rows(left, right):
    return lax.dot_general(left, right, (((1,), (0,)), ((), ())), preferred_element_type=jnp.float32)


def softmax_rows(scores, keep):
    scores = jnp.where(keep, scores, -1e30)
    weights = jnp.exp(scores - jnp.max(scores, axis=-1, keepdims=True))
    total = jnp.sum(weights, axis=-1, keepdims=True)
    return (weights / total).astype(jnp.bfloat16)


def first_kernel(x_ref, left_ref, right_ref, gain_ref, qkv_ref, window_ref, lat_ref, out_ref):
    steps = lat_ref.shape[0]
    own, side = x_ref.shape[0] // steps, left_ref.shape[0] // steps
    lane = lax.broadcasted_iota(jnp.int32, (own, 128), 1)
    key_lane = lax.broadcasted_iota(jnp.int32, (own + 2 * side, 128), 1)
    gain = gain_ref[...]
    for step in range(steps):
        rows = jnp.concatenate(
            [
                x_ref[step * own : (step + 1) * own, :],
                left_ref[step * side : (step + 1) * side, :],
                right_ref[step * side : (step + 1) * side, :],
            ],
            axis=0,
        )
        normed = norm_rows(rows.astype(jnp.float32), gain).astype(jnp.bfloat16)
        query = dot_rows(normed[:own], qkv_ref[0]).astype(jnp.bfloat16)
        query = (query * 0.125).astype(jnp.bfloat16)
        key = dot_rows(normed, qkv_ref[1]).astype(jnp.bfloat16)
        value = dot_rows(normed, qkv_ref[2]).astype(jnp.bfloat16)
        keep = window_ref[...] * lat_ref[step] > 0.0
        first = own // 2 if step == 0 else 0
        last = own // 2 if step == steps - 1 else own
        start = step * own - own // 2 + first
        for pair in range(query.shape[1] // 128):
            here = slice(pair * 128, pair * 128 + 128)
            parts = []
            for odd in range(2):
                picked = (key_lane < HD) if odd == 0 else (key_lane >= HD)
                key_side = jnp.where(picked, key[:, here], jnp.zeros_like(key[:, here]))
                scores = lax.dot_general(
                    query[:, here],
                    key_side,
                    (((1,), (1,)), ((), ())),
                    preferred_element_type=jnp.float32,
                )
                parts.append(dot_rows(softmax_rows(scores, keep), value[:, here]))
            mixed = jnp.where(lane < HD, parts[0], parts[1]).astype(jnp.bfloat16)
            out_ref[start : start + last - first, here] = mixed[first:last]


def pick_matrix(lat_count, lon_count, lat_side, lon_side):
    shape = (2 * lat_count * lon_count, 8 * lat_count * lon_count)
    row = lax.broadcasted_iota(jnp.int32, shape, 0)
    column = lax.broadcasted_iota(jnp.int32, shape, 1)
    bits = lon_count.bit_length() - 1
    lon = row & (lon_count - 1)
    level = jnp.right_shift(row, bits) & 1
    lat = jnp.right_shift(row, bits + 1)
    source = ((2 * lat + lat_side) * 2 + level) * (2 * lon_count) + 2 * lon + lon_side
    return jnp.where(source == column, 1.0, 0.0).astype(jnp.bfloat16)


def join_quads(cells, lat_count, lon_count, gain_ref, out_ref):
    width = cells.shape[1]
    parts = [
        dot_rows(pick_matrix(lat_count, lon_count, lat_side, lon_side), cells)
        for lat_side in range(2)
        for lon_side in range(2)
    ]
    count = 1.0 / (4 * width)
    row_mean = sum(jnp.sum(part, axis=-1, keepdims=True) for part in parts) * count
    parts = [part - row_mean for part in parts]
    spread = sum(jnp.sum(part * part, axis=-1, keepdims=True) for part in parts) * count
    scale = lax.rsqrt(spread + 1e-05)
    for place, part in enumerate(parts):
        here = slice(place * width, place * width + width)
        out_ref[:, here] = (part * scale * gain_ref[:, here]).astype(jnp.bfloat16)


def skip_kernel(attended_ref, hidden_ref, tiles_ref, gain_ref, skip_ref, merged_ref):
    total = None
    for ring in range(2):
        for z in range(0, 8, 4):
            right = jnp.concatenate(
                [
                    jnp.concatenate(
                        [
                            tiles_ref[row * 4 + part, zz, ring]
                            for zz in range(z, z + 4)
                            for row in range(2)
                        ],
                        axis=0,
                    )
                    for part in range(4)
                ],
                axis=1,
            )
            start = (ring * 8 + z) * 32
            product = dot_rows(attended_ref[:, start : start + 128], right)
            total = product if total is None else total + product
    skip = (hidden_ref[...].astype(jnp.float32) + total).astype(jnp.bfloat16)
    skip_ref[...] = skip
    join_quads(skip, 6, 8, gain_ref, merged_ref)


def join_kernel(core_ref, own_ref, recv_ref, gain_ref, second_ref, coarse_ref, halves_ref):
    core = core_ref[0]
    halves_ref[core] = own_ref[...]
    halves_ref[1 - core] = recv_ref[...]
    second = jnp.concatenate([halves_ref[0], halves_ref[1]], axis=1)
    second_ref[...] = second
    join_quads(second, 3, 4, gain_ref, coarse_ref)


def third_kernel(
    core_ref, own_ref, other_ref, gain_ref, qkv_ref, out_ref, coarse_ref, normed_ref, raw_ref
):
    blocks, sides, line, width = own_ref.shape
    core = core_ref[0]
    half = blocks * width
    count = 1.0 / (2 * half)
    rows = 32
    for side in range(sides):
        for start in range(0, line, rows):
            mine = slice(start, start + rows)
            tiles = [own_ref[z, side, mine, :].astype(jnp.float32) for z in range(blocks)]
            tiles += [other_ref[z, 1 - side, mine, :].astype(jnp.float32) for z in range(blocks)]
            if side == 0:
                for place, tile in enumerate(tiles):
                    raw_ref[mine, place * width : (place + 1) * width] = tile
            row_mean = jnp.sum(sum(tiles), axis=-1, keepdims=True) * count
            tiles = [tile - row_mean for tile in tiles]
            spread = jnp.sum(sum(tile * tile for tile in tiles), axis=-1, keepdims=True)
            scale = lax.rsqrt(spread * count + 1e-05)
            for place, tile in enumerate(tiles):
                origin = core if place < blocks else 1 - core
                gain = gain_ref[origin * blocks + place % blocks]
                normed_ref[
                    side * line + start : side * line + start + rows,
                    place * width : (place + 1) * width,
                ] = (tile * scale * gain).astype(jnp.bfloat16)
    tokens = line // blocks
    coarse_ref[...] = raw_ref[pl.ds(pl.multiple_of(core_ref[1] * tokens, 8), tokens), :]
    own_rows = pl.multiple_of(core * half, half)
    other_rows = pl.multiple_of((1 - core) * half, half)
    triple = (
        dot_rows(normed_ref[:, :half], qkv_ref[pl.ds(own_rows, half), :])
        + dot_rows(normed_ref[:, half:], qkv_ref[pl.ds(other_rows, half), :])
    ).astype(jnp.bfloat16)
    query = (triple[:, :HD] * 0.125).astype(jnp.bfloat16)
    key = triple[:, HD : 2 * HD]
    value = triple[:, 2 * HD :]
    token = lax.broadcasted_iota(jnp.int32, (128, 128), 0)
    other = lax.broadcasted_iota(jnp.int32, (128, 128), 1)
    keep = jnp.right_shift(token, 5) == jnp.right_shift(other, 5)
    mixed = []
    for group in range(sides * line // 128):
        mine = slice(group * 128, group * 128 + 128)
        scores = lax.dot_general(
            query[mine], key[mine], (((1,), (1,)), ((), ())), preferred_element_type=jnp.float32
        )
        mixed.append(dot_rows(softmax_rows(scores, keep), value[mine]))
    mixed = jnp.concatenate(mixed, axis=0)
    for z in range(blocks):
        for side in range(sides):
            start = side * line + z * tokens
            out_ref[z, side] = mixed[start : start + tokens].astype(jnp.bfloat16)


def heads_kernel(heads_ref, late_ref, own_ref, send_ref):
    total = [None, None]
    for z in range(heads_ref.shape[0]):
        left = jnp.concatenate(
            [heads_ref[z, 0].astype(jnp.float32), heads_ref[z, 1].astype(jnp.float32)], axis=0
        ).astype(jnp.bfloat16)
        for part in range(2):
            right = jnp.concatenate(
                [late_ref[(2 * row + part) * 8 + z, :, 1280:2304] for row in range(4)], axis=0
            )
            product = dot_rows(left, right)
            total[part] = product if z == 0 else total[part] + product
    count = heads_ref.shape[2]
    for part in range(2):
        here = slice(part * 1024, part * 1024 + 1024)
        own_ref[:, here] = total[part][:count]
        send_ref[:, here] = total[part][count:].astype(jnp.bfloat16)


def spread_matrix(lat_count, lon_count):
    fine = (2 * lat_count * lon_count, lat_count * lon_count // 2)
    row = lax.broadcasted_iota(jnp.int32, fine, 0)
    column = lax.broadcasted_iota(jnp.int32, fine, 1)
    bits = lon_count.bit_length() - 1
    lat = jnp.right_shift(row, bits + 2)
    level = jnp.right_shift(row, bits) & 1
    lon = jnp.right_shift(row & (lon_count - 1), 1)
    source = (lat * 2 + level) * (lon_count // 2) + lon
    return jnp.where(source == column, 1.0, 0.0).astype(jnp.float32)


def spread_rows(values, lat_count, lon_count):
    return lax.dot_general(
        spread_matrix(lat_count, lon_count),
        values,
        (((1,), (0,)), ((), ())),
        precision=lax.Precision.HIGHEST,
        preferred_element_type=jnp.float32,
    )


def up_kernel(
    core_ref, own_coarse_ref, part_ref, recv_ref, late_ref, swapped_ref,
    second_ref, skip_ref, out_ref, coarse_ref, lift_ref, level_ref, small_ref,
):
    core = core_ref[0]
    blocks, width = 8, 128
    for z in range(blocks):
        for place, origin in ((z, core), (blocks + z, 1 - core)):
            coarse_ref[origin * blocks + z] = own_coarse_ref[:, place * width : (place + 1) * width]
    level_three = []
    for place in range(2 * blocks):
        here = slice(place * width, place * width + width)
        level_three.append(
            (coarse_ref[place] + (part_ref[:, here] + recv_ref[:, here].astype(jnp.float32))).astype(
                jnp.bfloat16
            )
        )
    for weights_ref, origin in ((late_ref, core), (swapped_ref, 1 - core)):
        total = None
        for ring in range(2):
            for z in range(8):
                right = jnp.concatenate(
                    [weights_ref[y * 8 + z, :, ring * 640 : ring * 640 + 512] for y in range(8)],
                    axis=0,
                )
                product = dot_rows(level_three[ring * 8 + z], right)
                total = product if total is None else total + product
        lift_ref[origin] = total
    lat_count, lon_count = 6, 8
    for side in range(2):
        here = slice(side * 512, side * 512 + 512)
        level_ref[:, here] = (
            second_ref[:, here].astype(jnp.float32)
            + spread_rows(lift_ref[side], lat_count, lon_count)
        ).astype(jnp.bfloat16)
    for weights_ref, origin in ((late_ref, core), (swapped_ref, 1 - core)):
        total = None
        for ring in range(2):
            for z in range(0, 8, 2):
                right = jnp.concatenate(
                    [
                        jnp.concatenate(
                            [
                                weights_ref[
                                    (2 * row + part) * 8 + zz, :, ring * 640 + 512 : ring * 640 + 640
                                ]
                                for zz in (z, z + 1)
                                for row in range(4)
                            ],
                            axis=0,
                        )
                        for part in range(2)
                    ],
                    axis=1,
                )
                start = (ring * 8 + z) * 64
                product = dot_rows(level_ref[:, start : start + 128], right)
                total = product if total is None else total + product
        small_ref[origin] = total
    for side in range(2):
        here = slice(side * 256, side * 256 + 256)
        out_ref[:, here] = (
            skip_ref[:, here].astype(jnp.float32)
            + spread_rows(small_ref[side], 2 * lat_count, 2 * lon_count)
        ).astype(jnp.bfloat16)


Z_RING = 8
RINGS = [[ring * Z_RING + place for place in range(Z_RING)] for ring in range(2)]


def neighbours(first, last, axis):
    count = lax.axis_size(axis)
    before = lax.ppermute(last, axis, [(i, (i + 1) % count) for i in range(count)])
    behind = lax.ppermute(first, axis, [((i + 1) % count, i) for i in range(count)])
    return before, behind


def swap_cores(values):
    count = lax.axis_size("lon")
    return lax.ppermute(values, "lon", [(i, i ^ 1) for i in range(count)])


def swap_rings(values):
    count = lax.axis_size("lat")
    return lax.ppermute(values, "lat", [(i, (i + Z_RING) % count) for i in range(count)])


def swap_shards(values):
    lon_count = lax.axis_size("lon")
    pairs = []
    for lat in range(lax.axis_size("lat")):
        for lon in range(lon_count):
            ring, place = divmod(lat, Z_RING)
            target = (lat, lon)
            if ring != lon % 2:
                target = ((1 - ring) * Z_RING + place, lon ^ 1)
            pairs.append((lat * lon_count + lon, target[0] * lon_count + target[1]))
    return lax.ppermute(values, ("lat", "lon"), pairs)


def ring_scatter(blocks):
    return lax.all_to_all(blocks, "lat", 0, 0, axis_index_groups=RINGS, tiled=True)


def ring_gather(values):
    return ring_scatter(jnp.broadcast_to(values[None], (Z_RING,) + values.shape))


def in_order(flag, own, other, axis):
    return jnp.where(
        flag == 0,
        jnp.concatenate([own, other], axis=axis),
        jnp.concatenate([other, own], axis=axis),
    )


def cut(values, row, rows, column, columns):
    return lax.dynamic_slice(values, (row, column), (rows, columns))


def after(values, *before):
    return lax.optimization_barrier((values,) + before)[0]


def column_gather(values):
    groups = [[4 * y + x for y in range(8)] for x in range(4)]
    return lax.all_to_all(
        jnp.broadcast_to(values[None], (8,) + values.shape),
        "lon",
        0,
        0,
        axis_index_groups=groups,
        tiled=True,
    )


def on_device(
    fields,
    land_ids,
    surface_table,
    level_table,
    norm_first,
    qkv_first,
    out_first,
    norm_merge2,
    merge_second,
    norm_merge3,
    merge_third,
    norm_third,
    qkv_third,
    out_third,
    up_third,
    up_second,
):
    tile_rows, levels, tile_cols, feat_dim = fields.shape
    lat_count = lax.axis_size("lat")
    ring = lax.axis_index("lat") // Z_RING
    core = lax.axis_index("lon") % 2
    column = lax.axis_index("lon") // 4

    own_merge = lax.dynamic_slice_in_dim(merge_second, core * 512, 512, 1)[None]
    both_merge = in_order(ring, own_merge, swap_rings(own_merge), 0)
    merge_half = lax.all_gather(
        both_merge,
        "lat",
        axis=1,
        axis_index_groups=RINGS,
        tiled=True,
    ).reshape(-1, 512)

    own_rest = jnp.concatenate(
        [
            cut(out_first, column // 4 * 16, 16, column % 4 * 128, 128),
            cut(up_third, column * 16, 16, core * 512, 512),
            cut(up_second, column // 2 * 16, 16, core * 256 + column % 2 * 128, 128),
        ],
        axis=1,
    )[None]
    both_rest = in_order(ring, own_rest, swap_rings(own_rest), 0)
    core_place = jnp.stack([core, lax.axis_index("lat") % Z_RING]).astype(jnp.int32)
    out_third = swap_shards(out_third)
    merge_third = swap_shards(merge_third)
    qkv_third = swap_shards(qkv_third)

    picks = (land_ids[:, :, None] == jnp.arange(3, dtype=jnp.int32)).astype(jnp.float32)
    surface = jnp.einsum("ijs,sc->ijc", picks, surface_table.astype(jnp.float32))
    hidden = (
        fields.astype(jnp.float32)
        + surface[:, None, :, :]
        + level_table.astype(jnp.float32)[None, :, None, :]
    ).astype(jnp.bfloat16)
    hidden = after(hidden, both_merge)
    above, below = neighbours(hidden[:2], hidden[-2:], "lat")
    cells = jnp.concatenate([above, hidden, below], axis=0)
    cells = after(cells, both_rest)
    left, right = neighbours(cells[:, :, :2], cells[:, :, -2:], "lon")
    out_first_rows = ring_gather(after(both_rest, cells)[:, :, :128])
    left = after(left, out_first_rows, out_third, merge_third, qkv_third)
    out_first_tiles = column_gather(out_first_rows).reshape(8, Z_RING, 2, 16, 128)

    ext_rows = tile_rows + 4
    own_window = (jnp.arange(32 * 4) % tile_cols + 2) // 4
    key_window = jnp.concatenate(
        [own_window, jnp.zeros((16,), jnp.int32), jnp.full((16,), tile_cols // 4, jnp.int32)]
    )
    same_window = (own_window[:, None] == key_window[None, :]).astype(jnp.float32)
    lat_place = lax.axis_index("lat") * tile_rows + jnp.arange(ext_rows) - 2
    valid_rows = ((lat_place >= 0) & (lat_place < tile_rows * lat_count)).astype(jnp.float32)
    valid_rows = valid_rows.reshape(ext_rows // 4, 1, 4)
    valid_keys = jnp.concatenate(
        [jnp.repeat(valid_rows, 2 * count, axis=2) for count in (tile_cols, 2, 2)], axis=2
    )
    attended = call_kernel(
        first_kernel,
        jax.ShapeDtypeStruct((tile_rows * levels * tile_cols, feat_dim), jnp.bfloat16),
        (
            cells.reshape(-1, feat_dim),
            left.reshape(-1, feat_dim),
            right.reshape(-1, feat_dim),
            norm_first[None],
            qkv_first,
            same_window,
            valid_keys,
        ),
        flops=2 * 640 * 512 * 1536,
    )
    late = jnp.concatenate(
        [
            both_rest[0, :, 128:],
            both_rest[1, :, 128:],
            cut(out_third, column // 2 * 16, 16, column % 2 * 1024, 1024),
        ],
        axis=1,
    )
    late_rows = ring_gather(after(late, attended))
    tokens = attended.shape[0]
    skip_first, merged_in = call_kernel(
        skip_kernel,
        (
            jax.ShapeDtypeStruct((tokens, feat_dim), jnp.bfloat16),
            jax.ShapeDtypeStruct((tokens // 4, 4 * feat_dim), jnp.bfloat16),
        ),
        (attended, hidden.reshape(-1, feat_dim), out_first_tiles, norm_merge2[None]),
        flops=2 * 384 * 512 * 512,
    )
    merged_pair = jnp.concatenate([merged_in, swap_cores(merged_in)], axis=0)
    second_half = jnp.dot(merged_pair, merge_half, preferred_element_type=jnp.float32).astype(
        jnp.bfloat16
    )
    own_rows = merged_in.shape[0]
    second_cells, coarse_in = call_kernel(
        join_kernel,
        (
            jax.ShapeDtypeStruct((own_rows, 1024), jnp.bfloat16),
            jax.ShapeDtypeStruct((own_rows // 4, 4096), jnp.bfloat16),
        ),
        (core_place, second_half[:own_rows], swap_cores(second_half[own_rows:]), norm_merge3[None]),
        (pltpu.VMEM((2, own_rows, 512), jnp.bfloat16),),
        flops=2 * 96 * 96 * 1024,
    )
    late_rows = after(late_rows, second_half)
    late = lax.all_gather(
        late_rows,
        "lon",
        axis=0,
        axis_index_groups=[[4 * y + x for y in range(8)] for x in range(4)],
        tiled=True,
    )

    qkv_joined = jnp.concatenate([qkv_third[0], qkv_third[1], qkv_third[2]], axis=1)
    coarse_in = after(coarse_in, late_rows, qkv_joined)
    own_count = coarse_in.shape[0]
    line = Z_RING * own_count

    ring_tokens = ring_gather(coarse_in).reshape(line, -1)
    column_block = jnp.stack(
        [
            jnp.dot(tokens, merge_third, preferred_element_type=jnp.float32).astype(jnp.bfloat16)
            for tokens in (ring_tokens, swap_cores(ring_tokens))
        ]
    )
    own_columns = ring_gather(column_block)
    other_columns = swap_cores(own_columns)
    blocks, _, _, width = own_columns.shape
    head_feats = qkv_third.shape[2]
    heads_out, own_coarse = call_kernel(
        third_kernel,
        (
            jax.ShapeDtypeStruct((Z_RING, 2, own_count, head_feats), jnp.bfloat16),
            jax.ShapeDtypeStruct((own_count, 2 * blocks * width), jnp.float32),
        ),
        (
            core_place,
            own_columns,
            other_columns,
            norm_third.reshape(2 * blocks, 1, width),
            qkv_joined,
        ),
        (
            pltpu.VMEM((2 * line, 2 * blocks * width), jnp.bfloat16),
            pltpu.VMEM((line, 2 * blocks * width), jnp.float32),
        ),
        flops=2 * 384 * 2048 * 192,
    )

    chip_heads = ring_scatter(heads_out)
    own_part, send_part = call_kernel(
        heads_kernel,
        (
            jax.ShapeDtypeStruct((own_count, 2048), jnp.float32),
            jax.ShapeDtypeStruct((own_count, 2048), jnp.bfloat16),
        ),
        (chip_heads, late),
        flops=2 * 48 * 512 * 2048,
    )
    late_swapped = swap_cores(after(late, heads_out))
    decoded = call_kernel(
        up_kernel,
        jax.ShapeDtypeStruct((tile_rows * levels * tile_cols, feat_dim), jnp.bfloat16),
        (
            core_place,
            own_coarse,
            own_part,
            swap_cores(send_part),
            late,
            late_swapped,
            second_cells,
            skip_first,
        ),
        (
            pltpu.VMEM((2 * blocks, own_count, width), jnp.float32),
            pltpu.VMEM((2, own_count, 512), jnp.float32),
            pltpu.VMEM((second_cells.shape[0], 1024), jnp.bfloat16),
            pltpu.VMEM((2, second_cells.shape[0], 256), jnp.float32),
        ),
        flops=2 * (24 * 2048 * 1024 + 96 * 1024 * 512),
    )
    return decoded.reshape(fields.shape)


def solution(mesh):
    in_specs = (
        P("lat", None, "lon", None),
        P("lat", "lon"),
        P(),
        P(),
        P(),
        P(),
        P("lat", None),
        P(),
        P("lat", None),
        P(),
        P(None, "lat"),
        P(),
        P(None, None, "lat"),
        P("lat", None),
        P("lat", None),
        P("lat", None),
    )
    out_specs = P("lat", None, "lon", None)
    return jax.shard_map(
        on_device, mesh=mesh, in_specs=in_specs, out_specs=out_specs, check_vma=False
    )
```

```python
import jax
import jax.numpy as jnp
from jax import lax
from jax.experimental import pallas as pl
from jax.experimental.pallas import tpu as pltpu
from jax.sharding import PartitionSpec as P

HD = 64


def norm_rows(values, gain):
    row_mean = jnp.mean(values, axis=-1, keepdims=True)
    centred = values - row_mean
    spread = jnp.mean(centred * centred, axis=-1, keepdims=True)
    return centred * lax.rsqrt(spread + 1e-05) * gain


def call_kernel(body, out_shape, operands, scratch=(), flops=0):
    smem = [operand.dtype == jnp.int32 for operand in operands]
    return pl.pallas_call(
        body,
        out_shape=out_shape,
        in_specs=[
            pl.BlockSpec(memory_space=pltpu.SMEM if scalar else pltpu.VMEM) for scalar in smem
        ],
        out_specs=jax.tree.map(lambda _: pl.BlockSpec(memory_space=pltpu.VMEM), out_shape),
        scratch_shapes=list(scratch),
        compiler_params=pltpu.CompilerParams(vmem_limit_bytes=48 * 1024 * 1024),
        cost_estimate=pl.CostEstimate(
            flops=flops,
            bytes_accessed=sum(operand.size * operand.dtype.itemsize for operand in operands),
            transcendentals=0,
        ),
    )(*operands)


def dot_rows(left, right):
    return lax.dot_general(left, right, (((1,), (0,)), ((), ())), preferred_element_type=jnp.float32)


def mix_tokens(query, key, value, keep):
    scores = lax.dot_general(
        key, query, (((1,), (1,)), ((), ())), preferred_element_type=jnp.float32
    )
    scores = jnp.where(keep, scores, -1e30)
    weights = jnp.exp(scores - jnp.max(scores, axis=0, keepdims=True))
    weights = (weights / jnp.sum(weights, axis=0, keepdims=True)).astype(jnp.bfloat16)
    return lax.dot_general(
        weights, value, (((0,), (0,)), ((), ())), preferred_element_type=jnp.float32
    )


def first_kernel(x_ref, left_ref, right_ref, gain_ref, qkv_ref, window_ref, lat_ref, out_ref):
    steps = lat_ref.shape[0]
    own, side = x_ref.shape[0] // steps, left_ref.shape[0] // steps
    lane = lax.broadcasted_iota(jnp.int32, (own, 128), 1)
    key_lane = lax.broadcasted_iota(jnp.int32, (own + 2 * side, 128), 1)
    gain = gain_ref[...]
    for step in range(steps):
        rows = jnp.concatenate(
            [
                x_ref[step * own : (step + 1) * own, :],
                left_ref[step * side : (step + 1) * side, :],
                right_ref[step * side : (step + 1) * side, :],
            ],
            axis=0,
        )
        normed = norm_rows(rows.astype(jnp.float32), gain).astype(jnp.bfloat16)
        query = dot_rows(normed[:own], qkv_ref[0]).astype(jnp.bfloat16)
        query = (query * 0.125).astype(jnp.bfloat16)
        key = dot_rows(normed, qkv_ref[1]).astype(jnp.bfloat16)
        value = dot_rows(normed, qkv_ref[2]).astype(jnp.bfloat16)
        keep = window_ref[...] * lat_ref[step] > 0.0
        first = own // 2 if step == 0 else 0
        last = own // 2 if step == steps - 1 else own
        start = step * own - own // 2 + first
        for pair in range(query.shape[1] // 128):
            here = slice(pair * 128, pair * 128 + 128)
            parts = []
            for odd in range(2):
                picked = (key_lane < HD) if odd == 0 else (key_lane >= HD)
                key_side = jnp.where(picked, key[:, here], jnp.zeros_like(key[:, here]))
                parts.append(mix_tokens(query[:, here], key_side, value[:, here], keep))
            mixed = jnp.where(lane < HD, parts[0], parts[1]).astype(jnp.bfloat16)
            out_ref[start : start + last - first, here] = mixed[first:last]


def pick_matrix(lat_count, lon_count, lat_side, lon_side):
    shape = (2 * lat_count * lon_count, 8 * lat_count * lon_count)
    row = lax.broadcasted_iota(jnp.int32, shape, 0)
    column = lax.broadcasted_iota(jnp.int32, shape, 1)
    bits = lon_count.bit_length() - 1
    lon = row & (lon_count - 1)
    level = jnp.right_shift(row, bits) & 1
    lat = jnp.right_shift(row, bits + 1)
    source = ((2 * lat + lat_side) * 2 + level) * (2 * lon_count) + 2 * lon + lon_side
    return jnp.where(source == column, 1.0, 0.0).astype(jnp.bfloat16)


def join_quads(cells, lat_count, lon_count, gain_ref, out_ref):
    width = cells.shape[1]
    parts = [
        dot_rows(pick_matrix(lat_count, lon_count, lat_side, lon_side), cells)
        for lat_side in range(2)
        for lon_side in range(2)
    ]
    count = 1.0 / (4 * width)
    row_mean = sum(jnp.sum(part, axis=-1, keepdims=True) for part in parts) * count
    parts = [part - row_mean for part in parts]
    spread = sum(jnp.sum(part * part, axis=-1, keepdims=True) for part in parts) * count
    scale = lax.rsqrt(spread + 1e-05)
    for place, part in enumerate(parts):
        here = slice(place * width, place * width + width)
        out_ref[:, here] = (part * scale * gain_ref[:, here]).astype(jnp.bfloat16)


def skip_kernel(attended_ref, hidden_ref, weights_ref, gain_ref, skip_ref, merged_ref):
    total = None
    for ring in range(2):
        for z in range(0, 8, 4):
            right = jnp.concatenate(
                [weights_ref[ring, zz * 160 + 128 : zz * 160 + 160, :] for zz in range(z, z + 4)],
                axis=0,
            )
            start = (ring * 8 + z) * 32
            product = dot_rows(attended_ref[:, start : start + 128], right)
            total = product if total is None else total + product
    skip = (hidden_ref[...].astype(jnp.float32) + total).astype(jnp.bfloat16)
    skip_ref[...] = skip
    join_quads(skip, 6, 8, gain_ref, merged_ref)


def merge_kernel(own_ref, other_ref, weights_ref, own_out_ref, send_ref):
    left = jnp.concatenate([own_ref[...], other_ref[...]], axis=0)
    total = None
    for ring in range(2):
        for z in range(0, 8, 2):
            right = jnp.concatenate(
                [weights_ref[ring, zz * 160 : zz * 160 + 128, :] for zz in (z, z + 1)], axis=0
            )
            start = (ring * 8 + z) * 128
            product = dot_rows(left[:, start : start + 256], right)
            total = product if total is None else total + product
    rows = own_ref.shape[0]
    own_out_ref[...] = total[:rows].astype(jnp.bfloat16)
    send_ref[...] = total[rows:].astype(jnp.bfloat16)


def join_kernel(core_ref, own_ref, recv_ref, gain_ref, second_ref, coarse_ref, halves_ref):
    core = core_ref[0]
    halves_ref[core] = own_ref[...]
    halves_ref[1 - core] = recv_ref[...]
    second = jnp.concatenate([halves_ref[0], halves_ref[1]], axis=1)
    second_ref[...] = second
    join_quads(second, 3, 4, gain_ref, coarse_ref)


RING_ORDER = (0, -1, 1, -2, 2, -3, 3, 4)


def columns_kernel(place_ref, near_ref, far_ref, near_other_ref, far_other_ref, weights_ref, out_ref):
    for side, refs in enumerate(((near_ref, far_ref), (near_other_ref, far_other_ref))):
        places = iter(RING_ORDER)
        for ref in refs:
            count, rows, width = ref.shape
            left = jnp.concatenate([ref[at].astype(jnp.float32) for at in range(count)], axis=0)
            product = dot_rows(left.astype(jnp.bfloat16), weights_ref[...])
            for at in range(count):
                place = jnp.bitwise_and(place_ref[1] + (next(places) + 8), 7)
                out_ref[side, place] = product[at * rows : (at + 1) * rows].astype(jnp.bfloat16)


def third_kernel(
    core_ref, own_ref, other_ref, gain_ref, qkv_ref, out_ref, coarse_ref, normed_ref, raw_ref
):
    blocks, sides, line, width = own_ref.shape
    core = core_ref[0]
    half = blocks * width
    count = 1.0 / (2 * half)
    rows = 32
    for side in range(sides):
        for start in range(0, line, rows):
            mine = slice(start, start + rows)
            tiles = [own_ref[z, side, mine, :].astype(jnp.float32) for z in range(blocks)]
            tiles += [other_ref[z, 1 - side, mine, :].astype(jnp.float32) for z in range(blocks)]
            if side == 0:
                for place, tile in enumerate(tiles):
                    raw_ref[mine, place * width : (place + 1) * width] = tile
            row_mean = jnp.sum(sum(tiles), axis=-1, keepdims=True) * count
            tiles = [tile - row_mean for tile in tiles]
            spread = jnp.sum(sum(tile * tile for tile in tiles), axis=-1, keepdims=True)
            scale = lax.rsqrt(spread * count + 1e-05)
            for place, tile in enumerate(tiles):
                origin = core if place < blocks else 1 - core
                gain = gain_ref[origin * blocks + place % blocks]
                normed_ref[
                    side * line + start : side * line + start + rows,
                    place * width : (place + 1) * width,
                ] = (tile * scale * gain).astype(jnp.bfloat16)
    tokens = line // blocks
    coarse_ref[...] = raw_ref[pl.ds(pl.multiple_of(core_ref[1] * tokens, 8), tokens), :]
    own_rows = pl.multiple_of(core * half, half)
    other_rows = pl.multiple_of((1 - core) * half, half)
    triple = (
        dot_rows(normed_ref[:, :half], qkv_ref[pl.ds(own_rows, half), :])
        + dot_rows(normed_ref[:, half:], qkv_ref[pl.ds(other_rows, half), :])
    ).astype(jnp.bfloat16)
    query = (triple[:, :HD] * 0.125).astype(jnp.bfloat16)
    key = triple[:, HD : 2 * HD]
    value = triple[:, 2 * HD :]
    token = lax.broadcasted_iota(jnp.int32, (128, 128), 0)
    other = lax.broadcasted_iota(jnp.int32, (128, 128), 1)
    keep = jnp.right_shift(token, 5) == jnp.right_shift(other, 5)
    mixed = []
    for group in range(sides * line // 128):
        mine = slice(group * 128, group * 128 + 128)
        mixed.append(mix_tokens(query[mine], key[mine], value[mine], keep))
    mixed = jnp.concatenate(mixed, axis=0)
    for z in range(blocks):
        for side in range(sides):
            start = side * line + z * tokens
            out_ref[z, side] = mixed[start : start + tokens].astype(jnp.bfloat16)


def heads_kernel(heads_ref, late_ref, own_ref, send_ref):
    total = [None, None]
    for z in range(heads_ref.shape[0]):
        left = jnp.concatenate(
            [heads_ref[z, 0].astype(jnp.float32), heads_ref[z, 1].astype(jnp.float32)], axis=0
        ).astype(jnp.bfloat16)
        for part in range(2):
            right = jnp.concatenate(
                [late_ref[(2 * row + part) * 8 + z, :, 1280:2304] for row in range(4)], axis=0
            )
            product = dot_rows(left, right)
            total[part] = product if z == 0 else total[part] + product
    count = heads_ref.shape[2]
    for part in range(2):
        here = slice(part * 1024, part * 1024 + 1024)
        own_ref[:, here] = total[part][:count]
        send_ref[:, here] = total[part][count:].astype(jnp.bfloat16)


def spread_matrix(lat_count, lon_count):
    fine = (2 * lat_count * lon_count, lat_count * lon_count // 2)
    row = lax.broadcasted_iota(jnp.int32, fine, 0)
    column = lax.broadcasted_iota(jnp.int32, fine, 1)
    bits = lon_count.bit_length() - 1
    lat = jnp.right_shift(row, bits + 2)
    level = jnp.right_shift(row, bits) & 1
    lon = jnp.right_shift(row & (lon_count - 1), 1)
    source = (lat * 2 + level) * (lon_count // 2) + lon
    return jnp.where(source == column, 1.0, 0.0).astype(jnp.float32)


def spread_rows(values, lat_count, lon_count):
    return lax.dot_general(
        spread_matrix(lat_count, lon_count),
        values,
        (((1,), (0,)), ((), ())),
        precision=lax.Precision.HIGHEST,
        preferred_element_type=jnp.float32,
    )


def up_kernel(
    core_ref, own_coarse_ref, part_ref, recv_ref, late_ref, swapped_ref,
    second_ref, skip_ref, out_ref, coarse_ref, lift_ref, level_ref, small_ref,
):
    core = core_ref[0]
    blocks, width = 8, 128
    for z in range(blocks):
        for place, origin in ((z, core), (blocks + z, 1 - core)):
            coarse_ref[origin * blocks + z] = own_coarse_ref[:, place * width : (place + 1) * width]
    level_three = []
    for place in range(2 * blocks):
        here = slice(place * width, place * width + width)
        level_three.append(
            (coarse_ref[place] + (part_ref[:, here] + recv_ref[:, here].astype(jnp.float32))).astype(
                jnp.bfloat16
            )
        )
    for weights_ref, origin in ((late_ref, core), (swapped_ref, 1 - core)):
        total = None
        for ring in range(2):
            for z in range(8):
                right = jnp.concatenate(
                    [weights_ref[y * 8 + z, :, ring * 640 : ring * 640 + 512] for y in range(8)],
                    axis=0,
                )
                product = dot_rows(level_three[ring * 8 + z], right)
                total = product if total is None else total + product
        lift_ref[origin] = total
    lat_count, lon_count = 6, 8
    for side in range(2):
        here = slice(side * 512, side * 512 + 512)
        level_ref[:, here] = (
            second_ref[:, here].astype(jnp.float32)
            + spread_rows(lift_ref[side], lat_count, lon_count)
        ).astype(jnp.bfloat16)
    for weights_ref, origin in ((late_ref, core), (swapped_ref, 1 - core)):
        total = None
        for ring in range(2):
            for z in range(0, 8, 2):
                right = jnp.concatenate(
                    [
                        jnp.concatenate(
                            [
                                weights_ref[
                                    (2 * row + part) * 8 + zz, :, ring * 640 + 512 : ring * 640 + 640
                                ]
                                for zz in (z, z + 1)
                                for row in range(4)
                            ],
                            axis=0,
                        )
                        for part in range(2)
                    ],
                    axis=1,
                )
                start = (ring * 8 + z) * 64
                product = dot_rows(level_ref[:, start : start + 128], right)
                total = product if total is None else total + product
        small_ref[origin] = total
    for side in range(2):
        here = slice(side * 256, side * 256 + 256)
        out_ref[:, here] = (
            skip_ref[:, here].astype(jnp.float32)
            + spread_rows(small_ref[side], 2 * lat_count, 2 * lon_count)
        ).astype(jnp.bfloat16)


Z_RING = 8
RINGS = [[ring * Z_RING + place for place in range(Z_RING)] for ring in range(2)]


def neighbours(first, last, axis):
    count = lax.axis_size(axis)
    before = lax.ppermute(last, axis, [(i, (i + 1) % count) for i in range(count)])
    behind = lax.ppermute(first, axis, [((i + 1) % count, i) for i in range(count)])
    return before, behind


def swap_cores(values):
    count = lax.axis_size("lon")
    return lax.ppermute(values, "lon", [(i, i ^ 1) for i in range(count)])


def swap_rings(values):
    count = lax.axis_size("lat")
    return lax.ppermute(values, "lat", [(i, (i + Z_RING) % count) for i in range(count)])


def swap_shards(values):
    lon_count = lax.axis_size("lon")
    pairs = []
    for lat in range(lax.axis_size("lat")):
        for lon in range(lon_count):
            ring, place = divmod(lat, Z_RING)
            target = (lat, lon)
            if ring != lon % 2:
                target = ((1 - ring) * Z_RING + place, lon ^ 1)
            pairs.append((lat * lon_count + lon, target[0] * lon_count + target[1]))
    return lax.ppermute(values, ("lat", "lon"), pairs)


def ring_scatter(blocks):
    return lax.all_to_all(blocks, "lat", 0, 0, axis_index_groups=RINGS, tiled=True)


def ring_shift(values, step):
    pairs = [(at, at // Z_RING * Z_RING + (at + step) % Z_RING) for at in range(2 * Z_RING)]
    return lax.ppermute(values, "lat", pairs)


def ring_gather(values):
    return ring_scatter(jnp.broadcast_to(values[None], (Z_RING,) + values.shape))


def in_order(flag, own, other, axis):
    return jnp.where(
        flag == 0,
        jnp.concatenate([own, other], axis=axis),
        jnp.concatenate([other, own], axis=axis),
    )


def cut(values, row, rows, column, columns):
    return lax.dynamic_slice(values, (row, column), (rows, columns))


def after(values, *before):
    return lax.optimization_barrier((values,) + before)[0]


def on_device(
    fields,
    land_ids,
    surface_table,
    level_table,
    norm_first,
    qkv_first,
    out_first,
    norm_merge2,
    merge_second,
    norm_merge3,
    merge_third,
    norm_third,
    qkv_third,
    out_third,
    up_third,
    up_second,
):
    tile_rows, levels, tile_cols, feat_dim = fields.shape
    lat_count = lax.axis_size("lat")
    ring = lax.axis_index("lat") // Z_RING
    core = lax.axis_index("lon") % 2
    column = lax.axis_index("lon") // 4

    own_merge = jnp.concatenate(
        [lax.dynamic_slice_in_dim(merge_second, core * 512, 512, 1), out_first], axis=0
    )[None]
    both_merge = in_order(ring, own_merge, swap_rings(own_merge), 0)
    merge_weights = lax.all_gather(
        both_merge, "lat", axis=1, axis_index_groups=RINGS, tiled=True
    )
    core_place = jnp.stack([core, lax.axis_index("lat") % Z_RING]).astype(jnp.int32)
    picks = (land_ids[:, :, None] == jnp.arange(3, dtype=jnp.int32)).astype(jnp.float32)
    surface = jnp.einsum("ijs,sc->ijc", picks, surface_table.astype(jnp.float32))
    hidden = (
        fields.astype(jnp.float32)
        + surface[:, None, :, :]
        + level_table.astype(jnp.float32)[None, :, None, :]
    ).astype(jnp.bfloat16)
    hidden = after(hidden, both_merge)
    above, below = neighbours(hidden[:2], hidden[-2:], "lat")
    cells = jnp.concatenate([above, hidden, below], axis=0)
    left, right = neighbours(cells[:, :, :2], cells[:, :, -2:], "lon")

    out_third, merge_third, qkv_third, up_third, up_second, _, _ = lax.optimization_barrier(
        (out_third, merge_third, qkv_third, up_third, up_second, left, right)
    )
    own_rest = jnp.concatenate(
        [
            cut(up_third, column * 16, 16, core * 512, 512),
            cut(up_second, column // 2 * 16, 16, core * 256 + column % 2 * 128, 128),
        ],
        axis=1,
    )[None]
    both_rest = in_order(ring, own_rest, swap_rings(own_rest), 0)
    out_third = swap_shards(out_third)
    merge_third = swap_shards(merge_third)
    qkv_third = swap_shards(qkv_third)
    late = jnp.concatenate(
        [
            both_rest[0],
            both_rest[1],
            cut(out_third, column // 2 * 16, 16, column % 2 * 1024, 1024),
        ],
        axis=1,
    )
    qkv_joined = jnp.concatenate([qkv_third[0], qkv_third[1], qkv_third[2]], axis=1)

    ext_rows = tile_rows + 4
    own_window = (jnp.arange(32 * 4) % tile_cols + 2) // 4
    key_window = jnp.concatenate(
        [own_window, jnp.zeros((16,), jnp.int32), jnp.full((16,), tile_cols // 4, jnp.int32)]
    )
    same_window = (key_window[:, None] == own_window[None, :]).astype(jnp.float32)
    lat_place = lax.axis_index("lat") * tile_rows + jnp.arange(ext_rows) - 2
    valid_rows = ((lat_place >= 0) & (lat_place < tile_rows * lat_count)).astype(jnp.float32)
    valid_rows = valid_rows.reshape(ext_rows // 4, 4, 1)
    valid_keys = jnp.concatenate(
        [jnp.repeat(valid_rows, 2 * count, axis=1) for count in (tile_cols, 2, 2)], axis=1
    )
    attended = call_kernel(
        first_kernel,
        jax.ShapeDtypeStruct((tile_rows * levels * tile_cols, feat_dim), jnp.bfloat16),
        (
            cells.reshape(-1, feat_dim),
            left.reshape(-1, feat_dim),
            right.reshape(-1, feat_dim),
            norm_first[None],
            qkv_first,
            same_window,
            valid_keys,
        ),
        flops=2 * 640 * 512 * 1536,
    )
    attended = after(attended, late, merge_third, qkv_joined)
    tokens = attended.shape[0]
    skip_first, merged_in = call_kernel(
        skip_kernel,
        (
            jax.ShapeDtypeStruct((tokens, feat_dim), jnp.bfloat16),
            jax.ShapeDtypeStruct((tokens // 4, 4 * feat_dim), jnp.bfloat16),
        ),
        (attended, hidden.reshape(-1, feat_dim), merge_weights, norm_merge2[None]),
        flops=2 * 384 * 512 * 512,
    )
    late_rows = ring_gather(after(late, merged_in))
    own_rows = merged_in.shape[0]
    half_shape = jax.ShapeDtypeStruct((own_rows, 512), jnp.bfloat16)
    second_half, second_send = call_kernel(
        merge_kernel,
        (half_shape, half_shape),
        (merged_in, swap_cores(merged_in), merge_weights),
        flops=2 * 192 * 2048 * 512,
    )
    second_cells, coarse_in = call_kernel(
        join_kernel,
        (
            jax.ShapeDtypeStruct((own_rows, 1024), jnp.bfloat16),
            jax.ShapeDtypeStruct((own_rows // 4, 4096), jnp.bfloat16),
        ),
        (core_place, second_half, swap_cores(second_send), norm_merge3[None]),
        (pltpu.VMEM((2, own_rows, 512), jnp.bfloat16),),
        flops=2 * 96 * 96 * 1024,
    )
    late_rows = after(late_rows, coarse_in)
    late = lax.all_gather(
        late_rows,
        "lon",
        axis=0,
        axis_index_groups=[[4 * y + x for y in range(8)] for x in range(4)],
        tiled=True,
    )

    own_count = coarse_in.shape[0]
    line = Z_RING * own_count

    pieces, forth, back = [coarse_in], coarse_in, coarse_in
    for _ in range(3):
        forth, back = ring_shift(forth, 1), ring_shift(back, -1)
        pieces += [forth, back]
    half_feats = coarse_in.shape[1] // 2
    pieces.append(
        jnp.concatenate(
            [ring_shift(forth[:, :half_feats], 1), ring_shift(back[:, half_feats:], -1)], axis=1
        )
    )
    near, far = jnp.stack(pieces[:5]), jnp.stack(pieces[5:])
    column_block = call_kernel(
        columns_kernel,
        jax.ShapeDtypeStruct((2, Z_RING, own_count, 128), jnp.bfloat16),
        (core_place, near, far, swap_cores(near), swap_cores(far), merge_third),
        flops=2 * 384 * 4096 * 128,
    ).reshape(2, line, 128)
    own_columns = ring_gather(column_block)
    other_columns = swap_cores(own_columns)
    blocks, _, _, width = own_columns.shape
    head_feats = qkv_third.shape[2]
    heads_out, own_coarse = call_kernel(
        third_kernel,
        (
            jax.ShapeDtypeStruct((Z_RING, 2, own_count, head_feats), jnp.bfloat16),
            jax.ShapeDtypeStruct((own_count, 2 * blocks * width), jnp.float32),
        ),
        (
            core_place,
            own_columns,
            other_columns,
            norm_third.reshape(2 * blocks, 1, width),
            qkv_joined,
        ),
        (
            pltpu.VMEM((2 * line, 2 * blocks * width), jnp.bfloat16),
            pltpu.VMEM((line, 2 * blocks * width), jnp.float32),
        ),
        flops=2 * 384 * 2048 * 192,
    )

    chip_heads = ring_scatter(heads_out)
    own_part, send_part = call_kernel(
        heads_kernel,
        (
            jax.ShapeDtypeStruct((own_count, 2048), jnp.float32),
            jax.ShapeDtypeStruct((own_count, 2048), jnp.bfloat16),
        ),
        (chip_heads, late),
        flops=2 * 48 * 512 * 2048,
    )
    late_swapped = swap_cores(after(late, heads_out))
    decoded = call_kernel(
        up_kernel,
        jax.ShapeDtypeStruct((tile_rows * levels * tile_cols, feat_dim), jnp.bfloat16),
        (
            core_place,
            own_coarse,
            own_part,
            swap_cores(send_part),
            late,
            late_swapped,
            second_cells,
            skip_first,
        ),
        (
            pltpu.VMEM((2 * blocks, own_count, width), jnp.float32),
            pltpu.VMEM((2, own_count, 512), jnp.float32),
            pltpu.VMEM((second_cells.shape[0], 1024), jnp.bfloat16),
            pltpu.VMEM((2, second_cells.shape[0], 256), jnp.float32),
        ),
        flops=2 * (24 * 2048 * 1024 + 96 * 1024 * 512),
    )
    return decoded.reshape(fields.shape)


def solution(mesh):
    in_specs = (
        P("lat", None, "lon", None),
        P("lat", "lon"),
        P(),
        P(),
        P(),
        P(),
        P("lat", None),
        P(),
        P("lat", None),
        P(),
        P(None, "lat"),
        P(),
        P(None, None, "lat"),
        P("lat", None),
        P("lat", None),
        P("lat", None),
    )
    out_specs = P("lat", None, "lon", None)
    return jax.shard_map(
        on_device, mesh=mesh, in_specs=in_specs, out_specs=out_specs, check_vma=False
    )
```

```python
import jax
import jax.numpy as jnp
from jax import lax
from jax.experimental import pallas as pl
from jax.experimental.pallas import tpu as pltpu
from jax.sharding import PartitionSpec as P

HD = 64


def norm_rows(values, gain):
    row_mean = jnp.mean(values, axis=-1, keepdims=True)
    centred = values - row_mean
    spread = jnp.mean(centred * centred, axis=-1, keepdims=True)
    return centred * lax.rsqrt(spread + 1e-05) * gain


def call_kernel(body, out_shape, operands, scratch=(), flops=0):
    smem = [operand.dtype == jnp.int32 for operand in operands]
    return pl.pallas_call(
        body,
        out_shape=out_shape,
        in_specs=[
            pl.BlockSpec(memory_space=pltpu.SMEM if scalar else pltpu.VMEM) for scalar in smem
        ],
        out_specs=jax.tree.map(lambda _: pl.BlockSpec(memory_space=pltpu.VMEM), out_shape),
        scratch_shapes=list(scratch),
        compiler_params=pltpu.CompilerParams(vmem_limit_bytes=48 * 1024 * 1024),
        cost_estimate=pl.CostEstimate(
            flops=flops,
            bytes_accessed=sum(operand.size * operand.dtype.itemsize for operand in operands),
            transcendentals=0,
        ),
    )(*operands)


def dot_rows(left, right):
    return lax.dot_general(left, right, (((1,), (0,)), ((), ())), preferred_element_type=jnp.float32)


def mix_tokens(query, key, value, keep):
    scores = lax.dot_general(
        key, query, (((1,), (1,)), ((), ())), preferred_element_type=jnp.float32
    )
    scores = jnp.where(keep, scores, -1e30)
    weights = jnp.exp(scores - jnp.max(scores, axis=0, keepdims=True))
    weights = (weights / jnp.sum(weights, axis=0, keepdims=True)).astype(jnp.bfloat16)
    return lax.dot_general(
        weights, value, (((0,), (0,)), ((), ())), preferred_element_type=jnp.float32
    )


def first_kernel(x_ref, left_ref, right_ref, gain_ref, qkv_ref, window_ref, lat_ref, out_ref):
    steps = lat_ref.shape[0]
    own, side = x_ref.shape[0] // steps, left_ref.shape[0] // steps
    lane = lax.broadcasted_iota(jnp.int32, (own, 128), 1)
    key_lane = lax.broadcasted_iota(jnp.int32, (own + 2 * side, 128), 1)
    gain = gain_ref[...]
    for step in range(steps):
        rows = jnp.concatenate(
            [
                x_ref[step * own : (step + 1) * own, :],
                left_ref[step * side : (step + 1) * side, :],
                right_ref[step * side : (step + 1) * side, :],
            ],
            axis=0,
        )
        normed = norm_rows(rows.astype(jnp.float32), gain).astype(jnp.bfloat16)
        query = dot_rows(normed[:own], qkv_ref[0]).astype(jnp.bfloat16)
        query = (query * 0.125).astype(jnp.bfloat16)
        key = dot_rows(normed, qkv_ref[1]).astype(jnp.bfloat16)
        value = dot_rows(normed, qkv_ref[2]).astype(jnp.bfloat16)
        keep = window_ref[...] * lat_ref[step] > 0.0
        first = own // 2 if step == 0 else 0
        last = own // 2 if step == steps - 1 else own
        start = step * own - own // 2 + first
        for pair in range(query.shape[1] // 128):
            here = slice(pair * 128, pair * 128 + 128)
            parts = []
            for odd in range(2):
                picked = (key_lane < HD) if odd == 0 else (key_lane >= HD)
                key_side = jnp.where(picked, key[:, here], jnp.zeros_like(key[:, here]))
                parts.append(mix_tokens(query[:, here], key_side, value[:, here], keep))
            mixed = jnp.where(lane < HD, parts[0], parts[1]).astype(jnp.bfloat16)
            out_ref[start : start + last - first, here] = mixed[first:last]


def pick_matrix(lat_count, lon_count, lat_side, lon_side):
    shape = (2 * lat_count * lon_count, 8 * lat_count * lon_count)
    row = lax.broadcasted_iota(jnp.int32, shape, 0)
    column = lax.broadcasted_iota(jnp.int32, shape, 1)
    bits = lon_count.bit_length() - 1
    lon = row & (lon_count - 1)
    level = jnp.right_shift(row, bits) & 1
    lat = jnp.right_shift(row, bits + 1)
    source = ((2 * lat + lat_side) * 2 + level) * (2 * lon_count) + 2 * lon + lon_side
    return jnp.where(source == column, 1.0, 0.0).astype(jnp.bfloat16)


def join_quads(cells, lat_count, lon_count, gain_ref, out_ref):
    width = cells.shape[1]
    parts = [
        dot_rows(pick_matrix(lat_count, lon_count, lat_side, lon_side), cells)
        for lat_side in range(2)
        for lon_side in range(2)
    ]
    count = 1.0 / (4 * width)
    row_mean = sum(jnp.sum(part, axis=-1, keepdims=True) for part in parts) * count
    parts = [part - row_mean for part in parts]
    spread = sum(jnp.sum(part * part, axis=-1, keepdims=True) for part in parts) * count
    scale = lax.rsqrt(spread + 1e-05)
    for place, part in enumerate(parts):
        here = slice(place * width, place * width + width)
        out_ref[:, here] = (part * scale * gain_ref[:, here]).astype(jnp.bfloat16)


def skip_kernel(attended_ref, hidden_ref, weights_ref, gain_ref, skip_ref, merged_ref):
    total = None
    for ring in range(2):
        for z in range(0, 8, 4):
            right = jnp.concatenate(
                [weights_ref[ring, zz * 160 + 128 : zz * 160 + 160, :] for zz in range(z, z + 4)],
                axis=0,
            )
            start = (ring * 8 + z) * 32
            product = dot_rows(attended_ref[:, start : start + 128], right)
            total = product if total is None else total + product
    skip = (hidden_ref[...].astype(jnp.float32) + total).astype(jnp.bfloat16)
    skip_ref[...] = skip
    join_quads(skip, 6, 8, gain_ref, merged_ref)


def merge_kernel(own_ref, other_ref, weights_ref, own_out_ref, send_ref):
    left = jnp.concatenate([own_ref[...], other_ref[...]], axis=0)
    total = None
    for ring in range(2):
        for z in range(0, 8, 2):
            right = jnp.concatenate(
                [weights_ref[ring, zz * 160 : zz * 160 + 128, :] for zz in (z, z + 1)], axis=0
            )
            start = (ring * 8 + z) * 128
            product = dot_rows(left[:, start : start + 256], right)
            total = product if total is None else total + product
    rows = own_ref.shape[0]
    own_out_ref[...] = total[:rows].astype(jnp.bfloat16)
    send_ref[...] = total[rows:].astype(jnp.bfloat16)


def join_kernel(core_ref, own_ref, recv_ref, gain_ref, second_ref, coarse_ref, halves_ref):
    core = core_ref[0]
    halves_ref[core] = own_ref[...]
    halves_ref[1 - core] = recv_ref[...]
    second = jnp.concatenate([halves_ref[0], halves_ref[1]], axis=1)
    second_ref[...] = second
    join_quads(second, 3, 4, gain_ref, coarse_ref)


RING_ORDER = (0, -1, 1, -2, 2, -3, 3, 4)


def columns_kernel(place_ref, near_ref, far_ref, near_other_ref, far_other_ref, weights_ref, out_ref):
    for side, (near, far) in enumerate(((near_ref, far_ref), (near_other_ref, far_other_ref))):
        count, rows, width = near.shape
        tiles = [near[at].astype(jnp.float32) for at in range(count)]
        tiles.append(far[...].astype(jnp.float32))
        left = jnp.concatenate(tiles, axis=0).astype(jnp.bfloat16)
        product = dot_rows(left, weights_ref[...])
        for at, offset in enumerate(RING_ORDER):
            place = jnp.bitwise_and(place_ref[1] + (offset + 8), 7)
            out_ref[side, place] = product[at * rows : (at + 1) * rows].astype(jnp.bfloat16)


def third_kernel(
    core_ref, own_ref, other_ref, gain_ref, qkv_ref, out_ref, coarse_ref, normed_ref, raw_ref
):
    blocks, sides, line, width = own_ref.shape
    core = core_ref[0]
    half = blocks * width
    count = 1.0 / (2 * half)
    rows = 32
    for side in range(sides):
        for start in range(0, line, rows):
            mine = slice(start, start + rows)
            tiles = [own_ref[z, side, mine, :].astype(jnp.float32) for z in range(blocks)]
            tiles += [other_ref[z, 1 - side, mine, :].astype(jnp.float32) for z in range(blocks)]
            if side == 0:
                for place, tile in enumerate(tiles):
                    raw_ref[mine, place * width : (place + 1) * width] = tile
            row_mean = jnp.sum(sum(tiles), axis=-1, keepdims=True) * count
            tiles = [tile - row_mean for tile in tiles]
            spread = jnp.sum(sum(tile * tile for tile in tiles), axis=-1, keepdims=True)
            scale = lax.rsqrt(spread * count + 1e-05)
            for place, tile in enumerate(tiles):
                origin = core if place < blocks else 1 - core
                gain = gain_ref[origin * blocks + place % blocks]
                normed_ref[
                    side * line + start : side * line + start + rows,
                    place * width : (place + 1) * width,
                ] = (tile * scale * gain).astype(jnp.bfloat16)
    tokens = line // blocks
    coarse_ref[...] = raw_ref[pl.ds(pl.multiple_of(core_ref[1] * tokens, 8), tokens), :]
    triple = None
    for place, origin in ((0, core), (half, 1 - core)):
        columns = pl.ds(pl.multiple_of(origin * half, half), half)
        product = lax.dot_general(
            normed_ref[:, place : place + half],
            qkv_ref[:, columns],
            (((1,), (1,)), ((), ())),
            preferred_element_type=jnp.float32,
        )
        triple = product if triple is None else triple + product
    triple = triple.astype(jnp.bfloat16)
    query = (triple[:, :HD] * 0.125).astype(jnp.bfloat16)
    key = triple[:, HD : 2 * HD]
    value = triple[:, 2 * HD :]
    token = lax.broadcasted_iota(jnp.int32, (128, 128), 0)
    other = lax.broadcasted_iota(jnp.int32, (128, 128), 1)
    keep = jnp.right_shift(token, 5) == jnp.right_shift(other, 5)
    mixed = []
    for group in range(sides * line // 128):
        mine = slice(group * 128, group * 128 + 128)
        mixed.append(mix_tokens(query[mine], key[mine], value[mine], keep))
    mixed = jnp.concatenate(mixed, axis=0)
    for z in range(blocks):
        for side in range(sides):
            start = side * line + z * tokens
            out_ref[z, side] = mixed[start : start + tokens].astype(jnp.bfloat16)


def heads_kernel(heads_ref, late_ref, own_ref, send_ref):
    total = [None, None]
    for z in range(heads_ref.shape[0]):
        left = jnp.concatenate(
            [heads_ref[z, 0].astype(jnp.float32), heads_ref[z, 1].astype(jnp.float32)], axis=0
        ).astype(jnp.bfloat16)
        for part in range(2):
            right = jnp.concatenate(
                [late_ref[(2 * row + part) * 8 + z, :, 1280:2304] for row in range(4)], axis=0
            )
            product = dot_rows(left, right)
            total[part] = product if z == 0 else total[part] + product
    count = heads_ref.shape[2]
    for part in range(2):
        here = slice(part * 1024, part * 1024 + 1024)
        own_ref[:, here] = total[part][:count]
        send_ref[:, here] = total[part][count:].astype(jnp.bfloat16)


def spread_matrix(lat_count, lon_count):
    fine = (2 * lat_count * lon_count, lat_count * lon_count // 2)
    row = lax.broadcasted_iota(jnp.int32, fine, 0)
    column = lax.broadcasted_iota(jnp.int32, fine, 1)
    bits = lon_count.bit_length() - 1
    lat = jnp.right_shift(row, bits + 2)
    level = jnp.right_shift(row, bits) & 1
    lon = jnp.right_shift(row & (lon_count - 1), 1)
    source = (lat * 2 + level) * (lon_count // 2) + lon
    return jnp.where(source == column, 1.0, 0.0).astype(jnp.bfloat16)


def spread_rows(values, lat_count, lon_count):
    matrix = spread_matrix(lat_count, lon_count)
    high = values.astype(jnp.bfloat16)
    rest = values - high.astype(jnp.float32)
    middle = rest.astype(jnp.bfloat16)
    low = (rest - middle.astype(jnp.float32)).astype(jnp.bfloat16)
    return dot_rows(matrix, high) + (dot_rows(matrix, middle) + dot_rows(matrix, low))


def up_kernel(
    core_ref, own_coarse_ref, part_ref, recv_ref, late_ref, swapped_ref,
    second_ref, skip_ref, out_ref, coarse_ref, lift_ref, level_ref, small_ref,
):
    core = core_ref[0]
    blocks, width = 8, 128
    for z in range(blocks):
        for place, origin in ((z, core), (blocks + z, 1 - core)):
            coarse_ref[origin * blocks + z] = own_coarse_ref[:, place * width : (place + 1) * width]
    level_three = []
    for place in range(2 * blocks):
        here = slice(place * width, place * width + width)
        level_three.append(
            (coarse_ref[place] + (part_ref[:, here] + recv_ref[:, here].astype(jnp.float32))).astype(
                jnp.bfloat16
            )
        )
    for weights_ref, origin in ((late_ref, core), (swapped_ref, 1 - core)):
        total = None
        for ring in range(2):
            for z in range(8):
                right = jnp.concatenate(
                    [weights_ref[y * 8 + z, :, ring * 640 : ring * 640 + 512] for y in range(8)],
                    axis=0,
                )
                product = dot_rows(level_three[ring * 8 + z], right)
                total = product if total is None else total + product
        lift_ref[origin] = total
    lat_count, lon_count = 6, 8
    for side in range(2):
        here = slice(side * 512, side * 512 + 512)
        level_ref[:, here] = (
            second_ref[:, here].astype(jnp.float32)
            + spread_rows(lift_ref[side], lat_count, lon_count)
        ).astype(jnp.bfloat16)
    for weights_ref, origin in ((late_ref, core), (swapped_ref, 1 - core)):
        total = None
        for ring in range(2):
            for z in range(0, 8, 2):
                right = jnp.concatenate(
                    [
                        jnp.concatenate(
                            [
                                weights_ref[
                                    (2 * row + part) * 8 + zz, :, ring * 640 + 512 : ring * 640 + 640
                                ]
                                for zz in (z, z + 1)
                                for row in range(4)
                            ],
                            axis=0,
                        )
                        for part in range(2)
                    ],
                    axis=1,
                )
                start = (ring * 8 + z) * 64
                product = dot_rows(level_ref[:, start : start + 128], right)
                total = product if total is None else total + product
        small_ref[origin] = total
    for side in range(2):
        here = slice(side * 256, side * 256 + 256)
        out_ref[:, here] = (
            skip_ref[:, here].astype(jnp.float32)
            + spread_rows(small_ref[side], 2 * lat_count, 2 * lon_count)
        ).astype(jnp.bfloat16)


Z_RING = 8
RINGS = [[ring * Z_RING + place for place in range(Z_RING)] for ring in range(2)]


def neighbours(first, last, axis):
    count = lax.axis_size(axis)
    before = lax.ppermute(last, axis, [(i, (i + 1) % count) for i in range(count)])
    behind = lax.ppermute(first, axis, [((i + 1) % count, i) for i in range(count)])
    return before, behind


def swap_cores(values):
    count = lax.axis_size("lon")
    return lax.ppermute(values, "lon", [(i, i ^ 1) for i in range(count)])


def swap_rings(values):
    count = lax.axis_size("lat")
    return lax.ppermute(values, "lat", [(i, (i + Z_RING) % count) for i in range(count)])


def swap_shards(values):
    lon_count = lax.axis_size("lon")
    pairs = []
    for lat in range(lax.axis_size("lat")):
        for lon in range(lon_count):
            ring, place = divmod(lat, Z_RING)
            target = (lat, lon)
            if ring != lon % 2:
                target = ((1 - ring) * Z_RING + place, lon ^ 1)
            pairs.append((lat * lon_count + lon, target[0] * lon_count + target[1]))
    return lax.ppermute(values, ("lat", "lon"), pairs)


def ring_scatter(blocks):
    return lax.all_to_all(blocks, "lat", 0, 0, axis_index_groups=RINGS, tiled=True)


def ring_shift(values, step, flip=0):
    lon_count = lax.axis_size("lon")
    pairs = []
    for lat in range(lax.axis_size("lat")):
        target = lat // Z_RING * Z_RING + (lat + step) % Z_RING
        for lon in range(lon_count):
            pairs.append((lat * lon_count + lon, target * lon_count + (lon ^ flip)))
    return lax.ppermute(values, ("lat", "lon"), pairs)


def ring_gather(values):
    return ring_scatter(jnp.broadcast_to(values[None], (Z_RING,) + values.shape))


def in_order(flag, own, other, axis):
    return jnp.where(
        flag == 0,
        jnp.concatenate([own, other], axis=axis),
        jnp.concatenate([other, own], axis=axis),
    )


def cut(values, row, rows, column, columns):
    return lax.dynamic_slice(values, (row, column), (rows, columns))


def after(values, *before):
    return lax.optimization_barrier((values,) + before)[0]


def on_device(
    fields,
    land_ids,
    surface_table,
    level_table,
    norm_first,
    qkv_first,
    out_first,
    norm_merge2,
    merge_second,
    norm_merge3,
    merge_third,
    norm_third,
    qkv_third,
    out_third,
    up_third,
    up_second,
):
    tile_rows, levels, tile_cols, feat_dim = fields.shape
    lat_count = lax.axis_size("lat")
    ring = lax.axis_index("lat") // Z_RING
    core = lax.axis_index("lon") % 2
    column = lax.axis_index("lon") // 4

    own_merge = jnp.concatenate(
        [lax.dynamic_slice_in_dim(merge_second, core * 512, 512, 1), out_first], axis=0
    )[None]
    both_merge = in_order(ring, own_merge, swap_rings(own_merge), 0)
    merge_weights = lax.all_gather(
        both_merge, "lat", axis=1, axis_index_groups=RINGS, tiled=True
    )
    core_place = jnp.stack([core, lax.axis_index("lat") % Z_RING]).astype(jnp.int32)
    picks = (land_ids[:, :, None] == jnp.arange(3, dtype=jnp.int32)).astype(jnp.float32)
    surface = jnp.einsum("ijs,sc->ijc", picks, surface_table.astype(jnp.float32))
    hidden = (
        fields.astype(jnp.float32)
        + surface[:, None, :, :]
        + level_table.astype(jnp.float32)[None, :, None, :]
    ).astype(jnp.bfloat16)
    hidden = after(hidden, both_merge)
    above, below = neighbours(hidden[:2], hidden[-2:], "lat")
    cells = jnp.concatenate([above, hidden, below], axis=0)
    qkv_third = qkv_third.transpose(0, 2, 1).reshape(-1, qkv_third.shape[1])

    out_third, merge_third, qkv_third, up_third, up_second, cells = lax.optimization_barrier(
        (out_third, merge_third, qkv_third, up_third, up_second, cells)
    )
    left, right = neighbours(cells[:, :, :2], cells[:, :, -2:], "lon")
    own_rest = jnp.concatenate(
        [
            cut(up_third, column * 16, 16, core * 512, 512),
            cut(up_second, column // 2 * 16, 16, core * 256 + column % 2 * 128, 128),
        ],
        axis=1,
    )[None]
    both_rest = in_order(ring, own_rest, swap_rings(own_rest), 0)
    out_third = swap_shards(out_third)
    merge_third = swap_shards(merge_third)
    qkv_third = swap_shards(qkv_third)
    late = jnp.concatenate(
        [
            both_rest[0],
            both_rest[1],
            cut(out_third, column // 2 * 16, 16, column % 2 * 1024, 1024),
        ],
        axis=1,
    )

    ext_rows = tile_rows + 4
    own_window = (jnp.arange(32 * 4) % tile_cols + 2) // 4
    key_window = jnp.concatenate(
        [own_window, jnp.zeros((16,), jnp.int32), jnp.full((16,), tile_cols // 4, jnp.int32)]
    )
    same_window = (key_window[:, None] == own_window[None, :]).astype(jnp.float32)
    lat_place = lax.axis_index("lat") * tile_rows + jnp.arange(ext_rows) - 2
    valid_rows = ((lat_place >= 0) & (lat_place < tile_rows * lat_count)).astype(jnp.float32)
    valid_rows = valid_rows.reshape(ext_rows // 4, 4, 1)
    valid_keys = jnp.concatenate(
        [jnp.repeat(valid_rows, 2 * count, axis=1) for count in (tile_cols, 2, 2)], axis=1
    )
    attended = call_kernel(
        first_kernel,
        jax.ShapeDtypeStruct((tile_rows * levels * tile_cols, feat_dim), jnp.bfloat16),
        (
            cells.reshape(-1, feat_dim),
            left.reshape(-1, feat_dim),
            right.reshape(-1, feat_dim),
            norm_first[None],
            qkv_first,
            same_window,
            valid_keys,
        ),
        flops=2 * 640 * 512 * 1536,
    )
    late = after(late, attended)
    late_rows = ring_gather(late)
    attended = after(attended, late, merge_third, qkv_third)
    tokens = attended.shape[0]
    skip_first, merged_in = call_kernel(
        skip_kernel,
        (
            jax.ShapeDtypeStruct((tokens, feat_dim), jnp.bfloat16),
            jax.ShapeDtypeStruct((tokens // 4, 4 * feat_dim), jnp.bfloat16),
        ),
        (attended, hidden.reshape(-1, feat_dim), merge_weights, norm_merge2[None]),
        flops=2 * 384 * 512 * 512,
    )
    own_rows = merged_in.shape[0]
    half_shape = jax.ShapeDtypeStruct((own_rows, 512), jnp.bfloat16)
    second_half, second_send = call_kernel(
        merge_kernel,
        (half_shape, half_shape),
        (merged_in, swap_cores(merged_in), merge_weights),
        flops=2 * 192 * 2048 * 512,
    )
    second_cells, coarse_in = call_kernel(
        join_kernel,
        (
            jax.ShapeDtypeStruct((own_rows, 1024), jnp.bfloat16),
            jax.ShapeDtypeStruct((own_rows // 4, 4096), jnp.bfloat16),
        ),
        (core_place, second_half, swap_cores(second_send), norm_merge3[None]),
        (pltpu.VMEM((2, own_rows, 512), jnp.bfloat16),),
        flops=2 * 96 * 96 * 1024,
    )
    late_rows = after(late_rows, coarse_in)
    late = lax.all_gather(
        late_rows,
        "lon",
        axis=0,
        axis_index_groups=[[4 * y + x for y in range(8)] for x in range(4)],
        tiled=True,
    )

    own_count = coarse_in.shape[0]
    line = Z_RING * own_count

    pieces, forth, back = [coarse_in], coarse_in, coarse_in
    for _ in range(3):
        forth, back = ring_shift(forth, 1), ring_shift(back, -1)
        pieces += [forth, back]
    near = jnp.stack(pieces)
    far, far_other = ring_shift(forth, 1), ring_shift(back, -1, 1)
    column_block = call_kernel(
        columns_kernel,
        jax.ShapeDtypeStruct((2, Z_RING, own_count, 128), jnp.bfloat16),
        (core_place, near, far, swap_cores(near), far_other, merge_third),
        flops=2 * 384 * 4096 * 128,
    ).reshape(2, line, 128)
    own_columns = ring_gather(column_block)
    other_columns = swap_cores(own_columns)
    blocks, _, _, width = own_columns.shape
    head_feats = HD
    heads_out, own_coarse = call_kernel(
        third_kernel,
        (
            jax.ShapeDtypeStruct((Z_RING, 2, own_count, head_feats), jnp.bfloat16),
            jax.ShapeDtypeStruct((own_count, 2 * blocks * width), jnp.float32),
        ),
        (
            core_place,
            own_columns,
            other_columns,
            norm_third.reshape(2 * blocks, 1, width),
            qkv_third,
        ),
        (
            pltpu.VMEM((2 * line, 2 * blocks * width), jnp.bfloat16),
            pltpu.VMEM((line, 2 * blocks * width), jnp.float32),
        ),
        flops=2 * 384 * 2048 * 192,
    )

    chip_heads = ring_scatter(heads_out)
    own_part, send_part = call_kernel(
        heads_kernel,
        (
            jax.ShapeDtypeStruct((own_count, 2048), jnp.float32),
            jax.ShapeDtypeStruct((own_count, 2048), jnp.bfloat16),
        ),
        (chip_heads, late),
        flops=2 * 48 * 512 * 2048,
    )
    late_swapped = swap_cores(after(late, heads_out))
    decoded = call_kernel(
        up_kernel,
        jax.ShapeDtypeStruct((tile_rows * levels * tile_cols, feat_dim), jnp.bfloat16),
        (
            core_place,
            own_coarse,
            own_part,
            swap_cores(send_part),
            late,
            late_swapped,
            second_cells,
            skip_first,
        ),
        (
            pltpu.VMEM((2 * blocks, own_count, width), jnp.float32),
            pltpu.VMEM((2, own_count, 512), jnp.float32),
            pltpu.VMEM((second_cells.shape[0], 1024), jnp.bfloat16),
            pltpu.VMEM((2, second_cells.shape[0], 256), jnp.float32),
        ),
        flops=2 * (24 * 2048 * 1024 + 96 * 1024 * 512),
    )
    return decoded.reshape(fields.shape)


def solution(mesh):
    in_specs = (
        P("lat", None, "lon", None),
        P("lat", "lon"),
        P(),
        P(),
        P(),
        P(),
        P("lat", None),
        P(),
        P("lat", None),
        P(),
        P(None, "lat"),
        P(),
        P(None, None, "lat"),
        P("lat", None),
        P("lat", None),
        P("lat", None),
    )
    out_specs = P("lat", None, "lon", None)
    return jax.shard_map(
        on_device, mesh=mesh, in_specs=in_specs, out_specs=out_specs, check_vma=False
    )
```

```python
import jax
import jax.numpy as jnp
from jax import lax
from jax.experimental import pallas as pl
from jax.experimental.pallas import tpu as pltpu
from jax.sharding import PartitionSpec as P

HD = 64


def norm_rows(values, gain):
    row_mean = jnp.mean(values, axis=-1, keepdims=True)
    centred = values - row_mean
    spread = jnp.mean(centred * centred, axis=-1, keepdims=True)
    return centred * lax.rsqrt(spread + 1e-05) * gain


def call_kernel(body, out_shape, operands, scratch=(), flops=0):
    smem = [operand.dtype == jnp.int32 for operand in operands]
    return pl.pallas_call(
        body,
        out_shape=out_shape,
        in_specs=[
            pl.BlockSpec(memory_space=pltpu.SMEM if scalar else pltpu.VMEM) for scalar in smem
        ],
        out_specs=jax.tree.map(lambda _: pl.BlockSpec(memory_space=pltpu.VMEM), out_shape),
        scratch_shapes=list(scratch),
        compiler_params=pltpu.CompilerParams(vmem_limit_bytes=48 * 1024 * 1024),
        cost_estimate=pl.CostEstimate(
            flops=flops,
            bytes_accessed=sum(operand.size * operand.dtype.itemsize for operand in operands),
            transcendentals=0,
        ),
    )(*operands)


def dot_rows(left, right):
    return lax.dot_general(left, right, (((1,), (0,)), ((), ())), preferred_element_type=jnp.float32)


def mix_tokens(query, key, value, keep):
    scores = lax.dot_general(
        key, query, (((1,), (1,)), ((), ())), preferred_element_type=jnp.float32
    )
    scores = jnp.where(keep, scores, -1e30)
    weights = jnp.exp(scores - jnp.max(scores, axis=0, keepdims=True))
    weights = (weights / jnp.sum(weights, axis=0, keepdims=True)).astype(jnp.bfloat16)
    return lax.dot_general(
        weights, value, (((0,), (0,)), ((), ())), preferred_element_type=jnp.float32
    )


def first_kernel(x_ref, left_ref, right_ref, gain_ref, qkv_ref, window_ref, lat_ref, out_ref):
    steps = lat_ref.shape[0]
    own, side = x_ref.shape[0] // steps, left_ref.shape[0] // steps
    lane = lax.broadcasted_iota(jnp.int32, (own, 128), 1)
    key_lane = lax.broadcasted_iota(jnp.int32, (own + 2 * side, 128), 1)
    gain = gain_ref[...]
    for step in range(steps):
        rows = jnp.concatenate(
            [
                x_ref[step * own : (step + 1) * own, :],
                left_ref[step * side : (step + 1) * side, :],
                right_ref[step * side : (step + 1) * side, :],
            ],
            axis=0,
        )
        normed = norm_rows(rows.astype(jnp.float32), gain).astype(jnp.bfloat16)
        query = dot_rows(normed[:own], qkv_ref[0]).astype(jnp.bfloat16)
        query = (query * 0.125).astype(jnp.bfloat16)
        key = dot_rows(normed, qkv_ref[1]).astype(jnp.bfloat16)
        value = dot_rows(normed, qkv_ref[2]).astype(jnp.bfloat16)
        keep = window_ref[...] * lat_ref[step] > 0.0
        first = own // 2 if step == 0 else 0
        last = own // 2 if step == steps - 1 else own
        start = step * own - own // 2 + first
        for pair in range(query.shape[1] // 128):
            here = slice(pair * 128, pair * 128 + 128)
            parts = []
            for odd in range(2):
                picked = (key_lane < HD) if odd == 0 else (key_lane >= HD)
                key_side = jnp.where(picked, key[:, here], jnp.zeros_like(key[:, here]))
                parts.append(mix_tokens(query[:, here], key_side, value[:, here], keep))
            mixed = jnp.where(lane < HD, parts[0], parts[1]).astype(jnp.bfloat16)
            out_ref[start : start + last - first, here] = mixed[first:last]


def pick_matrix(lat_count, lon_count, lat_side, lon_side):
    shape = (2 * lat_count * lon_count, 8 * lat_count * lon_count)
    row = lax.broadcasted_iota(jnp.int32, shape, 0)
    column = lax.broadcasted_iota(jnp.int32, shape, 1)
    bits = lon_count.bit_length() - 1
    lon = row & (lon_count - 1)
    level = jnp.right_shift(row, bits) & 1
    lat = jnp.right_shift(row, bits + 1)
    source = ((2 * lat + lat_side) * 2 + level) * (2 * lon_count) + 2 * lon + lon_side
    return jnp.where(source == column, 1.0, 0.0).astype(jnp.bfloat16)


def join_quads(cells, lat_count, lon_count, gain_ref, out_ref):
    width = cells.shape[1]
    parts = [
        dot_rows(pick_matrix(lat_count, lon_count, lat_side, lon_side), cells)
        for lat_side in range(2)
        for lon_side in range(2)
    ]
    count = 1.0 / (4 * width)
    row_mean = sum(jnp.sum(part, axis=-1, keepdims=True) for part in parts) * count
    parts = [part - row_mean for part in parts]
    spread = sum(jnp.sum(part * part, axis=-1, keepdims=True) for part in parts) * count
    scale = lax.rsqrt(spread + 1e-05)
    for place, part in enumerate(parts):
        here = slice(place * width, place * width + width)
        out_ref[:, here] = (part * scale * gain_ref[:, here]).astype(jnp.bfloat16)


def skip_kernel(attended_ref, hidden_ref, weights_ref, gain_ref, skip_ref, merged_ref):
    total = None
    for ring in range(2):
        for z in range(0, 8, 4):
            right = jnp.concatenate(
                [weights_ref[ring, zz * 160 + 128 : zz * 160 + 160, :] for zz in range(z, z + 4)],
                axis=0,
            )
            start = (ring * 8 + z) * 32
            product = dot_rows(attended_ref[:, start : start + 128], right)
            total = product if total is None else total + product
    skip = (hidden_ref[...].astype(jnp.float32) + total).astype(jnp.bfloat16)
    skip_ref[...] = skip
    join_quads(skip, 6, 8, gain_ref, merged_ref)


def merge_kernel(own_ref, other_ref, weights_ref, own_out_ref, send_ref):
    left = jnp.concatenate([own_ref[...], other_ref[...]], axis=0)
    total = None
    for ring in range(2):
        for z in range(0, 8, 2):
            right = jnp.concatenate(
                [weights_ref[ring, zz * 160 : zz * 160 + 128, :] for zz in (z, z + 1)], axis=0
            )
            start = (ring * 8 + z) * 128
            product = dot_rows(left[:, start : start + 256], right)
            total = product if total is None else total + product
    rows = own_ref.shape[0]
    own_out_ref[...] = total[:rows].astype(jnp.bfloat16)
    send_ref[...] = total[rows:].astype(jnp.bfloat16)


def join_kernel(core_ref, own_ref, recv_ref, gain_ref, second_ref, coarse_ref, halves_ref):
    core = core_ref[0]
    halves_ref[core] = own_ref[...]
    halves_ref[1 - core] = recv_ref[...]
    second = jnp.concatenate([halves_ref[0], halves_ref[1]], axis=1)
    second_ref[...] = second
    join_quads(second, 3, 4, gain_ref, coarse_ref)


RING_ORDER = (0, -1, 1, -2, 2, -3, 3)


def columns_kernel(place_ref, *refs):
    near, (far_low, far_high), (own_ref, other_ref, out_ref) = refs[:7], refs[7:9], refs[9:]
    rows, half = far_low.shape
    left = jnp.concatenate([ref[...].astype(jnp.float32) for ref in near], axis=0)
    left = left.astype(jnp.bfloat16)
    ring = place_ref[2]
    for weights, shard in ((own_ref, ring), (other_ref, 1 - ring)):
        product = dot_rows(left, weights[...])
        for at, offset in enumerate(RING_ORDER):
            place = jnp.bitwise_and(place_ref[1] + (offset + 8), 7)
            out_ref[place, shard] = product[at * rows : (at + 1) * rows].astype(jnp.bfloat16)
        far = dot_rows(far_low[...], weights[:half, :]) + dot_rows(far_high[...], weights[half:, :])
        out_ref[jnp.bitwise_and(place_ref[1] + 4, 7), shard] = far.astype(jnp.bfloat16)


def third_kernel(place_ref, x_ref, gain_ref, own_ref, other_ref, out_ref, coarse_ref, normed_ref):
    blocks, places, shards, rows, width = x_ref.shape
    count = 1.0 / (blocks * shards * width)
    order = [(z, shard) for shard in range(shards) for z in range(blocks)]
    for first in range(0, places, 2):
        tiles = [
            jnp.concatenate(
                [x_ref[z, first + at, shard].astype(jnp.float32) for at in range(2)], axis=0
            )
            for z, shard in order
        ]
        row_mean = jnp.sum(sum(tiles), axis=-1, keepdims=True) * count
        tiles = [tile - row_mean for tile in tiles]
        spread = jnp.sum(sum(tile * tile for tile in tiles), axis=-1, keepdims=True)
        scale = lax.rsqrt(spread * count + 1e-05)
        for at, tile in enumerate(tiles):
            here = slice(at * width, (at + 1) * width)
            normed_ref[first * rows : (first + 2) * rows, here] = (
                tile * scale * gain_ref[:, here]
            ).astype(jnp.bfloat16)
    for at, (z, shard) in enumerate(order):
        coarse_ref[:, at * width : (at + 1) * width] = x_ref[z, place_ref[1], shard].astype(
            jnp.float32
        )
    token = lax.broadcasted_iota(jnp.int32, (96, 96), 0)
    other = lax.broadcasted_iota(jnp.int32, (96, 96), 1)
    keep = jnp.right_shift(token, 5) == jnp.right_shift(other, 5)
    ring = place_ref[2]
    for weights, shard in ((own_ref, ring), (other_ref, 1 - ring)):
        triple = lax.dot_general(
            normed_ref[...],
            weights[...],
            (((1,), (1,)), ((), ())),
            preferred_element_type=jnp.float32,
        ).astype(jnp.bfloat16)
        query = (triple[:, :HD] * 0.125).astype(jnp.bfloat16)
        key = triple[:, HD : 2 * HD]
        value = triple[:, 2 * HD :]
        for group in range(places * rows // 96):
            mine = slice(group * 96, group * 96 + 96)
            mixed = mix_tokens(query[mine], key[mine], value[mine], keep)
            for at in range(96 // rows):
                out_ref[group * (96 // rows) + at, shard] = mixed[
                    at * rows : (at + 1) * rows
                ].astype(jnp.bfloat16)


def spread_matrix(lat_count, lon_count):
    fine = (2 * lat_count * lon_count, lat_count * lon_count // 2)
    row = lax.broadcasted_iota(jnp.int32, fine, 0)
    column = lax.broadcasted_iota(jnp.int32, fine, 1)
    bits = lon_count.bit_length() - 1
    lat = jnp.right_shift(row, bits + 2)
    level = jnp.right_shift(row, bits) & 1
    lon = jnp.right_shift(row & (lon_count - 1), 1)
    source = (lat * 2 + level) * (lon_count // 2) + lon
    return jnp.where(source == column, 1.0, 0.0).astype(jnp.bfloat16)


def spread_rows(values, lat_count, lon_count):
    matrix = spread_matrix(lat_count, lon_count)
    high = values.astype(jnp.bfloat16)
    rest = values - high.astype(jnp.float32)
    middle = rest.astype(jnp.bfloat16)
    low = (rest - middle.astype(jnp.float32)).astype(jnp.bfloat16)
    return dot_rows(matrix, high) + (dot_rows(matrix, middle) + dot_rows(matrix, low))


def up_kernel(
    core_ref, heads_ref, own_coarse_ref, late_ref, swapped_ref, second_ref, skip_ref, out_ref,
    third_ref, lift_ref, level_ref, small_ref,
):
    core = core_ref[0]
    pairs = []
    for ring in range(2):
        for z in range(0, 8, 2):
            pairs.append(
                jnp.concatenate(
                    [heads_ref[z, ring].astype(jnp.float32), heads_ref[z + 1, ring].astype(jnp.float32)],
                    axis=1,
                ).astype(jnp.bfloat16)
            )
    for weights_ref, origin in ((late_ref, core), (swapped_ref, 1 - core)):
        for part in range(2):
            total = None
            for ring in range(2):
                for z in range(0, 8, 2):
                    right = jnp.concatenate(
                        [
                            weights_ref[
                                (2 * row + part) * 8 + zz, :, ring * 1152 + 640 : ring * 1152 + 1152
                            ]
                            for zz in (z, z + 1)
                            for row in range(4)
                        ],
                        axis=0,
                    )
                    product = dot_rows(pairs[ring * 4 + z // 2], right)
                    total = product if total is None else total + product
            third_ref[part, origin] = total
    level_three = []
    for place in range(16):
        here = slice(place * 128, place * 128 + 128)
        quarter = place // 4
        update = third_ref[quarter // 2, quarter % 2][:, place % 4 * 128 : place % 4 * 128 + 128]
        level_three.append((own_coarse_ref[:, here] + update).astype(jnp.bfloat16))
    for weights_ref, origin in ((late_ref, core), (swapped_ref, 1 - core)):
        total = None
        for ring in range(2):
            for z in range(8):
                right = jnp.concatenate(
                    [weights_ref[y * 8 + z, :, ring * 1152 : ring * 1152 + 512] for y in range(8)],
                    axis=0,
                )
                product = dot_rows(level_three[ring * 8 + z], right)
                total = product if total is None else total + product
        lift_ref[origin] = total
    lat_count, lon_count = 6, 8
    for side in range(2):
        here = slice(side * 512, side * 512 + 512)
        level_ref[:, here] = (
            second_ref[:, here].astype(jnp.float32)
            + spread_rows(lift_ref[side], lat_count, lon_count)
        ).astype(jnp.bfloat16)
    for weights_ref, origin in ((late_ref, core), (swapped_ref, 1 - core)):
        total = None
        for ring in range(2):
            for z in range(0, 8, 2):
                right = jnp.concatenate(
                    [
                        jnp.concatenate(
                            [
                                weights_ref[
                                    (2 * row + part) * 8 + zz, :, ring * 1152 + 512 : ring * 1152 + 640
                                ]
                                for zz in (z, z + 1)
                                for row in range(4)
                            ],
                            axis=0,
                        )
                        for part in range(2)
                    ],
                    axis=1,
                )
                start = (ring * 8 + z) * 64
                product = dot_rows(level_ref[:, start : start + 128], right)
                total = product if total is None else total + product
        small_ref[origin] = total
    for side in range(2):
        here = slice(side * 256, side * 256 + 256)
        out_ref[:, here] = (
            skip_ref[:, here].astype(jnp.float32)
            + spread_rows(small_ref[side], 2 * lat_count, 2 * lon_count)
        ).astype(jnp.bfloat16)


Z_RING = 8
RINGS = [[ring * Z_RING + place for place in range(Z_RING)] for ring in range(2)]


def neighbours(first, last, axis):
    count = lax.axis_size(axis)
    before = lax.ppermute(last, axis, [(i, (i + 1) % count) for i in range(count)])
    behind = lax.ppermute(first, axis, [((i + 1) % count, i) for i in range(count)])
    return before, behind


def swap_cores(values):
    count = lax.axis_size("lon")
    return lax.ppermute(values, "lon", [(i, i ^ 1) for i in range(count)])


def swap_rings(values):
    count = lax.axis_size("lat")
    return lax.ppermute(values, "lat", [(i, (i + Z_RING) % count) for i in range(count)])


def ring_scatter(blocks):
    return lax.all_to_all(blocks, "lat", 0, 0, axis_index_groups=RINGS, tiled=True)


def ring_shift(values, step):
    pairs = [(at, at // Z_RING * Z_RING + (at + step) % Z_RING) for at in range(2 * Z_RING)]
    return lax.ppermute(values, "lat", pairs)


def ring_gather(values):
    return ring_scatter(jnp.broadcast_to(values[None], (Z_RING,) + values.shape))


def in_order(flag, own, other, axis):
    return jnp.where(
        flag == 0,
        jnp.concatenate([own, other], axis=axis),
        jnp.concatenate([other, own], axis=axis),
    )


def cut(values, row, rows, column, columns):
    return lax.dynamic_slice(values, (row, column), (rows, columns))


def after(values, *before):
    return lax.optimization_barrier((values,) + before)[0]


def on_device(
    fields,
    land_ids,
    surface_table,
    level_table,
    norm_first,
    qkv_first,
    out_first,
    norm_merge2,
    merge_second,
    norm_merge3,
    merge_third,
    norm_third,
    qkv_third,
    out_third,
    up_third,
    up_second,
):
    tile_rows, levels, tile_cols, feat_dim = fields.shape
    lat_count = lax.axis_size("lat")
    ring = lax.axis_index("lat") // Z_RING
    core = lax.axis_index("lon") % 2
    column = lax.axis_index("lon") // 4

    own_merge = jnp.concatenate(
        [lax.dynamic_slice_in_dim(merge_second, core * 512, 512, 1), out_first], axis=0
    )[None]
    both_merge = in_order(ring, own_merge, swap_rings(own_merge), 0)
    merge_weights = lax.all_gather(
        both_merge, "lat", axis=1, axis_index_groups=RINGS, tiled=True
    )
    core_place = jnp.stack([core, lax.axis_index("lat") % Z_RING, ring]).astype(jnp.int32)
    own_rest = jnp.concatenate(
        [
            cut(up_third, column * 16, 16, core * 512, 512),
            cut(up_second, column // 2 * 16, 16, core * 256 + column % 2 * 128, 128),
            cut(out_third, column // 2 * 16, 16, column % 2 * 1024 + core * 512, 512),
        ],
        axis=1,
    )
    other_rest = swap_rings(own_rest)
    late = in_order(ring, own_rest, other_rest, 1)

    picks = (land_ids[:, :, None] == jnp.arange(3, dtype=jnp.int32)).astype(jnp.float32)
    surface = jnp.einsum("ijs,sc->ijc", picks, surface_table.astype(jnp.float32))
    hidden = (
        fields.astype(jnp.float32)
        + surface[:, None, :, :]
        + level_table.astype(jnp.float32)[None, :, None, :]
    ).astype(jnp.bfloat16)
    hidden = after(hidden, both_merge, other_rest)
    above, below = neighbours(hidden[:2], hidden[-2:], "lat")
    cells = jnp.concatenate([above, hidden, below], axis=0)
    qkv_third = qkv_third.transpose(0, 2, 1).reshape(-1, qkv_third.shape[1])

    merge_third, qkv_third, cells = lax.optimization_barrier((merge_third, qkv_third, cells))
    left, right = neighbours(cells[:, :, :2], cells[:, :, -2:], "lon")
    merge_other = swap_rings(merge_third)
    qkv_other = swap_rings(qkv_third)
    late, left = lax.optimization_barrier((late, left))
    late_rows = ring_gather(late)

    ext_rows = tile_rows + 4
    own_window = (jnp.arange(32 * 4) % tile_cols + 2) // 4
    key_window = jnp.concatenate(
        [own_window, jnp.zeros((16,), jnp.int32), jnp.full((16,), tile_cols // 4, jnp.int32)]
    )
    same_window = (key_window[:, None] == own_window[None, :]).astype(jnp.float32)
    lat_place = lax.axis_index("lat") * tile_rows + jnp.arange(ext_rows) - 2
    valid_rows = ((lat_place >= 0) & (lat_place < tile_rows * lat_count)).astype(jnp.float32)
    valid_rows = valid_rows.reshape(ext_rows // 4, 4, 1)
    valid_keys = jnp.concatenate(
        [jnp.repeat(valid_rows, 2 * count, axis=1) for count in (tile_cols, 2, 2)], axis=1
    )
    attended = call_kernel(
        first_kernel,
        jax.ShapeDtypeStruct((tile_rows * levels * tile_cols, feat_dim), jnp.bfloat16),
        (
            cells.reshape(-1, feat_dim),
            left.reshape(-1, feat_dim),
            right.reshape(-1, feat_dim),
            norm_first[None],
            qkv_first,
            same_window,
            valid_keys,
        ),
        flops=2 * 640 * 512 * 1536,
    )
    attended = after(attended, merge_other, late_rows)
    tokens = attended.shape[0]
    skip_first, merged_in = call_kernel(
        skip_kernel,
        (
            jax.ShapeDtypeStruct((tokens, feat_dim), jnp.bfloat16),
            jax.ShapeDtypeStruct((tokens // 4, 4 * feat_dim), jnp.bfloat16),
        ),
        (attended, hidden.reshape(-1, feat_dim), merge_weights, norm_merge2[None]),
        flops=2 * 384 * 512 * 512,
    )
    own_rows = merged_in.shape[0]
    half_shape = jax.ShapeDtypeStruct((own_rows, 512), jnp.bfloat16)
    second_half, second_send = call_kernel(
        merge_kernel,
        (half_shape, half_shape),
        (merged_in, after(swap_cores(merged_in), qkv_other), merge_weights),
        flops=2 * 192 * 2048 * 512,
    )
    second_cells, coarse_in = call_kernel(
        join_kernel,
        (
            jax.ShapeDtypeStruct((own_rows, 1024), jnp.bfloat16),
            jax.ShapeDtypeStruct((own_rows // 4, 4096), jnp.bfloat16),
        ),
        (core_place, second_half, swap_cores(second_send), norm_merge3[None]),
        (pltpu.VMEM((2, own_rows, 512), jnp.bfloat16),),
        flops=2 * 96 * 96 * 1024,
    )
    late = lax.all_gather(
        after(late_rows, coarse_in),
        "lon",
        axis=0,
        axis_index_groups=[[4 * y + x for y in range(8)] for x in range(4)],
        tiled=True,
    ).reshape(64, 16, -1)

    own_count = coarse_in.shape[0]

    pieces, forth, back = [coarse_in], coarse_in, coarse_in
    for _ in range(3):
        forth, back = ring_shift(forth, 1), ring_shift(back, -1)
        pieces += [forth, back]
    half_feats = coarse_in.shape[1] // 2
    pieces += [ring_shift(forth[:, :half_feats], 1), ring_shift(back[:, half_feats:], -1)]
    column_block = call_kernel(
        columns_kernel,
        jax.ShapeDtypeStruct((Z_RING, 2, own_count, 128), jnp.bfloat16),
        (core_place, *pieces, merge_third, merge_other),
        flops=2 * 192 * 4096 * 256,
    )
    heads_out, own_coarse = call_kernel(
        third_kernel,
        (
            jax.ShapeDtypeStruct((Z_RING, 2, own_count, HD), jnp.bfloat16),
            jax.ShapeDtypeStruct((own_count, 2048), jnp.float32),
        ),
        (core_place, ring_gather(column_block), norm_third[None], qkv_third, qkv_other),
        (pltpu.VMEM((Z_RING * own_count, 2048), jnp.bfloat16),),
        flops=2 * 192 * 2048 * 384,
    )

    late_swapped = swap_cores(after(late, heads_out))
    decoded = call_kernel(
        up_kernel,
        jax.ShapeDtypeStruct((tile_rows * levels * tile_cols, feat_dim), jnp.bfloat16),
        (
            core_place,
            ring_scatter(heads_out),
            own_coarse,
            late,
            late_swapped,
            second_cells,
            skip_first,
        ),
        (
            pltpu.VMEM((2, 2, own_count, 512), jnp.float32),
            pltpu.VMEM((2, own_count, 512), jnp.float32),
            pltpu.VMEM((second_cells.shape[0], 1024), jnp.bfloat16),
            pltpu.VMEM((2, second_cells.shape[0], 256), jnp.float32),
        ),
        flops=2 * (24 * 1024 * 2048 + 24 * 2048 * 1024 + 96 * 1024 * 512),
    )
    return decoded.reshape(fields.shape)


def solution(mesh):
    in_specs = (
        P("lat", None, "lon", None),
        P("lat", "lon"),
        P(),
        P(),
        P(),
        P(),
        P("lat", None),
        P(),
        P("lat", None),
        P(),
        P(None, "lat"),
        P(),
        P(None, None, "lat"),
        P("lat", None),
        P("lat", None),
        P("lat", None),
    )
    out_specs = P("lat", None, "lon", None)
    return jax.shard_map(
        on_device, mesh=mesh, in_specs=in_specs, out_specs=out_specs, check_vma=False
    )
```

```python
import jax
import jax.numpy as jnp
from jax import lax
from jax.experimental import pallas as pl
from jax.experimental.pallas import tpu as pltpu
from jax.sharding import PartitionSpec as P

HD = 64


def norm_rows(values, gain):
    row_mean = jnp.mean(values, axis=-1, keepdims=True)
    centred = values - row_mean
    spread = jnp.mean(centred * centred, axis=-1, keepdims=True)
    return centred * lax.rsqrt(spread + 1e-05) * gain


def call_kernel(body, out_shape, operands, scratch=(), flops=0):
    smem = [operand.dtype == jnp.int32 for operand in operands]
    return pl.pallas_call(
        body,
        out_shape=out_shape,
        in_specs=[
            pl.BlockSpec(memory_space=pltpu.SMEM if scalar else pltpu.VMEM) for scalar in smem
        ],
        out_specs=jax.tree.map(lambda _: pl.BlockSpec(memory_space=pltpu.VMEM), out_shape),
        scratch_shapes=list(scratch),
        compiler_params=pltpu.CompilerParams(vmem_limit_bytes=48 * 1024 * 1024),
        cost_estimate=pl.CostEstimate(
            flops=flops,
            bytes_accessed=sum(operand.size * operand.dtype.itemsize for operand in operands),
            transcendentals=0,
        ),
    )(*operands)


def dot_rows(left, right):
    return lax.dot_general(left, right, (((1,), (0,)), ((), ())), preferred_element_type=jnp.float32)


def mix_tokens(query, key, value, keep):
    scores = lax.dot_general(
        key, query, (((1,), (1,)), ((), ())), preferred_element_type=jnp.float32
    )
    scores = jnp.where(keep, scores, -1e30)
    weights = jnp.exp(scores - jnp.max(scores, axis=0, keepdims=True))
    weights = (weights / jnp.sum(weights, axis=0, keepdims=True)).astype(jnp.bfloat16)
    return lax.dot_general(
        weights, value, (((0,), (0,)), ((), ())), preferred_element_type=jnp.float32
    )


def first_kernel(x_ref, left_ref, right_ref, gain_ref, qkv_ref, window_ref, lat_ref, out_ref):
    steps = lat_ref.shape[0]
    own, side = x_ref.shape[0] // steps, left_ref.shape[0] // steps
    lane = lax.broadcasted_iota(jnp.int32, (own, 128), 1)
    key_lane = lax.broadcasted_iota(jnp.int32, (own + 2 * side, 128), 1)
    gain = gain_ref[...]
    for step in range(steps):
        rows = jnp.concatenate(
            [
                x_ref[step * own : (step + 1) * own, :],
                left_ref[step * side : (step + 1) * side, :],
                right_ref[step * side : (step + 1) * side, :],
            ],
            axis=0,
        )
        normed = norm_rows(rows.astype(jnp.float32), gain).astype(jnp.bfloat16)
        query = dot_rows(normed[:own], qkv_ref[0]).astype(jnp.bfloat16)
        query = (query * 0.125).astype(jnp.bfloat16)
        key = dot_rows(normed, qkv_ref[1]).astype(jnp.bfloat16)
        value = dot_rows(normed, qkv_ref[2]).astype(jnp.bfloat16)
        keep = window_ref[...] * lat_ref[step] > 0.0
        first = own // 2 if step == 0 else 0
        last = own // 2 if step == steps - 1 else own
        start = step * own - own // 2 + first
        for pair in range(query.shape[1] // 128):
            here = slice(pair * 128, pair * 128 + 128)
            parts = []
            for odd in range(2):
                picked = (key_lane < HD) if odd == 0 else (key_lane >= HD)
                key_side = jnp.where(picked, key[:, here], jnp.zeros_like(key[:, here]))
                parts.append(mix_tokens(query[:, here], key_side, value[:, here], keep))
            mixed = jnp.where(lane < HD, parts[0], parts[1]).astype(jnp.bfloat16)
            out_ref[start : start + last - first, here] = mixed[first:last]


def pick_matrix(lat_count, lon_count, lat_side, lon_side):
    shape = (2 * lat_count * lon_count, 8 * lat_count * lon_count)
    row = lax.broadcasted_iota(jnp.int32, shape, 0)
    column = lax.broadcasted_iota(jnp.int32, shape, 1)
    bits = lon_count.bit_length() - 1
    lon = row & (lon_count - 1)
    level = jnp.right_shift(row, bits) & 1
    lat = jnp.right_shift(row, bits + 1)
    source = ((2 * lat + lat_side) * 2 + level) * (2 * lon_count) + 2 * lon + lon_side
    return jnp.where(source == column, 1.0, 0.0).astype(jnp.bfloat16)


def join_quads(cells, lat_count, lon_count, gain_ref, out_ref):
    width = cells.shape[1]
    parts = [
        dot_rows(pick_matrix(lat_count, lon_count, lat_side, lon_side), cells)
        for lat_side in range(2)
        for lon_side in range(2)
    ]
    count = 1.0 / (4 * width)
    row_mean = sum(jnp.sum(part, axis=-1, keepdims=True) for part in parts) * count
    parts = [part - row_mean for part in parts]
    spread = sum(jnp.sum(part * part, axis=-1, keepdims=True) for part in parts) * count
    scale = lax.rsqrt(spread + 1e-05)
    for place, part in enumerate(parts):
        here = slice(place * width, place * width + width)
        out_ref[:, here] = (part * scale * gain_ref[:, here]).astype(jnp.bfloat16)


def skip_kernel(attended_ref, hidden_ref, weights_ref, gain_ref, skip_ref, merged_ref):
    total = None
    for ring in range(2):
        for z in range(0, 8, 4):
            right = jnp.concatenate(
                [weights_ref[ring, zz * 160 + 128 : zz * 160 + 160, :] for zz in range(z, z + 4)],
                axis=0,
            )
            start = (ring * 8 + z) * 32
            product = dot_rows(attended_ref[:, start : start + 128], right)
            total = product if total is None else total + product
    skip = (hidden_ref[...].astype(jnp.float32) + total).astype(jnp.bfloat16)
    skip_ref[...] = skip
    join_quads(skip, 6, 8, gain_ref, merged_ref)


def merge_kernel(own_ref, other_ref, weights_ref, own_out_ref, send_ref):
    left = jnp.concatenate([own_ref[...], other_ref[...]], axis=0)
    total = None
    for ring in range(2):
        for z in range(0, 8, 2):
            right = jnp.concatenate(
                [weights_ref[ring, zz * 160 : zz * 160 + 128, :] for zz in (z, z + 1)], axis=0
            )
            start = (ring * 8 + z) * 128
            product = dot_rows(left[:, start : start + 256], right)
            total = product if total is None else total + product
    rows = own_ref.shape[0]
    own_out_ref[...] = total[:rows].astype(jnp.bfloat16)
    send_ref[...] = total[rows:].astype(jnp.bfloat16)


def join_kernel(core_ref, own_ref, recv_ref, gain_ref, second_ref, coarse_ref, halves_ref):
    core = core_ref[0]
    halves_ref[core] = own_ref[...]
    halves_ref[1 - core] = recv_ref[...]
    second = jnp.concatenate([halves_ref[0], halves_ref[1]], axis=1)
    second_ref[...] = second
    join_quads(second, 3, 4, gain_ref, coarse_ref)


RING_ORDER = (0, -1, 1, -2, 2, -3, 3)


def halves_in_order(core, mine_ref, partner_ref):
    mine, partner = mine_ref[...], partner_ref[...]
    first = core == 0
    return jnp.concatenate(
        [jnp.where(first, mine, partner), jnp.where(first, partner, mine)], axis=0
    )


def columns_kernel(place_ref, *refs):
    near, (far_low, far_high), (own_ref, *halves, out_ref) = refs[:7], refs[7:9], refs[9:]
    rows, half = far_low.shape
    left = jnp.concatenate([ref[...].astype(jnp.float32) for ref in near], axis=0)
    left = left.astype(jnp.bfloat16)
    ring = place_ref[2]
    own = own_ref[...]
    for weights, shard in ((own, ring), (halves_in_order(place_ref[0], *halves), 1 - ring)):
        product = dot_rows(left, weights)
        for at, offset in enumerate(RING_ORDER):
            place = jnp.bitwise_and(place_ref[1] + (offset + 8), 7)
            out_ref[place, shard] = product[at * rows : (at + 1) * rows].astype(jnp.bfloat16)
        far = dot_rows(far_low[...], weights[:half]) + dot_rows(far_high[...], weights[half:])
        out_ref[jnp.bitwise_and(place_ref[1] + 4, 7), shard] = far.astype(jnp.bfloat16)


def third_kernel(
    place_ref, x_ref, gain_ref, own_ref, mine_ref, partner_ref, out_ref, coarse_ref, normed_ref
):
    blocks, places, shards, rows, width = x_ref.shape
    count = 1.0 / (blocks * shards * width)
    order = [(z, shard) for shard in range(shards) for z in range(blocks)]
    for first in range(0, places, 2):
        tiles = [
            jnp.concatenate(
                [x_ref[z, first + at, shard].astype(jnp.float32) for at in range(2)], axis=0
            )
            for z, shard in order
        ]
        row_mean = jnp.sum(sum(tiles), axis=-1, keepdims=True) * count
        tiles = [tile - row_mean for tile in tiles]
        spread = jnp.sum(sum(tile * tile for tile in tiles), axis=-1, keepdims=True)
        scale = lax.rsqrt(spread * count + 1e-05)
        for at, tile in enumerate(tiles):
            here = slice(at * width, (at + 1) * width)
            normed_ref[first * rows : (first + 2) * rows, here] = (
                tile * scale * gain_ref[:, here]
            ).astype(jnp.bfloat16)
    for at, (z, shard) in enumerate(order):
        coarse_ref[:, at * width : (at + 1) * width] = x_ref[z, place_ref[1], shard].astype(
            jnp.float32
        )
    query_token = lax.broadcasted_iota(jnp.int32, (96, 96), 0)
    key_token = lax.broadcasted_iota(jnp.int32, (96, 96), 1)
    keep = jnp.right_shift(query_token, 5) == jnp.right_shift(key_token, 5)
    ring = place_ref[2]
    other = halves_in_order(place_ref[0], mine_ref, partner_ref)
    for weights, shard in ((own_ref[...], ring), (other, 1 - ring)):
        triple = lax.dot_general(
            normed_ref[...],
            weights,
            (((1,), (1,)), ((), ())),
            preferred_element_type=jnp.float32,
        ).astype(jnp.bfloat16)
        query = (triple[:, :HD] * 0.125).astype(jnp.bfloat16)
        key = triple[:, HD : 2 * HD]
        value = triple[:, 2 * HD :]
        for group in range(places * rows // 96):
            mine = slice(group * 96, group * 96 + 96)
            mixed = mix_tokens(query[mine], key[mine], value[mine], keep)
            for at in range(96 // rows):
                out_ref[group * (96 // rows) + at, shard] = mixed[
                    at * rows : (at + 1) * rows
                ].astype(jnp.bfloat16)


def spread_matrix(lat_count, lon_count):
    fine = (2 * lat_count * lon_count, lat_count * lon_count // 2)
    row = lax.broadcasted_iota(jnp.int32, fine, 0)
    column = lax.broadcasted_iota(jnp.int32, fine, 1)
    bits = lon_count.bit_length() - 1
    lat = jnp.right_shift(row, bits + 2)
    level = jnp.right_shift(row, bits) & 1
    lon = jnp.right_shift(row & (lon_count - 1), 1)
    source = (lat * 2 + level) * (lon_count // 2) + lon
    return jnp.where(source == column, 1.0, 0.0).astype(jnp.bfloat16)


def spread_rows(values, lat_count, lon_count):
    matrix = spread_matrix(lat_count, lon_count)
    high = values.astype(jnp.bfloat16)
    rest = values - high.astype(jnp.float32)
    middle = rest.astype(jnp.bfloat16)
    low = (rest - middle.astype(jnp.float32)).astype(jnp.bfloat16)
    return dot_rows(matrix, high) + (dot_rows(matrix, middle) + dot_rows(matrix, low))


def up_kernel(
    core_ref, heads_ref, own_coarse_ref, late_ref, swapped_ref, second_ref, skip_ref, out_ref,
    third_ref, lift_ref, level_ref, small_ref,
):
    core = core_ref[0]
    pairs = []
    for ring in range(2):
        for z in range(0, 8, 2):
            pairs.append(
                jnp.concatenate(
                    [heads_ref[z, ring].astype(jnp.float32), heads_ref[z + 1, ring].astype(jnp.float32)],
                    axis=1,
                ).astype(jnp.bfloat16)
            )
    for weights_ref, origin in ((late_ref, core), (swapped_ref, 1 - core)):
        for part in range(2):
            total = None
            for ring in range(2):
                for z in range(0, 8, 2):
                    right = jnp.concatenate(
                        [
                            weights_ref[
                                (2 * row + part) * 8 + zz, :, ring * 1152 + 640 : ring * 1152 + 1152
                            ]
                            for zz in (z, z + 1)
                            for row in range(4)
                        ],
                        axis=0,
                    )
                    product = dot_rows(pairs[ring * 4 + z // 2], right)
                    total = product if total is None else total + product
            third_ref[part, origin] = total
    level_three = []
    for place in range(16):
        here = slice(place * 128, place * 128 + 128)
        quarter = place // 4
        update = third_ref[quarter // 2, quarter % 2][:, place % 4 * 128 : place % 4 * 128 + 128]
        level_three.append((own_coarse_ref[:, here] + update).astype(jnp.bfloat16))
    for weights_ref, origin in ((late_ref, core), (swapped_ref, 1 - core)):
        total = None
        for ring in range(2):
            for z in range(8):
                right = jnp.concatenate(
                    [weights_ref[y * 8 + z, :, ring * 1152 : ring * 1152 + 512] for y in range(8)],
                    axis=0,
                )
                product = dot_rows(level_three[ring * 8 + z], right)
                total = product if total is None else total + product
        lift_ref[origin] = total
    lat_count, lon_count = 6, 8
    for side in range(2):
        here = slice(side * 512, side * 512 + 512)
        level_ref[:, here] = (
            second_ref[:, here].astype(jnp.float32)
            + spread_rows(lift_ref[side], lat_count, lon_count)
        ).astype(jnp.bfloat16)
    for weights_ref, origin in ((late_ref, core), (swapped_ref, 1 - core)):
        total = None
        for ring in range(2):
            for z in range(0, 8, 2):
                right = jnp.concatenate(
                    [
                        jnp.concatenate(
                            [
                                weights_ref[
                                    (2 * row + part) * 8 + zz, :, ring * 1152 + 512 : ring * 1152 + 640
                                ]
                                for zz in (z, z + 1)
                                for row in range(4)
                            ],
                            axis=0,
                        )
                        for part in range(2)
                    ],
                    axis=1,
                )
                start = (ring * 8 + z) * 64
                product = dot_rows(level_ref[:, start : start + 128], right)
                total = product if total is None else total + product
        small_ref[origin] = total
    for side in range(2):
        here = slice(side * 256, side * 256 + 256)
        out_ref[:, here] = (
            skip_ref[:, here].astype(jnp.float32)
            + spread_rows(small_ref[side], 2 * lat_count, 2 * lon_count)
        ).astype(jnp.bfloat16)


Z_RING = 8
RINGS = [[ring * Z_RING + place for place in range(Z_RING)] for ring in range(2)]


def neighbours(first, last, axis):
    count = lax.axis_size(axis)
    before = lax.ppermute(last, axis, [(i, (i + 1) % count) for i in range(count)])
    behind = lax.ppermute(first, axis, [((i + 1) % count, i) for i in range(count)])
    return before, behind


def swap_cores(values):
    count = lax.axis_size("lon")
    return lax.ppermute(values, "lon", [(i, i ^ 1) for i in range(count)])


def swap_rings(values):
    count = lax.axis_size("lat")
    return lax.ppermute(values, "lat", [(i, (i + Z_RING) % count) for i in range(count)])


def ring_scatter(blocks):
    return lax.all_to_all(blocks, "lat", 0, 0, axis_index_groups=RINGS, tiled=True)


def ring_shift(values, step):
    pairs = [(at, at // Z_RING * Z_RING + (at + step) % Z_RING) for at in range(2 * Z_RING)]
    return lax.ppermute(values, "lat", pairs)


def ring_gather(values):
    return ring_scatter(jnp.broadcast_to(values[None], (Z_RING,) + values.shape))


def in_order(flag, own, other, axis):
    return jnp.where(
        flag == 0,
        jnp.concatenate([own, other], axis=axis),
        jnp.concatenate([other, own], axis=axis),
    )


def cut(values, row, rows, column, columns):
    return lax.dynamic_slice(values, (row, column), (rows, columns))


def after(values, *before):
    return lax.optimization_barrier((values,) + before)[0]


def on_device(
    fields,
    land_ids,
    surface_table,
    level_table,
    norm_first,
    qkv_first,
    out_first,
    norm_merge2,
    merge_second,
    norm_merge3,
    merge_third,
    norm_third,
    qkv_third,
    out_third,
    up_third,
    up_second,
):
    tile_rows, levels, tile_cols, feat_dim = fields.shape
    lat_count = lax.axis_size("lat")
    ring = lax.axis_index("lat") // Z_RING
    core = lax.axis_index("lon") % 2
    column = lax.axis_index("lon") // 4

    own_merge = jnp.concatenate(
        [lax.dynamic_slice_in_dim(merge_second, core * 512, 512, 1), out_first], axis=0
    )[None]
    both_merge = in_order(ring, own_merge, swap_rings(own_merge), 0)
    merge_weights = lax.all_gather(
        both_merge, "lat", axis=1, axis_index_groups=RINGS, tiled=True
    )
    core_place = jnp.stack([core, lax.axis_index("lat") % Z_RING, ring]).astype(jnp.int32)
    picks = (land_ids[:, :, None] == jnp.arange(3, dtype=jnp.int32)).astype(jnp.float32)
    surface = jnp.einsum("ijs,sc->ijc", picks, surface_table.astype(jnp.float32))
    hidden = (
        fields.astype(jnp.float32)
        + surface[:, None, :, :]
        + level_table.astype(jnp.float32)[None, :, None, :]
    ).astype(jnp.bfloat16)
    hidden = after(hidden, both_merge)
    above, below = neighbours(hidden[:2], hidden[-2:], "lat")
    cells = jnp.concatenate([above, hidden, below], axis=0)
    qkv_third = qkv_third.transpose(0, 2, 1).reshape(-1, qkv_third.shape[1])

    merge_third, qkv_third, up_third, up_second, out_third, cells = lax.optimization_barrier(
        (merge_third, qkv_third, up_third, up_second, out_third, cells)
    )
    left, right = neighbours(cells[:, :, :2], cells[:, :, -2:], "lon")

    merge_mine, qkv_mine = [
        swap_rings(lax.dynamic_slice_in_dim(table, core * (table.shape[0] // 2), table.shape[0] // 2))
        for table in (merge_third, qkv_third)
    ]

    own_rest = jnp.concatenate(
        [
            cut(up_third, column * 16, 16, core * 512, 512),
            cut(up_second, column // 2 * 16, 16, core * 256 + column % 2 * 128, 128),
            cut(out_third, column // 2 * 16, 16, column % 2 * 1024 + core * 512, 512),
        ],
        axis=1,
    )
    other_rest = swap_rings(own_rest)
    late = in_order(ring, own_rest, other_rest, 1)

    padded = jnp.pad(late, ((0, 0), (0, 4096 - late.shape[1])))
    late_rows = lax.all_gather(
        padded, "lat", axis=0, axis_index_groups=RINGS, tiled=True
    )

    ext_rows = tile_rows + 4
    own_window = (jnp.arange(32 * 4) % tile_cols + 2) // 4
    key_window = jnp.concatenate(
        [own_window, jnp.zeros((16,), jnp.int32), jnp.full((16,), tile_cols // 4, jnp.int32)]
    )
    same_window = (key_window[:, None] == own_window[None, :]).astype(jnp.float32)
    lat_place = lax.axis_index("lat") * tile_rows + jnp.arange(ext_rows) - 2
    valid_rows = ((lat_place >= 0) & (lat_place < tile_rows * lat_count)).astype(jnp.float32)
    valid_rows = valid_rows.reshape(ext_rows // 4, 4, 1)
    valid_keys = jnp.concatenate(
        [jnp.repeat(valid_rows, 2 * count, axis=1) for count in (tile_cols, 2, 2)], axis=1
    )
    attended = call_kernel(
        first_kernel,
        jax.ShapeDtypeStruct((tile_rows * levels * tile_cols, feat_dim), jnp.bfloat16),
        (
            cells.reshape(-1, feat_dim),
            left.reshape(-1, feat_dim),
            right.reshape(-1, feat_dim),
            norm_first[None],
            qkv_first,
            same_window,
            valid_keys,
        ),
        flops=2 * 640 * 512 * 1536,
    )
    attended = after(attended, merge_mine, qkv_mine, padded)
    tokens = attended.shape[0]
    skip_first, merged_in = call_kernel(
        skip_kernel,
        (
            jax.ShapeDtypeStruct((tokens, feat_dim), jnp.bfloat16),
            jax.ShapeDtypeStruct((tokens // 4, 4 * feat_dim), jnp.bfloat16),
        ),
        (attended, hidden.reshape(-1, feat_dim), merge_weights, norm_merge2[None]),
        flops=2 * 384 * 512 * 512,
    )
    own_rows = merged_in.shape[0]
    half_shape = jax.ShapeDtypeStruct((own_rows, 512), jnp.bfloat16)
    merge_partner, qkv_partner = swap_cores(merge_mine), swap_cores(qkv_mine)
    second_half, second_send = call_kernel(
        merge_kernel,
        (half_shape, half_shape),
        (merged_in, after(swap_cores(merged_in), merge_partner, qkv_partner), merge_weights),
        flops=2 * 192 * 2048 * 512,
    )
    second_cells, coarse_in = call_kernel(
        join_kernel,
        (
            jax.ShapeDtypeStruct((own_rows, 1024), jnp.bfloat16),
            jax.ShapeDtypeStruct((own_rows // 4, 4096), jnp.bfloat16),
        ),
        (core_place, second_half, swap_cores(second_send), norm_merge3[None]),
        (pltpu.VMEM((2, own_rows, 512), jnp.bfloat16),),
        flops=2 * 96 * 96 * 1024,
    )
    own_count = coarse_in.shape[0]

    pieces, forth, back = [coarse_in], coarse_in, coarse_in
    for _ in range(3):
        forth, back = ring_shift(forth, 1), ring_shift(back, -1)
        pieces += [forth, back]
    late = lax.all_gather(
        after(late_rows, pieces[1])[:, : late.shape[1]],
        "lon",
        axis=0,
        axis_index_groups=[[4 * y + x for y in range(8)] for x in range(4)],
        tiled=True,
    ).reshape(64, 16, -1)
    half_feats = coarse_in.shape[1] // 2
    pieces += [ring_shift(forth[:, :half_feats], 1), ring_shift(back[:, half_feats:], -1)]
    column_block = call_kernel(
        columns_kernel,
        jax.ShapeDtypeStruct((Z_RING, 2, own_count, 128), jnp.bfloat16),
        (core_place, *pieces, merge_third, merge_mine, merge_partner),
        flops=2 * 192 * 4096 * 256,
    )
    heads_out, own_coarse = call_kernel(
        third_kernel,
        (
            jax.ShapeDtypeStruct((Z_RING, 2, own_count, HD), jnp.bfloat16),
            jax.ShapeDtypeStruct((own_count, 2048), jnp.float32),
        ),
        (core_place, ring_gather(column_block), norm_third[None], qkv_third, qkv_mine, qkv_partner),
        (pltpu.VMEM((Z_RING * own_count, 2048), jnp.bfloat16),),
        flops=2 * 192 * 2048 * 384,
    )

    late_swapped = swap_cores(after(late, heads_out))
    decoded = call_kernel(
        up_kernel,
        jax.ShapeDtypeStruct((tile_rows * levels * tile_cols, feat_dim), jnp.bfloat16),
        (
            core_place,
            ring_scatter(heads_out),
            own_coarse,
            late,
            late_swapped,
            second_cells,
            skip_first,
        ),
        (
            pltpu.VMEM((2, 2, own_count, 512), jnp.float32),
            pltpu.VMEM((2, own_count, 512), jnp.float32),
            pltpu.VMEM((second_cells.shape[0], 1024), jnp.bfloat16),
            pltpu.VMEM((2, second_cells.shape[0], 256), jnp.float32),
        ),
        flops=2 * (24 * 1024 * 2048 + 24 * 2048 * 1024 + 96 * 1024 * 512),
    )
    return decoded.reshape(fields.shape)


def solution(mesh):
    in_specs = (
        P("lat", None, "lon", None),
        P("lat", "lon"),
        P(),
        P(),
        P(),
        P(),
        P("lat", None),
        P(),
        P("lat", None),
        P(),
        P(None, "lat"),
        P(),
        P(None, None, "lat"),
        P("lat", None),
        P("lat", None),
        P("lat", None),
    )
    out_specs = P("lat", None, "lon", None)
    return jax.shard_map(
        on_device, mesh=mesh, in_specs=in_specs, out_specs=out_specs, check_vma=False
    )
```

```python
import jax
import jax.numpy as jnp
from jax import lax
from jax.experimental import pallas as pl
from jax.experimental.pallas import tpu as pltpu
from jax.sharding import PartitionSpec as P

HD = 64


def norm_rows(values, gain):
    row_mean = jnp.mean(values, axis=-1, keepdims=True)
    centred = values - row_mean
    spread = jnp.mean(centred * centred, axis=-1, keepdims=True)
    return centred * lax.rsqrt(spread + 1e-05) * gain


def call_kernel(body, out_shape, operands, scratch=(), flops=0):
    smem = [operand.dtype == jnp.int32 for operand in operands]
    return pl.pallas_call(
        body,
        out_shape=out_shape,
        in_specs=[
            pl.BlockSpec(memory_space=pltpu.SMEM if scalar else pltpu.VMEM) for scalar in smem
        ],
        out_specs=jax.tree.map(lambda _: pl.BlockSpec(memory_space=pltpu.VMEM), out_shape),
        scratch_shapes=list(scratch),
        compiler_params=pltpu.CompilerParams(vmem_limit_bytes=48 * 1024 * 1024),
        cost_estimate=pl.CostEstimate(
            flops=flops,
            bytes_accessed=sum(operand.size * operand.dtype.itemsize for operand in operands),
            transcendentals=0,
        ),
    )(*operands)


def dot_rows(left, right):
    return lax.dot_general(left, right, (((1,), (0,)), ((), ())), preferred_element_type=jnp.float32)


def mix_tokens(query, key, value, keep):
    scores = lax.dot_general(
        key, query, (((1,), (1,)), ((), ())), preferred_element_type=jnp.float32
    )
    scores = jnp.where(keep, scores, -1e30)
    weights = jnp.exp(scores - jnp.max(scores, axis=0, keepdims=True))
    weights = (weights / jnp.sum(weights, axis=0, keepdims=True)).astype(jnp.bfloat16)
    return lax.dot_general(
        weights, value, (((0,), (0,)), ((), ())), preferred_element_type=jnp.float32
    )


def pack_kernel(place_ref, merge_ref, first_ref, up_third_ref, up_second_ref, out_third_ref, out_ref):
    core, column = place_ref[0], place_ref[1]
    out_ref[:128, :512] = merge_ref[:, pl.ds(pl.multiple_of(core * 512, 128), 512)]
    out_ref[128:, :512] = first_ref[...]
    high, low = jnp.right_shift(column, 1), jnp.bitwise_and(column, 1)
    rows = pl.ds(pl.multiple_of(high * 16, 16), 16)
    for tile in range(4):
        start = pl.multiple_of(core * 512 + tile * 128, 128)
        out_ref[tile * 16 : tile * 16 + 16, 512:] = up_third_ref[
            pl.ds(pl.multiple_of(column * 16, 16), 16), pl.ds(start, 128)
        ]
        start = pl.multiple_of(low * 1024 + core * 512 + tile * 128, 128)
        out_ref[64 + tile * 16 : 80 + tile * 16, 512:] = out_third_ref[rows, pl.ds(start, 128)]
    last = up_second_ref[rows, pl.ds(pl.multiple_of(core * 256 + low * 128, 128), 128)]
    out_ref[128:144, 512:] = last
    out_ref[144:, 512:] = last


def first_kernel(x_ref, left_ref, right_ref, gain_ref, qkv_ref, window_ref, lat_ref, out_ref):
    steps = lat_ref.shape[0]
    own, side = x_ref.shape[0] // steps, left_ref.shape[0] // steps
    lane = lax.broadcasted_iota(jnp.int32, (own, 128), 1)
    key_lane = lax.broadcasted_iota(jnp.int32, (own + 2 * side, 128), 1)
    gain = gain_ref[...]
    for step in range(steps):
        rows = jnp.concatenate(
            [
                x_ref[step * own : (step + 1) * own, :],
                left_ref[step * side : (step + 1) * side, :],
                right_ref[step * side : (step + 1) * side, :],
            ],
            axis=0,
        )
        normed = norm_rows(rows.astype(jnp.float32), gain).astype(jnp.bfloat16)
        query = dot_rows(normed[:own], qkv_ref[0]).astype(jnp.bfloat16)
        query = (query * 0.125).astype(jnp.bfloat16)
        key = dot_rows(normed, qkv_ref[1]).astype(jnp.bfloat16)
        value = dot_rows(normed, qkv_ref[2]).astype(jnp.bfloat16)
        keep = window_ref[...] * lat_ref[step] > 0.0
        first = own // 2 if step == 0 else 0
        last = own // 2 if step == steps - 1 else own
        start = step * own - own // 2 + first
        for pair in range(query.shape[1] // 128):
            here = slice(pair * 128, pair * 128 + 128)
            parts = []
            for odd in range(2):
                picked = (key_lane < HD) if odd == 0 else (key_lane >= HD)
                key_side = jnp.where(picked, key[:, here], jnp.zeros_like(key[:, here]))
                parts.append(mix_tokens(query[:, here], key_side, value[:, here], keep))
            mixed = jnp.where(lane < HD, parts[0], parts[1]).astype(jnp.bfloat16)
            out_ref[start : start + last - first, here] = mixed[first:last]


def pick_matrix(lat_count, lon_count, lat_side, lon_side):
    shape = (2 * lat_count * lon_count, 8 * lat_count * lon_count)
    row = lax.broadcasted_iota(jnp.int32, shape, 0)
    column = lax.broadcasted_iota(jnp.int32, shape, 1)
    bits = lon_count.bit_length() - 1
    lon = row & (lon_count - 1)
    level = jnp.right_shift(row, bits) & 1
    lat = jnp.right_shift(row, bits + 1)
    source = ((2 * lat + lat_side) * 2 + level) * (2 * lon_count) + 2 * lon + lon_side
    return jnp.where(source == column, 1.0, 0.0).astype(jnp.bfloat16)


def join_quads(cells, lat_count, lon_count, gain_ref, out_ref):
    width = cells.shape[1]
    parts = [
        dot_rows(pick_matrix(lat_count, lon_count, lat_side, lon_side), cells)
        for lat_side in range(2)
        for lon_side in range(2)
    ]
    count = 1.0 / (4 * width)
    row_mean = sum(jnp.sum(part, axis=-1, keepdims=True) for part in parts) * count
    parts = [part - row_mean for part in parts]
    spread = sum(jnp.sum(part * part, axis=-1, keepdims=True) for part in parts) * count
    scale = lax.rsqrt(spread + 1e-05)
    for place, part in enumerate(parts):
        here = slice(place * width, place * width + width)
        out_ref[:, here] = (part * scale * gain_ref[:, here]).astype(jnp.bfloat16)


def skip_kernel(attended_ref, hidden_ref, weights_ref, gain_ref, skip_ref, merged_ref):
    total = None
    for ring in range(2):
        for z in range(0, 8, 4):
            right = jnp.concatenate(
                [weights_ref[ring, zz * 160 + 128 : zz * 160 + 160, :512] for zz in range(z, z + 4)],
                axis=0,
            )
            start = (ring * 8 + z) * 32
            product = dot_rows(attended_ref[:, start : start + 128], right)
            total = product if total is None else total + product
    skip = (hidden_ref[...].astype(jnp.float32) + total).astype(jnp.bfloat16)
    skip_ref[...] = skip
    join_quads(skip, 6, 8, gain_ref, merged_ref)


def merge_kernel(own_ref, other_ref, weights_ref, own_out_ref, send_ref):
    left = jnp.concatenate([own_ref[...], other_ref[...]], axis=0)
    total = None
    for ring in range(2):
        for z in range(0, 8, 2):
            right = jnp.concatenate(
                [weights_ref[ring, zz * 160 : zz * 160 + 128, :512] for zz in (z, z + 1)], axis=0
            )
            start = (ring * 8 + z) * 128
            product = dot_rows(left[:, start : start + 256], right)
            total = product if total is None else total + product
    rows = own_ref.shape[0]
    own_out_ref[...] = total[:rows].astype(jnp.bfloat16)
    send_ref[...] = total[rows:].astype(jnp.bfloat16)


def join_kernel(core_ref, own_ref, recv_ref, gain_ref, second_ref, coarse_ref, halves_ref):
    core = core_ref[0]
    halves_ref[core] = own_ref[...]
    halves_ref[1 - core] = recv_ref[...]
    second = jnp.concatenate([halves_ref[0], halves_ref[1]], axis=1)
    second_ref[...] = second
    join_quads(second, 3, 4, gain_ref, coarse_ref)


RING_ORDER = (0, -1, 1, -2, 2, -3, 3)


def halves_in_order(core, mine_ref, partner_ref):
    mine, partner = mine_ref[...], partner_ref[...]
    first = core == 0
    return jnp.concatenate(
        [jnp.where(first, mine, partner), jnp.where(first, partner, mine)], axis=0
    )


def columns_kernel(place_ref, *refs):
    near, (far_low, far_high), (own_ref, *halves, out_ref) = refs[:7], refs[7:9], refs[9:]
    rows, half = far_low.shape
    left = jnp.concatenate([ref[...].astype(jnp.float32) for ref in near], axis=0)
    left = left.astype(jnp.bfloat16)
    ring = place_ref[2]
    own = own_ref[...]
    for weights, shard in ((own, ring), (halves_in_order(place_ref[0], *halves), 1 - ring)):
        product = dot_rows(left, weights)
        for at, offset in enumerate(RING_ORDER):
            place = jnp.bitwise_and(place_ref[1] + (offset + 8), 7)
            out_ref[place, shard] = product[at * rows : (at + 1) * rows].astype(jnp.bfloat16)
        far = dot_rows(far_low[...], weights[:half]) + dot_rows(far_high[...], weights[half:])
        out_ref[jnp.bitwise_and(place_ref[1] + 4, 7), shard] = far.astype(jnp.bfloat16)


def third_kernel(
    place_ref, x_ref, gain_ref, own_ref, mine_ref, partner_ref, out_ref, coarse_ref, normed_ref
):
    blocks, places, shards, rows, width = x_ref.shape
    count = 1.0 / (blocks * shards * width)
    order = [(z, shard) for shard in range(shards) for z in range(blocks)]
    for first in range(0, places, 2):
        tiles = [
            jnp.concatenate(
                [x_ref[z, first + at, shard].astype(jnp.float32) for at in range(2)], axis=0
            )
            for z, shard in order
        ]
        row_mean = jnp.sum(sum(tiles), axis=-1, keepdims=True) * count
        tiles = [tile - row_mean for tile in tiles]
        spread = jnp.sum(sum(tile * tile for tile in tiles), axis=-1, keepdims=True)
        scale = lax.rsqrt(spread * count + 1e-05)
        for at, tile in enumerate(tiles):
            here = slice(at * width, (at + 1) * width)
            normed_ref[first * rows : (first + 2) * rows, here] = (
                tile * scale * gain_ref[:, here]
            ).astype(jnp.bfloat16)
    for at, (z, shard) in enumerate(order):
        coarse_ref[:, at * width : (at + 1) * width] = x_ref[z, place_ref[1], shard].astype(
            jnp.float32
        )
    query_token = lax.broadcasted_iota(jnp.int32, (96, 96), 0)
    key_token = lax.broadcasted_iota(jnp.int32, (96, 96), 1)
    keep = jnp.right_shift(query_token, 5) == jnp.right_shift(key_token, 5)
    ring = place_ref[2]
    other = halves_in_order(place_ref[0], mine_ref, partner_ref)
    for weights, shard in ((own_ref[...], ring), (other, 1 - ring)):
        triple = lax.dot_general(
            normed_ref[...],
            weights,
            (((1,), (1,)), ((), ())),
            preferred_element_type=jnp.float32,
        ).astype(jnp.bfloat16)
        query = (triple[:, :HD] * 0.125).astype(jnp.bfloat16)
        key = triple[:, HD : 2 * HD]
        value = triple[:, 2 * HD :]
        for group in range(places * rows // 96):
            mine = slice(group * 96, group * 96 + 96)
            mixed = mix_tokens(query[mine], key[mine], value[mine], keep)
            for at in range(96 // rows):
                out_ref[group * (96 // rows) + at, shard] = mixed[
                    at * rows : (at + 1) * rows
                ].astype(jnp.bfloat16)


def spread_matrix(lat_count, lon_count):
    fine = (2 * lat_count * lon_count, lat_count * lon_count // 2)
    row = lax.broadcasted_iota(jnp.int32, fine, 0)
    column = lax.broadcasted_iota(jnp.int32, fine, 1)
    bits = lon_count.bit_length() - 1
    lat = jnp.right_shift(row, bits + 2)
    level = jnp.right_shift(row, bits) & 1
    lon = jnp.right_shift(row & (lon_count - 1), 1)
    source = (lat * 2 + level) * (lon_count // 2) + lon
    return jnp.where(source == column, 1.0, 0.0).astype(jnp.bfloat16)


def spread_rows(values, lat_count, lon_count):
    matrix = spread_matrix(lat_count, lon_count)
    high = values.astype(jnp.bfloat16)
    rest = values - high.astype(jnp.float32)
    middle = rest.astype(jnp.bfloat16)
    low = (rest - middle.astype(jnp.float32)).astype(jnp.bfloat16)
    return dot_rows(matrix, high) + (dot_rows(matrix, middle) + dot_rows(matrix, low))


def late_tile(ref, column, ring, z, tile):
    return ref[((column * 2 + ring) * 8 + z) * 9 + tile]


def late_row(ref, column, ring, z, first):
    return jnp.concatenate([late_tile(ref, column, ring, z, first + at) for at in range(4)], axis=1)


def up_kernel(
    core_ref, heads_ref, own_coarse_ref, late_ref, swapped_ref, second_ref, skip_ref, out_ref,
    third_ref, lift_ref, level_ref, small_ref,
):
    core = core_ref[0]
    pairs = []
    for ring in range(2):
        for z in range(0, 8, 2):
            pairs.append(
                jnp.concatenate(
                    [heads_ref[z, ring].astype(jnp.float32), heads_ref[z + 1, ring].astype(jnp.float32)],
                    axis=1,
                ).astype(jnp.bfloat16)
            )
    for weights_ref, origin in ((late_ref, core), (swapped_ref, 1 - core)):
        for part in range(2):
            total = None
            for ring in range(2):
                for z in range(0, 8, 2):
                    right = jnp.concatenate(
                        [
                            late_row(weights_ref, 2 * row + part, ring, zz, 4)
                            for zz in (z, z + 1)
                            for row in range(4)
                        ],
                        axis=0,
                    )
                    product = dot_rows(pairs[ring * 4 + z // 2], right)
                    total = product if total is None else total + product
            third_ref[part, origin] = total
    level_three = []
    for place in range(16):
        here = slice(place * 128, place * 128 + 128)
        quarter = place // 4
        update = third_ref[quarter // 2, quarter % 2][:, place % 4 * 128 : place % 4 * 128 + 128]
        level_three.append((own_coarse_ref[:, here] + update).astype(jnp.bfloat16))
    for weights_ref, origin in ((late_ref, core), (swapped_ref, 1 - core)):
        total = None
        for ring in range(2):
            for z in range(8):
                right = jnp.concatenate(
                    [late_row(weights_ref, y, ring, z, 0) for y in range(8)],
                    axis=0,
                )
                product = dot_rows(level_three[ring * 8 + z], right)
                total = product if total is None else total + product
        lift_ref[origin] = total
    lat_count, lon_count = 6, 8
    for side in range(2):
        here = slice(side * 512, side * 512 + 512)
        level_ref[:, here] = (
            second_ref[:, here].astype(jnp.float32)
            + spread_rows(lift_ref[side], lat_count, lon_count)
        ).astype(jnp.bfloat16)
    for weights_ref, origin in ((late_ref, core), (swapped_ref, 1 - core)):
        total = None
        for ring in range(2):
            for z in range(0, 8, 2):
                right = jnp.concatenate(
                    [
                        jnp.concatenate(
                            [
                                late_tile(weights_ref, 2 * row + part, ring, zz, 8)
                                for zz in (z, z + 1)
                                for row in range(4)
                            ],
                            axis=0,
                        )
                        for part in range(2)
                    ],
                    axis=1,
                )
                start = (ring * 8 + z) * 64
                product = dot_rows(level_ref[:, start : start + 128], right)
                total = product if total is None else total + product
        small_ref[origin] = total
    for side in range(2):
        here = slice(side * 256, side * 256 + 256)
        out_ref[:, here] = (
            skip_ref[:, here].astype(jnp.float32)
            + spread_rows(small_ref[side], 2 * lat_count, 2 * lon_count)
        ).astype(jnp.bfloat16)


Z_RING = 8
RINGS = [[ring * Z_RING + place for place in range(Z_RING)] for ring in range(2)]


def neighbours(first, last, axis):
    count = lax.axis_size(axis)
    before = lax.ppermute(last, axis, [(i, (i + 1) % count) for i in range(count)])
    behind = lax.ppermute(first, axis, [((i + 1) % count, i) for i in range(count)])
    return before, behind


def swap_cores(values):
    count = lax.axis_size("lon")
    return lax.ppermute(values, "lon", [(i, i ^ 1) for i in range(count)])


def swap_rings(values):
    count = lax.axis_size("lat")
    return lax.ppermute(values, "lat", [(i, (i + Z_RING) % count) for i in range(count)])


def ring_scatter(blocks):
    return lax.all_to_all(blocks, "lat", 0, 0, axis_index_groups=RINGS, tiled=True)


def ring_shift(values, step):
    pairs = [(at, at // Z_RING * Z_RING + (at + step) % Z_RING) for at in range(2 * Z_RING)]
    return lax.ppermute(values, "lat", pairs)


def ring_gather(values):
    return ring_scatter(jnp.broadcast_to(values[None], (Z_RING,) + values.shape))


def in_order(flag, own, other, axis):
    return jnp.where(
        flag == 0,
        jnp.concatenate([own, other], axis=axis),
        jnp.concatenate([other, own], axis=axis),
    )


def after(values, *before):
    return lax.optimization_barrier((values,) + before)[0]


def on_device(
    fields,
    land_ids,
    surface_table,
    level_table,
    norm_first,
    qkv_first,
    out_first,
    norm_merge2,
    merge_second,
    norm_merge3,
    merge_third,
    norm_third,
    qkv_third,
    out_third,
    up_third,
    up_second,
):
    tile_rows, levels, tile_cols, feat_dim = fields.shape
    lat_count = lax.axis_size("lat")
    ring = lax.axis_index("lat") // Z_RING
    core = lax.axis_index("lon") % 2
    column = lax.axis_index("lon") // 4

    own_merge = call_kernel(
        pack_kernel,
        jax.ShapeDtypeStruct((160, 640), jnp.bfloat16),
        (
            jnp.stack([core, column]).astype(jnp.int32),
            merge_second,
            out_first,
            up_third,
            up_second,
            out_third,
        ),
    )[None]
    both_merge = in_order(ring, own_merge, swap_rings(own_merge), 0)
    merge_weights = lax.all_gather(
        both_merge, "lat", axis=1, axis_index_groups=RINGS, tiled=True
    )
    core_place = jnp.stack([core, lax.axis_index("lat") % Z_RING, ring]).astype(jnp.int32)
    picks = (land_ids[:, :, None] == jnp.arange(3, dtype=jnp.int32)).astype(jnp.float32)
    surface = jnp.einsum("ijs,sc->ijc", picks, surface_table.astype(jnp.float32))
    hidden = (
        fields.astype(jnp.float32)
        + surface[:, None, :, :]
        + level_table.astype(jnp.float32)[None, :, None, :]
    ).astype(jnp.bfloat16)
    hidden = after(hidden, both_merge)
    above, below = neighbours(hidden[:2], hidden[-2:], "lat")
    cells = jnp.concatenate([above, hidden, below], axis=0)
    qkv_third = qkv_third.transpose(0, 2, 1).reshape(-1, qkv_third.shape[1])

    left, right = neighbours(cells[:, :, :2], cells[:, :, -2:], "lon")
    merge_third, qkv_third, left, right = lax.optimization_barrier(
        (merge_third, qkv_third, left, right)
    )

    merge_mine, qkv_mine = [
        swap_rings(lax.dynamic_slice_in_dim(table, core * (table.shape[0] // 2), table.shape[0] // 2))
        for table in (merge_third, qkv_third)
    ]

    ext_rows = tile_rows + 4
    own_window = (jnp.arange(32 * 4) % tile_cols + 2) // 4
    key_window = jnp.concatenate(
        [own_window, jnp.zeros((16,), jnp.int32), jnp.full((16,), tile_cols // 4, jnp.int32)]
    )
    same_window = (key_window[:, None] == own_window[None, :]).astype(jnp.float32)
    lat_place = lax.axis_index("lat") * tile_rows + jnp.arange(ext_rows) - 2
    valid_rows = ((lat_place >= 0) & (lat_place < tile_rows * lat_count)).astype(jnp.float32)
    valid_rows = valid_rows.reshape(ext_rows // 4, 4, 1)
    valid_keys = jnp.concatenate(
        [jnp.repeat(valid_rows, 2 * count, axis=1) for count in (tile_cols, 2, 2)], axis=1
    )
    attended = call_kernel(
        first_kernel,
        jax.ShapeDtypeStruct((tile_rows * levels * tile_cols, feat_dim), jnp.bfloat16),
        (
            cells.reshape(-1, feat_dim),
            left.reshape(-1, feat_dim),
            right.reshape(-1, feat_dim),
            norm_first[None],
            qkv_first,
            same_window,
            valid_keys,
        ),
        flops=2 * 640 * 512 * 1536,
    )
    tokens = attended.shape[0]
    skip_first, merged_in = call_kernel(
        skip_kernel,
        (
            jax.ShapeDtypeStruct((tokens, feat_dim), jnp.bfloat16),
            jax.ShapeDtypeStruct((tokens // 4, 4 * feat_dim), jnp.bfloat16),
        ),
        (attended, hidden.reshape(-1, feat_dim), merge_weights, norm_merge2[None]),
        flops=2 * 384 * 512 * 512,
    )
    own_rows = merged_in.shape[0]
    half_shape = jax.ShapeDtypeStruct((own_rows, 512), jnp.bfloat16)
    merge_partner, qkv_partner = swap_cores(merge_mine), swap_cores(qkv_mine)
    second_half, second_send = call_kernel(
        merge_kernel,
        (half_shape, half_shape),
        (merged_in, after(swap_cores(merged_in), merge_mine, qkv_mine), merge_weights),
        flops=2 * 192 * 2048 * 512,
    )
    second_cells, coarse_in = call_kernel(
        join_kernel,
        (
            jax.ShapeDtypeStruct((own_rows, 1024), jnp.bfloat16),
            jax.ShapeDtypeStruct((own_rows // 4, 4096), jnp.bfloat16),
        ),
        (core_place, second_half, swap_cores(second_send), norm_merge3[None]),
        (pltpu.VMEM((2, own_rows, 512), jnp.bfloat16),),
        flops=2 * 96 * 96 * 1024,
    )
    coarse_in = after(coarse_in, merge_partner, qkv_partner)
    own_count = coarse_in.shape[0]

    pieces, forth, back = [coarse_in], coarse_in, coarse_in
    for _ in range(3):
        forth, back = ring_shift(forth, 1), ring_shift(back, -1)
        pieces += [forth, back]
    late = after(merge_weights, coarse_in).reshape(2, Z_RING, 10, 16, 640)[:, :, :9, :, 512:]
    late = lax.all_gather(
        late.reshape(-1, 128),
        "lon",
        axis=0,
        axis_index_groups=[[4 * y + x for y in range(8)] for x in range(4)],
        tiled=True,
    ).reshape(-1, 16, 128)
    half_feats = coarse_in.shape[1] // 2
    pieces += [ring_shift(forth[:, :half_feats], 1), ring_shift(back[:, half_feats:], -1)]
    column_block = call_kernel(
        columns_kernel,
        jax.ShapeDtypeStruct((Z_RING, 2, own_count, 128), jnp.bfloat16),
        (core_place, *pieces, merge_third, merge_mine, merge_partner),
        flops=2 * 192 * 4096 * 256,
    )
    heads_out, own_coarse = call_kernel(
        third_kernel,
        (
            jax.ShapeDtypeStruct((Z_RING, 2, own_count, HD), jnp.bfloat16),
            jax.ShapeDtypeStruct((own_count, 2048), jnp.float32),
        ),
        (core_place, ring_gather(column_block), norm_third[None], qkv_third, qkv_mine, qkv_partner),
        (pltpu.VMEM((Z_RING * own_count, 2048), jnp.bfloat16),),
        flops=2 * 192 * 2048 * 384,
    )

    late_swapped = swap_cores(after(late, heads_out))
    decoded = call_kernel(
        up_kernel,
        jax.ShapeDtypeStruct((tile_rows * levels * tile_cols, feat_dim), jnp.bfloat16),
        (
            core_place,
            ring_scatter(heads_out),
            own_coarse,
            late,
            late_swapped,
            second_cells,
            skip_first,
        ),
        (
            pltpu.VMEM((2, 2, own_count, 512), jnp.float32),
            pltpu.VMEM((2, own_count, 512), jnp.float32),
            pltpu.VMEM((second_cells.shape[0], 1024), jnp.bfloat16),
            pltpu.VMEM((2, second_cells.shape[0], 256), jnp.float32),
        ),
        flops=2 * (24 * 1024 * 2048 + 24 * 2048 * 1024 + 96 * 1024 * 512),
    )
    return decoded.reshape(fields.shape)


def solution(mesh):
    in_specs = (
        P("lat", None, "lon", None),
        P("lat", "lon"),
        P(),
        P(),
        P(),
        P(),
        P("lat", None),
        P(),
        P("lat", None),
        P(),
        P(None, "lat"),
        P(),
        P(None, None, "lat"),
        P("lat", None),
        P("lat", None),
        P("lat", None),
    )
    out_specs = P("lat", None, "lon", None)
    return jax.shard_map(
        on_device, mesh=mesh, in_specs=in_specs, out_specs=out_specs, check_vma=False
    )
```

```python
import jax
import jax.numpy as jnp
from jax import lax
from jax.experimental import pallas as pl
from jax.experimental.pallas import tpu as pltpu
from jax.sharding import PartitionSpec as P

HD = 64


def norm_rows(values, gain):
    row_mean = jnp.mean(values, axis=-1, keepdims=True)
    centred = values - row_mean
    spread = jnp.mean(centred * centred, axis=-1, keepdims=True)
    return centred * lax.rsqrt(spread + 1e-05) * gain


def call_kernel(body, out_shape, operands, scratch=(), flops=0, pulled=(), vmem_mib=48):
    spaces = [
        pltpu.SMEM if operand.dtype == jnp.int32 else pltpu.HBM if at in pulled else pltpu.VMEM
        for at, operand in enumerate(operands)
    ]
    return pl.pallas_call(
        body,
        out_shape=out_shape,
        in_specs=[pl.BlockSpec(memory_space=space) for space in spaces],
        out_specs=jax.tree.map(lambda _: pl.BlockSpec(memory_space=pltpu.VMEM), out_shape),
        scratch_shapes=list(scratch),
        compiler_params=pltpu.CompilerParams(vmem_limit_bytes=vmem_mib * 1024 * 1024),
        cost_estimate=pl.CostEstimate(
            flops=flops,
            bytes_accessed=sum(operand.size * operand.dtype.itemsize for operand in operands),
            transcendentals=0,
        ),
    )(*operands)


def pull(sems, *pairs):
    copies = [pltpu.make_async_copy(src, dst, sems.at[at]) for at, (src, dst) in enumerate(pairs)]
    for copy in copies:
        copy.start()
    return copies


def dot_rows(left, right):
    return lax.dot_general(left, right, (((1,), (0,)), ((), ())), preferred_element_type=jnp.float32)


def mix_tokens(query, key, value, keep):
    scores = lax.dot_general(
        key, query, (((1,), (1,)), ((), ())), preferred_element_type=jnp.float32
    )
    scores = jnp.where(keep, scores, -1e30)
    weights = jnp.exp(scores - jnp.max(scores, axis=0, keepdims=True))
    weights = (weights / jnp.sum(weights, axis=0, keepdims=True)).astype(jnp.bfloat16)
    return lax.dot_general(
        weights, value, (((0,), (0,)), ((), ())), preferred_element_type=jnp.float32
    )


def pack_kernel(
    place_ref, merge_ref, first_ref, up_third_ref, up_second_ref, out_third_ref, out_ref, sems
):
    core, column = place_ref[0], place_ref[1]
    high, low = jnp.right_shift(column, 1), jnp.bitwise_and(column, 1)

    def part(ref, row, lane, lanes=128, rows=16):
        return ref.at[pl.ds(pl.multiple_of(row, 16), rows), pl.ds(pl.multiple_of(lane, 128), lanes)]

    pairs = [
        (part(merge_ref, 0, core * 512, 512, 128), out_ref.at[:128, :512]),
        (first_ref, out_ref.at[128:, :512]),
    ]
    for tile in range(4):
        pairs.append(
            (
                part(up_third_ref, column * 16, core * 512 + tile * 128),
                out_ref.at[tile * 16 : tile * 16 + 16, 512:],
            )
        )
        pairs.append(
            (
                part(out_third_ref, high * 16, low * 1024 + core * 512 + tile * 128),
                out_ref.at[64 + tile * 16 : 80 + tile * 16, 512:],
            )
        )
    for row in (128, 144):
        pairs.append(
            (part(up_second_ref, high * 16, core * 256 + low * 128), out_ref.at[row : row + 16, 512:])
        )
    for copy in pull(sems, *pairs):
        copy.wait()


def first_kernel(x_ref, left_ref, right_ref, gain_ref, qkv_ref, window_ref, lat_ref, out_ref):
    steps = lat_ref.shape[0]
    own, side = x_ref.shape[0] // steps, left_ref.shape[0] // steps
    lane = lax.broadcasted_iota(jnp.int32, (own, 128), 1)
    key_lane = lax.broadcasted_iota(jnp.int32, (own + 2 * side, 128), 1)
    gain = gain_ref[...]
    for step in range(steps):
        rows = jnp.concatenate(
            [
                x_ref[step * own : (step + 1) * own, :],
                left_ref[step * side : (step + 1) * side, :],
                right_ref[step * side : (step + 1) * side, :],
            ],
            axis=0,
        )
        normed = norm_rows(rows.astype(jnp.float32), gain).astype(jnp.bfloat16)
        query = dot_rows(normed[:own], qkv_ref[0]).astype(jnp.bfloat16)
        query = (query * 0.125).astype(jnp.bfloat16)
        key = dot_rows(normed, qkv_ref[1]).astype(jnp.bfloat16)
        value = dot_rows(normed, qkv_ref[2]).astype(jnp.bfloat16)
        keep = window_ref[...] * lat_ref[step] > 0.0
        first = own // 2 if step == 0 else 0
        last = own // 2 if step == steps - 1 else own
        start = step * own - own // 2 + first
        for pair in range(query.shape[1] // 128):
            here = slice(pair * 128, pair * 128 + 128)
            parts = []
            for odd in range(2):
                picked = (key_lane < HD) if odd == 0 else (key_lane >= HD)
                key_side = jnp.where(picked, key[:, here], jnp.zeros_like(key[:, here]))
                parts.append(mix_tokens(query[:, here], key_side, value[:, here], keep))
            mixed = jnp.where(lane < HD, parts[0], parts[1]).astype(jnp.bfloat16)
            out_ref[start : start + last - first, here] = mixed[first:last]


def pick_matrix(lat_count, lon_count, lat_side, lon_side):
    shape = (2 * lat_count * lon_count, 8 * lat_count * lon_count)
    row = lax.broadcasted_iota(jnp.int32, shape, 0)
    column = lax.broadcasted_iota(jnp.int32, shape, 1)
    bits = lon_count.bit_length() - 1
    lon = row & (lon_count - 1)
    level = jnp.right_shift(row, bits) & 1
    lat = jnp.right_shift(row, bits + 1)
    source = ((2 * lat + lat_side) * 2 + level) * (2 * lon_count) + 2 * lon + lon_side
    return jnp.where(source == column, 1.0, 0.0).astype(jnp.bfloat16)


def join_quads(cells, lat_count, lon_count, gain_ref, out_ref):
    width = cells.shape[1]
    parts = [
        dot_rows(pick_matrix(lat_count, lon_count, lat_side, lon_side), cells)
        for lat_side in range(2)
        for lon_side in range(2)
    ]
    count = 1.0 / (4 * width)
    row_mean = sum(jnp.sum(part, axis=-1, keepdims=True) for part in parts) * count
    parts = [part - row_mean for part in parts]
    spread = sum(jnp.sum(part * part, axis=-1, keepdims=True) for part in parts) * count
    scale = lax.rsqrt(spread + 1e-05)
    for place, part in enumerate(parts):
        here = slice(place * width, place * width + width)
        out_ref[:, here] = (part * scale * gain_ref[:, here]).astype(jnp.bfloat16)


def skip_kernel(
    attended_ref, hidden_hbm, weights_hbm, gain_hbm, skip_ref, merged_ref,
    hidden_ref, weights_ref, gain_ref, sems,
):
    copies = pull(
        sems,
        (weights_hbm.at[:, :, 128:160, :512], weights_ref),
        (hidden_hbm, hidden_ref),
        (gain_hbm, gain_ref),
    )
    for copy in copies:
        copy.wait()
    total = None
    for ring in range(2):
        for z in range(0, 8, 4):
            right = jnp.concatenate(
                [weights_ref[ring, zz] for zz in range(z, z + 4)],
                axis=0,
            )
            start = (ring * 8 + z) * 32
            product = dot_rows(attended_ref[:, start : start + 128], right)
            total = product if total is None else total + product
    skip = (hidden_ref[...].astype(jnp.float32) + total).astype(jnp.bfloat16)
    skip_ref[...] = skip
    join_quads(skip, 6, 8, gain_ref, merged_ref)


def merge_kernel(own_ref, other_ref, weights_ref, own_out_ref, send_ref):
    left = jnp.concatenate([own_ref[...], other_ref[...]], axis=0)
    total = None
    for ring in range(2):
        for z in range(0, 8, 2):
            right = jnp.concatenate(
                [weights_ref[ring, zz * 160 : zz * 160 + 128, :512] for zz in (z, z + 1)], axis=0
            )
            start = (ring * 8 + z) * 128
            product = dot_rows(left[:, start : start + 256], right)
            total = product if total is None else total + product
    rows = own_ref.shape[0]
    own_out_ref[...] = total[:rows].astype(jnp.bfloat16)
    send_ref[...] = total[rows:].astype(jnp.bfloat16)


def join_kernel(core_ref, own_ref, recv_ref, gain_ref, second_ref, coarse_ref, halves_ref):
    core = core_ref[0]
    halves_ref[core] = own_ref[...]
    halves_ref[1 - core] = recv_ref[...]
    second = jnp.concatenate([halves_ref[0], halves_ref[1]], axis=1)
    second_ref[...] = second
    join_quads(second, 3, 4, gain_ref, coarse_ref)


RING_ORDER = (0, -1, 1, -2, 2, -3, 3)


def halves_in_order(core, mine_ref, partner_ref):
    mine, partner = mine_ref[...], partner_ref[...]
    first = core == 0
    return jnp.concatenate(
        [jnp.where(first, mine, partner), jnp.where(first, partner, mine)], axis=0
    )


def near_kernel(place_ref, *refs):
    near, (own_ref, *halves, out_ref) = refs[:7], refs[7:]
    left = jnp.concatenate([ref[...].astype(jnp.float32) for ref in near], axis=0)
    left = left.astype(jnp.bfloat16)
    rows = near[0].shape[0]
    own, other = own_ref[...], halves_in_order(place_ref[0], *halves)
    for weights, shard in ((own, place_ref[2]), (other, 1 - place_ref[2])):
        product = dot_rows(left, weights)
        for at in range(len(near)):
            out_ref[shard, at] = product[at * rows : (at + 1) * rows].astype(jnp.bfloat16)


def far_kernel(place_ref, near_ref, low_ref, high_ref, own_ref, mine_ref, partner_ref, out_ref):
    half = low_ref.shape[1]
    own, other = own_ref[...], halves_in_order(place_ref[0], mine_ref, partner_ref)
    for weights, shard in ((own, place_ref[2]), (other, 1 - place_ref[2])):
        far = dot_rows(low_ref[...], weights[:half]) + dot_rows(high_ref[...], weights[half:])
        out_ref[jnp.bitwise_and(place_ref[1] + 4, 7), shard] = far.astype(jnp.bfloat16)
    for shard in range(2):
        for at, offset in enumerate(RING_ORDER):
            place = jnp.bitwise_and(place_ref[1] + (offset + 8), 7)
            out_ref[place, shard] = near_ref[shard, at]


def third_kernel(
    place_ref, x_ref, gain_ref, own_hbm, mine_ref, partner_ref, out_ref, coarse_ref,
    normed_ref, own_ref, sems,
):
    (copy,) = pull(sems, (own_hbm, own_ref))
    blocks, places, shards, rows, width = x_ref.shape
    count = 1.0 / (blocks * shards * width)
    order = [(z, shard) for shard in range(shards) for z in range(blocks)]
    for first in range(0, places, 2):
        tiles = [
            jnp.concatenate(
                [x_ref[z, first + at, shard].astype(jnp.float32) for at in range(2)], axis=0
            )
            for z, shard in order
        ]
        row_mean = jnp.sum(sum(tiles), axis=-1, keepdims=True) * count
        tiles = [tile - row_mean for tile in tiles]
        spread = jnp.sum(sum(tile * tile for tile in tiles), axis=-1, keepdims=True)
        scale = lax.rsqrt(spread * count + 1e-05)
        for at, tile in enumerate(tiles):
            here = slice(at * width, (at + 1) * width)
            normed_ref[first * rows : (first + 2) * rows, here] = (
                tile * scale * gain_ref[:, here]
            ).astype(jnp.bfloat16)
    for at, (z, shard) in enumerate(order):
        coarse_ref[:, at * width : (at + 1) * width] = x_ref[z, place_ref[1], shard].astype(
            jnp.float32
        )
    query_token = lax.broadcasted_iota(jnp.int32, (96, 96), 0)
    key_token = lax.broadcasted_iota(jnp.int32, (96, 96), 1)
    keep = jnp.right_shift(query_token, 5) == jnp.right_shift(key_token, 5)
    ring = place_ref[2]
    other = halves_in_order(place_ref[0], mine_ref, partner_ref)
    copy.wait()
    for weights, shard in ((own_ref[...], ring), (other, 1 - ring)):
        triple = lax.dot_general(
            normed_ref[...],
            weights,
            (((1,), (1,)), ((), ())),
            preferred_element_type=jnp.float32,
        ).astype(jnp.bfloat16)
        query = (triple[:, :HD] * 0.125).astype(jnp.bfloat16)
        key = triple[:, HD : 2 * HD]
        value = triple[:, 2 * HD :]
        for group in range(places * rows // 96):
            mine = slice(group * 96, group * 96 + 96)
            mixed = mix_tokens(query[mine], key[mine], value[mine], keep)
            for at in range(96 // rows):
                out_ref[group * (96 // rows) + at, shard] = mixed[
                    at * rows : (at + 1) * rows
                ].astype(jnp.bfloat16)


def spread_matrix(lat_count, lon_count):
    fine = (2 * lat_count * lon_count, lat_count * lon_count // 2)
    row = lax.broadcasted_iota(jnp.int32, fine, 0)
    column = lax.broadcasted_iota(jnp.int32, fine, 1)
    bits = lon_count.bit_length() - 1
    lat = jnp.right_shift(row, bits + 2)
    level = jnp.right_shift(row, bits) & 1
    lon = jnp.right_shift(row & (lon_count - 1), 1)
    source = (lat * 2 + level) * (lon_count // 2) + lon
    return jnp.where(source == column, 1.0, 0.0).astype(jnp.bfloat16)


def spread_rows(values, lat_count, lon_count):
    matrix = spread_matrix(lat_count, lon_count)
    high = values.astype(jnp.bfloat16)
    rest = values - high.astype(jnp.float32)
    middle = rest.astype(jnp.bfloat16)
    low = (rest - middle.astype(jnp.float32)).astype(jnp.bfloat16)
    return dot_rows(matrix, high) + (dot_rows(matrix, middle) + dot_rows(matrix, low))


def late_tile(ref, column, ring, z, tile):
    return ref[((column * 2 + ring) * 8 + z) * 9 + tile]


def late_row(ref, column, ring, z, first):
    return jnp.concatenate([late_tile(ref, column, ring, z, first + at) for at in range(4)], axis=1)


def up_kernel(
    core_ref, heads_ref, own_coarse_ref, late_ref, swapped_ref, second_ref, skip_ref, out_ref,
    third_ref, lift_ref, level_ref, small_ref,
):
    core = core_ref[0]
    pairs = []
    for ring in range(2):
        for z in range(0, 8, 2):
            pairs.append(
                jnp.concatenate(
                    [heads_ref[z, ring].astype(jnp.float32), heads_ref[z + 1, ring].astype(jnp.float32)],
                    axis=1,
                ).astype(jnp.bfloat16)
            )
    for weights_ref, origin in ((swapped_ref, 1 - core), (late_ref, core)):
        for part in range(2):
            total = None
            for ring in range(2):
                for z in range(0, 8, 2):
                    right = jnp.concatenate(
                        [
                            late_row(weights_ref, 2 * row + part, ring, zz, 4)
                            for zz in (z, z + 1)
                            for row in range(4)
                        ],
                        axis=0,
                    )
                    product = dot_rows(pairs[ring * 4 + z // 2], right)
                    total = product if total is None else total + product
            third_ref[part, origin] = total
    level_three = []
    for place in range(16):
        here = slice(place * 128, place * 128 + 128)
        quarter = place // 4
        update = third_ref[quarter // 2, quarter % 2][:, place % 4 * 128 : place % 4 * 128 + 128]
        level_three.append((own_coarse_ref[:, here] + update).astype(jnp.bfloat16))
    for weights_ref, origin in ((late_ref, core), (swapped_ref, 1 - core)):
        total = None
        for ring in range(2):
            for z in range(8):
                right = jnp.concatenate(
                    [late_row(weights_ref, y, ring, z, 0) for y in range(8)],
                    axis=0,
                )
                product = dot_rows(level_three[ring * 8 + z], right)
                total = product if total is None else total + product
        lift_ref[origin] = total
    lat_count, lon_count = 6, 8
    for side in range(2):
        here = slice(side * 512, side * 512 + 512)
        level_ref[:, here] = (
            second_ref[:, here].astype(jnp.float32)
            + spread_rows(lift_ref[side], lat_count, lon_count)
        ).astype(jnp.bfloat16)
    for weights_ref, origin in ((late_ref, core), (swapped_ref, 1 - core)):
        total = None
        for ring in range(2):
            for z in range(0, 8, 2):
                right = jnp.concatenate(
                    [
                        jnp.concatenate(
                            [
                                late_tile(weights_ref, 2 * row + part, ring, zz, 8)
                                for zz in (z, z + 1)
                                for row in range(4)
                            ],
                            axis=0,
                        )
                        for part in range(2)
                    ],
                    axis=1,
                )
                start = (ring * 8 + z) * 64
                product = dot_rows(level_ref[:, start : start + 128], right)
                total = product if total is None else total + product
        small_ref[origin] = total
    for side in range(2):
        here = slice(side * 256, side * 256 + 256)
        out_ref[:, here] = (
            skip_ref[:, here].astype(jnp.float32)
            + spread_rows(small_ref[side], 2 * lat_count, 2 * lon_count)
        ).astype(jnp.bfloat16)


Z_RING = 8
RINGS = [[ring * Z_RING + place for place in range(Z_RING)] for ring in range(2)]


def neighbours(first, last, axis):
    count = lax.axis_size(axis)
    before = lax.ppermute(last, axis, [(i, (i + 1) % count) for i in range(count)])
    behind = lax.ppermute(first, axis, [((i + 1) % count, i) for i in range(count)])
    return before, behind


def swap_cores(values):
    count = lax.axis_size("lon")
    return lax.ppermute(values, "lon", [(i, i ^ 1) for i in range(count)])


def swap_rings(values):
    count = lax.axis_size("lat")
    return lax.ppermute(values, "lat", [(i, (i + Z_RING) % count) for i in range(count)])


def ring_scatter(blocks):
    return lax.all_to_all(blocks, "lat", 0, 0, axis_index_groups=RINGS, tiled=True)


def ring_shift(values, step):
    pairs = [(at, at // Z_RING * Z_RING + (at + step) % Z_RING) for at in range(2 * Z_RING)]
    return lax.ppermute(values, "lat", pairs)


def ring_gather(values):
    return ring_scatter(jnp.broadcast_to(values[None], (Z_RING,) + values.shape))


def in_order(flag, own, other, axis):
    return jnp.where(
        flag == 0,
        jnp.concatenate([own, other], axis=axis),
        jnp.concatenate([other, own], axis=axis),
    )


def after(values, *before):
    return lax.optimization_barrier((values,) + before)[0]


def on_device(
    fields,
    land_ids,
    surface_table,
    level_table,
    norm_first,
    qkv_first,
    out_first,
    norm_merge2,
    merge_second,
    norm_merge3,
    merge_third,
    norm_third,
    qkv_third,
    out_third,
    up_third,
    up_second,
):
    tile_rows, levels, tile_cols, feat_dim = fields.shape
    lat_count = lax.axis_size("lat")
    ring = lax.axis_index("lat") // Z_RING
    core = lax.axis_index("lon") % 2
    column = lax.axis_index("lon") // 4

    own_merge = call_kernel(
        pack_kernel,
        jax.ShapeDtypeStruct((160, 640), jnp.bfloat16),
        (
            jnp.stack([core, column]).astype(jnp.int32),
            merge_second,
            out_first,
            up_third,
            up_second,
            out_third,
        ),
        (pltpu.SemaphoreType.DMA((12,)),),
        pulled=(1, 2, 3, 4, 5),
        vmem_mib=62,
    )[None]
    both_merge = in_order(ring, own_merge, swap_rings(own_merge), 0)
    merge_weights = lax.all_gather(
        both_merge, "lat", axis=1, axis_index_groups=RINGS, tiled=True
    )
    core_place = jnp.stack([core, lax.axis_index("lat") % Z_RING, ring]).astype(jnp.int32)
    picks = (land_ids[:, :, None] == jnp.arange(3, dtype=jnp.int32)).astype(jnp.float32)
    surface = jnp.einsum("ijs,sc->ijc", picks, surface_table.astype(jnp.float32))
    hidden = (
        fields.astype(jnp.float32)
        + surface[:, None, :, :]
        + level_table.astype(jnp.float32)[None, :, None, :]
    ).astype(jnp.bfloat16)
    hidden = after(hidden, both_merge)
    above, below = neighbours(hidden[:2], hidden[-2:], "lat")
    cells = jnp.concatenate([above, hidden, below], axis=0)
    qkv_third = qkv_third.transpose(0, 2, 1).reshape(-1, qkv_third.shape[1])

    left, right = neighbours(cells[:, :, :2], cells[:, :, -2:], "lon")
    merge_third, qkv_third, left, right = lax.optimization_barrier(
        (merge_third, qkv_third, left, right)
    )

    merge_mine, qkv_mine = [
        swap_rings(lax.dynamic_slice_in_dim(table, core * (table.shape[0] // 2), table.shape[0] // 2))
        for table in (merge_third, qkv_third)
    ]

    ext_rows = tile_rows + 4
    own_window = (jnp.arange(32 * 4) % tile_cols + 2) // 4
    key_window = jnp.concatenate(
        [own_window, jnp.zeros((16,), jnp.int32), jnp.full((16,), tile_cols // 4, jnp.int32)]
    )
    same_window = (key_window[:, None] == own_window[None, :]).astype(jnp.float32)
    lat_place = lax.axis_index("lat") * tile_rows + jnp.arange(ext_rows) - 2
    valid_rows = ((lat_place >= 0) & (lat_place < tile_rows * lat_count)).astype(jnp.float32)
    valid_rows = valid_rows.reshape(ext_rows // 4, 4, 1)
    valid_keys = jnp.concatenate(
        [jnp.repeat(valid_rows, 2 * count, axis=1) for count in (tile_cols, 2, 2)], axis=1
    )
    attended = call_kernel(
        first_kernel,
        jax.ShapeDtypeStruct((tile_rows * levels * tile_cols, feat_dim), jnp.bfloat16),
        (
            cells.reshape(-1, feat_dim),
            left.reshape(-1, feat_dim),
            right.reshape(-1, feat_dim),
            norm_first[None],
            qkv_first,
            same_window,
            valid_keys,
        ),
        flops=2 * 640 * 512 * 1536,
    )
    tokens = attended.shape[0]
    skip_first, merged_in = call_kernel(
        skip_kernel,
        (
            jax.ShapeDtypeStruct((tokens, feat_dim), jnp.bfloat16),
            jax.ShapeDtypeStruct((tokens // 4, 4 * feat_dim), jnp.bfloat16),
        ),
        (
            attended,
            hidden.reshape(-1, feat_dim),
            merge_weights.reshape(2, Z_RING, 160, 640),
            norm_merge2[None],
        ),
        (
            pltpu.VMEM((tokens, feat_dim), jnp.bfloat16),
            pltpu.VMEM((2, Z_RING, 32, 512), jnp.bfloat16),
            pltpu.VMEM((1, 4 * feat_dim), jnp.float32),
            pltpu.SemaphoreType.DMA((3,)),
        ),
        flops=2 * 384 * 512 * 512,
        pulled=(1, 2, 3),
        vmem_mib=58,
    )
    late = after(merge_weights, merged_in).reshape(2, Z_RING, 10, 16, 640)[:, :, :9, :, 512:]
    late = lax.all_gather(
        late.reshape(-1, 128),
        "lon",
        axis=0,
        axis_index_groups=[[4 * y + x for y in range(8)] for x in range(4)],
        tiled=True,
    ).reshape(-1, 16, 128)
    own_rows = merged_in.shape[0]
    half_shape = jax.ShapeDtypeStruct((own_rows, 512), jnp.bfloat16)
    second_half, second_send = call_kernel(
        merge_kernel,
        (half_shape, half_shape),
        (merged_in, after(swap_cores(merged_in), merge_mine, qkv_mine), merge_weights),
        flops=2 * 192 * 2048 * 512,
    )
    second_cells, coarse_in = call_kernel(
        join_kernel,
        (
            jax.ShapeDtypeStruct((own_rows, 1024), jnp.bfloat16),
            jax.ShapeDtypeStruct((own_rows // 4, 4096), jnp.bfloat16),
        ),
        (core_place, second_half, swap_cores(second_send), norm_merge3[None]),
        (pltpu.VMEM((2, own_rows, 512), jnp.bfloat16),),
        flops=2 * 96 * 96 * 1024,
    )
    own_count = coarse_in.shape[0]

    pieces, forth, back = [coarse_in], coarse_in, coarse_in
    for _ in range(3):
        forth, back = ring_shift(forth, 1), ring_shift(back, -1)
        pieces += [forth, back]
    merge_mine, qkv_mine = after(merge_mine, pieces[1]), after(qkv_mine, pieces[3])
    merge_partner, qkv_partner = swap_cores(merge_mine), swap_cores(qkv_mine)
    half_feats = coarse_in.shape[1] // 2
    forth, back = after(forth, merge_partner), after(back, qkv_partner)
    far_low, far_high = ring_shift(forth[:, :half_feats], 1), ring_shift(back[:, half_feats:], -1)
    tables = (merge_third, merge_mine, merge_partner)
    near = call_kernel(
        near_kernel,
        jax.ShapeDtypeStruct((2, len(RING_ORDER), own_count, 128), jnp.bfloat16),
        (core_place, *pieces, *tables),
        flops=2 * 168 * 4096 * 256,
    )
    column_block = call_kernel(
        far_kernel,
        jax.ShapeDtypeStruct((Z_RING, 2, own_count, 128), jnp.bfloat16),
        (core_place, near, far_low, far_high, *tables),
        flops=2 * 24 * 4096 * 256,
    )
    heads_out, own_coarse = call_kernel(
        third_kernel,
        (
            jax.ShapeDtypeStruct((Z_RING, 2, own_count, HD), jnp.bfloat16),
            jax.ShapeDtypeStruct((own_count, 2048), jnp.float32),
        ),
        (core_place, ring_gather(column_block), norm_third[None], qkv_third, qkv_mine, qkv_partner),
        (
            pltpu.VMEM((Z_RING * own_count, 2048), jnp.bfloat16),
            pltpu.VMEM(qkv_third.shape, jnp.bfloat16),
            pltpu.SemaphoreType.DMA((1,)),
        ),
        flops=2 * 192 * 2048 * 384,
        pulled=(3,),
    )

    late_swapped = swap_cores(after(late, heads_out))
    decoded = call_kernel(
        up_kernel,
        jax.ShapeDtypeStruct((tile_rows * levels * tile_cols, feat_dim), jnp.bfloat16),
        (
            core_place,
            ring_scatter(heads_out),
            own_coarse,
            late,
            late_swapped,
            second_cells,
            skip_first,
        ),
        (
            pltpu.VMEM((2, 2, own_count, 512), jnp.float32),
            pltpu.VMEM((2, own_count, 512), jnp.float32),
            pltpu.VMEM((second_cells.shape[0], 1024), jnp.bfloat16),
            pltpu.VMEM((2, second_cells.shape[0], 256), jnp.float32),
        ),
        flops=2 * (24 * 1024 * 2048 + 24 * 2048 * 1024 + 96 * 1024 * 512),
    )
    return decoded.reshape(fields.shape)


def solution(mesh):
    in_specs = (
        P("lat", None, "lon", None),
        P("lat", "lon"),
        P(),
        P(),
        P(),
        P(),
        P("lat", None),
        P(),
        P("lat", None),
        P(),
        P(None, "lat"),
        P(),
        P(None, None, "lat"),
        P("lat", None),
        P("lat", None),
        P("lat", None),
    )
    out_specs = P("lat", None, "lon", None)
    return jax.shard_map(
        on_device, mesh=mesh, in_specs=in_specs, out_specs=out_specs, check_vma=False
    )
```

```python
import jax
import jax.numpy as jnp
from jax import lax
from jax.experimental import pallas as pl
from jax.experimental.pallas import tpu as pltpu
from jax.sharding import PartitionSpec as P

HD = 64


def norm_rows(values, gain):
    row_mean = jnp.mean(values, axis=-1, keepdims=True)
    centred = values - row_mean
    spread = jnp.mean(centred * centred, axis=-1, keepdims=True)
    return centred * lax.rsqrt(spread + 1e-05) * gain


def call_kernel(body, out_shape, operands, scratch=(), flops=0, pulled=(), vmem_mib=48):
    spaces = [
        pltpu.SMEM if operand.dtype == jnp.int32 else pltpu.HBM if at in pulled else pltpu.VMEM
        for at, operand in enumerate(operands)
    ]
    return pl.pallas_call(
        body,
        out_shape=out_shape,
        in_specs=[pl.BlockSpec(memory_space=space) for space in spaces],
        out_specs=jax.tree.map(lambda _: pl.BlockSpec(memory_space=pltpu.VMEM), out_shape),
        scratch_shapes=list(scratch),
        compiler_params=pltpu.CompilerParams(vmem_limit_bytes=vmem_mib * 1024 * 1024),
        cost_estimate=pl.CostEstimate(
            flops=flops,
            bytes_accessed=sum(operand.size * operand.dtype.itemsize for operand in operands),
            transcendentals=0,
        ),
    )(*operands)


def pull(sems, *pairs):
    copies = [pltpu.make_async_copy(src, dst, sems.at[at]) for at, (src, dst) in enumerate(pairs)]
    for copy in copies:
        copy.start()
    return copies


def dot_rows(left, right):
    return lax.dot_general(left, right, (((1,), (0,)), ((), ())), preferred_element_type=jnp.float32)


def mix_tokens(query, key, value, keep):
    scores = lax.dot_general(
        key, query, (((1,), (1,)), ((), ())), preferred_element_type=jnp.float32
    )
    scores = jnp.where(keep, scores, -1e30)
    weights = jnp.exp(scores - jnp.max(scores, axis=0, keepdims=True))
    weights = (weights / jnp.sum(weights, axis=0, keepdims=True)).astype(jnp.bfloat16)
    return lax.dot_general(
        weights, value, (((0,), (0,)), ((), ())), preferred_element_type=jnp.float32
    )


def pack_kernel(
    place_ref, merge_ref, first_ref, up_third_ref, up_second_ref, out_third_ref, out_ref, sems
):
    core, column = place_ref[0], place_ref[1]
    high, low = jnp.right_shift(column, 1), jnp.bitwise_and(column, 1)

    def part(ref, row, lane, lanes=128, rows=16):
        return ref.at[pl.ds(pl.multiple_of(row, 16), rows), pl.ds(pl.multiple_of(lane, 128), lanes)]

    pairs = [
        (part(merge_ref, 0, core * 512, 512, 128), out_ref.at[:128, :512]),
        (first_ref, out_ref.at[128:, :512]),
    ]
    for tile in range(4):
        pairs.append(
            (
                part(up_third_ref, column * 16, core * 512 + tile * 128),
                out_ref.at[tile * 16 : tile * 16 + 16, 512:],
            )
        )
        pairs.append(
            (
                part(out_third_ref, high * 16, low * 1024 + core * 512 + tile * 128),
                out_ref.at[64 + tile * 16 : 80 + tile * 16, 512:],
            )
        )
    for row in (128, 144):
        pairs.append(
            (part(up_second_ref, high * 16, core * 256 + low * 128), out_ref.at[row : row + 16, 512:])
        )
    for copy in pull(sems, *pairs):
        copy.wait()


def first_kernel(x_ref, left_ref, right_ref, gain_ref, qkv_ref, window_ref, lat_ref, out_ref):
    steps = lat_ref.shape[0]
    own, side = x_ref.shape[0] // steps, left_ref.shape[0] // steps
    lane = lax.broadcasted_iota(jnp.int32, (own, 128), 1)
    key_lane = lax.broadcasted_iota(jnp.int32, (own + 2 * side, 128), 1)
    gain = gain_ref[...]
    for step in range(steps):
        rows = jnp.concatenate(
            [
                x_ref[step * own : (step + 1) * own, :],
                left_ref[step * side : (step + 1) * side, :],
                right_ref[step * side : (step + 1) * side, :],
            ],
            axis=0,
        )
        normed = norm_rows(rows.astype(jnp.float32), gain).astype(jnp.bfloat16)
        query = dot_rows(normed[:own], qkv_ref[0]).astype(jnp.bfloat16)
        query = (query * 0.125).astype(jnp.bfloat16)
        key = dot_rows(normed, qkv_ref[1]).astype(jnp.bfloat16)
        value = dot_rows(normed, qkv_ref[2]).astype(jnp.bfloat16)
        keep = window_ref[...] * lat_ref[step] > 0.0
        first = own // 2 if step == 0 else 0
        last = own // 2 if step == steps - 1 else own
        start = step * own - own // 2 + first
        for pair in range(query.shape[1] // 128):
            here = slice(pair * 128, pair * 128 + 128)
            parts = []
            for odd in range(2):
                picked = (key_lane < HD) if odd == 0 else (key_lane >= HD)
                key_side = jnp.where(picked, key[:, here], jnp.zeros_like(key[:, here]))
                parts.append(mix_tokens(query[:, here], key_side, value[:, here], keep))
            mixed = jnp.where(lane < HD, parts[0], parts[1]).astype(jnp.bfloat16)
            out_ref[start : start + last - first, here] = mixed[first:last]


def pick_matrix(lat_count, lon_count, lat_side, lon_side):
    shape = (2 * lat_count * lon_count, 8 * lat_count * lon_count)
    row = lax.broadcasted_iota(jnp.int32, shape, 0)
    column = lax.broadcasted_iota(jnp.int32, shape, 1)
    bits = lon_count.bit_length() - 1
    lon = row & (lon_count - 1)
    level = jnp.right_shift(row, bits) & 1
    lat = jnp.right_shift(row, bits + 1)
    source = ((2 * lat + lat_side) * 2 + level) * (2 * lon_count) + 2 * lon + lon_side
    return jnp.where(source == column, 1.0, 0.0).astype(jnp.bfloat16)


def join_quads(cells, lat_count, lon_count, gain_ref, out_ref):
    width = cells.shape[1]
    parts = [
        dot_rows(pick_matrix(lat_count, lon_count, lat_side, lon_side), cells)
        for lat_side in range(2)
        for lon_side in range(2)
    ]
    count = 1.0 / (4 * width)
    row_mean = sum(jnp.sum(part, axis=-1, keepdims=True) for part in parts) * count
    parts = [part - row_mean for part in parts]
    spread = sum(jnp.sum(part * part, axis=-1, keepdims=True) for part in parts) * count
    scale = lax.rsqrt(spread + 1e-05)
    for place, part in enumerate(parts):
        here = slice(place * width, place * width + width)
        out_ref[:, here] = (part * scale * gain_ref[:, here]).astype(jnp.bfloat16)


def skip_kernel(
    attended_ref, hidden_hbm, weights_hbm, gain_hbm, skip_ref, merged_ref,
    hidden_ref, weights_ref, gain_ref, sems,
):
    copies = pull(
        sems,
        (weights_hbm.at[:, :, 128:160, :512], weights_ref),
        (hidden_hbm, hidden_ref),
        (gain_hbm, gain_ref),
    )
    for copy in copies:
        copy.wait()
    total = None
    for ring in range(2):
        for z in range(0, 8, 4):
            right = jnp.concatenate(
                [weights_ref[ring, zz] for zz in range(z, z + 4)],
                axis=0,
            )
            start = (ring * 8 + z) * 32
            product = dot_rows(attended_ref[:, start : start + 128], right)
            total = product if total is None else total + product
    skip = (hidden_ref[...].astype(jnp.float32) + total).astype(jnp.bfloat16)
    skip_ref[...] = skip
    join_quads(skip, 6, 8, gain_ref, merged_ref)


def merge_kernel(own_ref, other_ref, weights_ref, own_out_ref, send_ref):
    left = jnp.concatenate([own_ref[...], other_ref[...]], axis=0)
    total = None
    for ring in range(2):
        for z in range(0, 8, 2):
            right = jnp.concatenate(
                [weights_ref[ring, zz * 160 : zz * 160 + 128, :512] for zz in (z, z + 1)], axis=0
            )
            start = (ring * 8 + z) * 128
            product = dot_rows(left[:, start : start + 256], right)
            total = product if total is None else total + product
    rows = own_ref.shape[0]
    own_out_ref[...] = total[:rows].astype(jnp.bfloat16)
    send_ref[...] = total[rows:].astype(jnp.bfloat16)


def join_kernel(core_ref, own_ref, recv_ref, gain_ref, second_ref, coarse_ref, halves_ref):
    core = core_ref[0]
    halves_ref[core] = own_ref[...]
    halves_ref[1 - core] = recv_ref[...]
    second = jnp.concatenate([halves_ref[0], halves_ref[1]], axis=1)
    second_ref[...] = second
    join_quads(second, 3, 4, gain_ref, coarse_ref)


RING_ORDER = (0, -1, 1, -2, 2, -3, 3)


def halves_in_order(core, mine_ref, partner_ref):
    mine, partner = mine_ref[...], partner_ref[...]
    first = core == 0
    return jnp.concatenate(
        [jnp.where(first, mine, partner), jnp.where(first, partner, mine)], axis=0
    )


def near_kernel(place_ref, *refs):
    near, (own_ref, *halves, out_ref) = refs[:7], refs[7:]
    left = jnp.concatenate([ref[...].astype(jnp.float32) for ref in near], axis=0)
    left = left.astype(jnp.bfloat16)
    rows = near[0].shape[0]
    own, other = own_ref[...], halves_in_order(place_ref[0], *halves)
    for weights, shard in ((own, place_ref[2]), (other, 1 - place_ref[2])):
        product = dot_rows(left, weights)
        for at in range(len(near)):
            out_ref[shard, at] = product[at * rows : (at + 1) * rows].astype(jnp.bfloat16)


def far_kernel(place_ref, near_ref, low_ref, high_ref, own_ref, mine_ref, partner_ref, out_ref):
    half = low_ref.shape[1]
    own, other = own_ref[...], halves_in_order(place_ref[0], mine_ref, partner_ref)
    for weights, shard in ((own, place_ref[2]), (other, 1 - place_ref[2])):
        far = dot_rows(low_ref[...], weights[:half]) + dot_rows(high_ref[...], weights[half:])
        out_ref[jnp.bitwise_and(place_ref[1] + 4, 7), shard] = far.astype(jnp.bfloat16)
    for shard in range(2):
        for at, offset in enumerate(RING_ORDER):
            place = jnp.bitwise_and(place_ref[1] + (offset + 8), 7)
            out_ref[place, shard] = near_ref[shard, at]


def third_kernel(
    place_ref, x_ref, gain_ref, own_hbm, mine_ref, partner_ref, out_ref, coarse_ref,
    normed_ref, own_ref, sems,
):
    (copy,) = pull(sems, (own_hbm, own_ref))
    blocks, places, shards, rows, width = x_ref.shape
    count = 1.0 / (blocks * shards * width)
    order = [(z, shard) for shard in range(shards) for z in range(blocks)]
    for first in range(0, places, 2):
        tiles = [
            jnp.concatenate(
                [x_ref[z, first + at, shard].astype(jnp.float32) for at in range(2)], axis=0
            )
            for z, shard in order
        ]
        row_mean = jnp.sum(sum(tiles), axis=-1, keepdims=True) * count
        tiles = [tile - row_mean for tile in tiles]
        spread = jnp.sum(sum(tile * tile for tile in tiles), axis=-1, keepdims=True)
        scale = lax.rsqrt(spread * count + 1e-05)
        for at, tile in enumerate(tiles):
            here = slice(at * width, (at + 1) * width)
            normed_ref[first * rows : (first + 2) * rows, here] = (
                tile * scale * gain_ref[:, here]
            ).astype(jnp.bfloat16)
    for at, (z, shard) in enumerate(order):
        coarse_ref[:, at * width : (at + 1) * width] = x_ref[z, place_ref[1], shard].astype(
            jnp.float32
        )
    query_token = lax.broadcasted_iota(jnp.int32, (96, 96), 0)
    key_token = lax.broadcasted_iota(jnp.int32, (96, 96), 1)
    keep = jnp.right_shift(query_token, 5) == jnp.right_shift(key_token, 5)
    ring = place_ref[2]
    other = halves_in_order(place_ref[0], mine_ref, partner_ref)
    copy.wait()
    for weights, shard in ((own_ref[...], ring), (other, 1 - ring)):
        triple = lax.dot_general(
            normed_ref[...],
            weights,
            (((1,), (1,)), ((), ())),
            preferred_element_type=jnp.float32,
        ).astype(jnp.bfloat16)
        query = (triple[:, :HD] * 0.125).astype(jnp.bfloat16)
        key = triple[:, HD : 2 * HD]
        value = triple[:, 2 * HD :]
        for group in range(places * rows // 96):
            mine = slice(group * 96, group * 96 + 96)
            mixed = mix_tokens(query[mine], key[mine], value[mine], keep)
            for at in range(96 // rows):
                out_ref[group * (96 // rows) + at, shard] = mixed[
                    at * rows : (at + 1) * rows
                ].astype(jnp.bfloat16)


def spread_matrix(lat_count, lon_count):
    fine = (2 * lat_count * lon_count, lat_count * lon_count // 2)
    row = lax.broadcasted_iota(jnp.int32, fine, 0)
    column = lax.broadcasted_iota(jnp.int32, fine, 1)
    bits = lon_count.bit_length() - 1
    lat = jnp.right_shift(row, bits + 2)
    level = jnp.right_shift(row, bits) & 1
    lon = jnp.right_shift(row & (lon_count - 1), 1)
    source = (lat * 2 + level) * (lon_count // 2) + lon
    return jnp.where(source == column, 1.0, 0.0).astype(jnp.bfloat16)


def spread_rows(values, lat_count, lon_count):
    matrix = spread_matrix(lat_count, lon_count)
    high = values.astype(jnp.bfloat16)
    rest = values - high.astype(jnp.float32)
    middle = rest.astype(jnp.bfloat16)
    low = (rest - middle.astype(jnp.float32)).astype(jnp.bfloat16)
    return dot_rows(matrix, high) + (dot_rows(matrix, middle) + dot_rows(matrix, low))


def late_tile(ref, column, ring, z, tile):
    return ref[((column * 2 + ring) * 8 + z) * 9 + tile]


def late_row(ref, column, ring, z, first):
    return jnp.concatenate([late_tile(ref, column, ring, z, first + at) for at in range(4)], axis=1)


def up_kernel(
    core_ref, heads_ref, own_coarse_ref, late_ref, swapped_ref, second_ref, skip_ref, out_ref,
    third_ref, lift_ref, level_ref, small_ref,
):
    core = core_ref[0]
    pairs = []
    for ring in range(2):
        for z in range(0, 8, 2):
            pairs.append(
                jnp.concatenate(
                    [heads_ref[z, ring].astype(jnp.float32), heads_ref[z + 1, ring].astype(jnp.float32)],
                    axis=1,
                ).astype(jnp.bfloat16)
            )
    for weights_ref, origin in ((swapped_ref, 1 - core), (late_ref, core)):
        for part in range(2):
            total = None
            for ring in range(2):
                for z in range(0, 8, 2):
                    right = jnp.concatenate(
                        [
                            late_row(weights_ref, 2 * row + part, ring, zz, 4)
                            for zz in (z, z + 1)
                            for row in range(4)
                        ],
                        axis=0,
                    )
                    product = dot_rows(pairs[ring * 4 + z // 2], right)
                    total = product if total is None else total + product
            third_ref[part, origin] = total
    level_three = []
    for place in range(16):
        here = slice(place * 128, place * 128 + 128)
        quarter = place // 4
        update = third_ref[quarter // 2, quarter % 2][:, place % 4 * 128 : place % 4 * 128 + 128]
        level_three.append((own_coarse_ref[:, here] + update).astype(jnp.bfloat16))
    for weights_ref, origin in ((late_ref, core), (swapped_ref, 1 - core)):
        total = None
        for ring in range(2):
            for z in range(8):
                right = jnp.concatenate(
                    [late_row(weights_ref, y, ring, z, 0) for y in range(8)],
                    axis=0,
                )
                product = dot_rows(level_three[ring * 8 + z], right)
                total = product if total is None else total + product
        lift_ref[origin] = total
    lat_count, lon_count = 6, 8
    for side in range(2):
        here = slice(side * 512, side * 512 + 512)
        level_ref[:, here] = (
            second_ref[:, here].astype(jnp.float32)
            + spread_rows(lift_ref[side], lat_count, lon_count)
        ).astype(jnp.bfloat16)
    for weights_ref, origin in ((late_ref, core), (swapped_ref, 1 - core)):
        total = None
        for ring in range(2):
            for z in range(0, 8, 2):
                right = jnp.concatenate(
                    [
                        jnp.concatenate(
                            [
                                late_tile(weights_ref, 2 * row + part, ring, zz, 8)
                                for zz in (z, z + 1)
                                for row in range(4)
                            ],
                            axis=0,
                        )
                        for part in range(2)
                    ],
                    axis=1,
                )
                start = (ring * 8 + z) * 64
                product = dot_rows(level_ref[:, start : start + 128], right)
                total = product if total is None else total + product
        small_ref[origin] = total
    for side in range(2):
        here = slice(side * 256, side * 256 + 256)
        out_ref[:, here] = (
            skip_ref[:, here].astype(jnp.float32)
            + spread_rows(small_ref[side], 2 * lat_count, 2 * lon_count)
        ).astype(jnp.bfloat16)


Z_RING = 8
RINGS = [[ring * Z_RING + place for place in range(Z_RING)] for ring in range(2)]


def neighbours(first, last, axis):
    count = lax.axis_size(axis)
    before = lax.ppermute(last, axis, [(i, (i + 1) % count) for i in range(count)])
    behind = lax.ppermute(first, axis, [((i + 1) % count, i) for i in range(count)])
    return before, behind


def swap_cores(values):
    count = lax.axis_size("lon")
    return lax.ppermute(values, "lon", [(i, i ^ 1) for i in range(count)])


def swap_rings(values):
    count = lax.axis_size("lat")
    return lax.ppermute(values, "lat", [(i, (i + Z_RING) % count) for i in range(count)])


def ring_scatter(blocks):
    return lax.all_to_all(blocks, "lat", 0, 0, axis_index_groups=RINGS, tiled=True)


def ring_shift(values, step):
    pairs = [(at, at // Z_RING * Z_RING + (at + step) % Z_RING) for at in range(2 * Z_RING)]
    return lax.ppermute(values, "lat", pairs)


def ring_gather(values):
    return ring_scatter(jnp.broadcast_to(values[None], (Z_RING,) + values.shape))


def in_order(flag, own, other, axis):
    return jnp.where(
        flag == 0,
        jnp.concatenate([own, other], axis=axis),
        jnp.concatenate([other, own], axis=axis),
    )


def after(values, *before):
    return lax.optimization_barrier((values,) + before)[0]


def on_device(
    fields,
    land_ids,
    surface_table,
    level_table,
    norm_first,
    qkv_first,
    out_first,
    norm_merge2,
    merge_second,
    norm_merge3,
    merge_third,
    norm_third,
    qkv_third,
    out_third,
    up_third,
    up_second,
):
    tile_rows, levels, tile_cols, feat_dim = fields.shape
    lat_count = lax.axis_size("lat")
    ring = lax.axis_index("lat") // Z_RING
    core = lax.axis_index("lon") % 2
    column = lax.axis_index("lon") // 4

    own_merge = call_kernel(
        pack_kernel,
        jax.ShapeDtypeStruct((160, 640), jnp.bfloat16),
        (
            jnp.stack([core, column]).astype(jnp.int32),
            merge_second,
            out_first,
            up_third,
            up_second,
            out_third,
        ),
        (pltpu.SemaphoreType.DMA((12,)),),
        pulled=(1, 2, 3, 4, 5),
        vmem_mib=62,
    )[None]
    both_merge = in_order(ring, own_merge, swap_rings(own_merge), 0)
    merge_weights = lax.all_gather(
        both_merge, "lat", axis=1, axis_index_groups=RINGS, tiled=True
    )
    core_place = jnp.stack([core, lax.axis_index("lat") % Z_RING, ring]).astype(jnp.int32)
    picks = (land_ids[:, :, None] == jnp.arange(3, dtype=jnp.int32)).astype(jnp.float32)
    surface = jnp.einsum("ijs,sc->ijc", picks, surface_table.astype(jnp.float32))
    hidden = (
        fields.astype(jnp.float32)
        + surface[:, None, :, :]
        + level_table.astype(jnp.float32)[None, :, None, :]
    ).astype(jnp.bfloat16)
    hidden = after(hidden, both_merge)
    above, below = neighbours(hidden[:2], hidden[-2:], "lat")
    cells = jnp.concatenate([above, hidden, below], axis=0)
    qkv_third = qkv_third.transpose(0, 2, 1).reshape(-1, qkv_third.shape[1])

    left, right = neighbours(cells[:, :, :2], cells[:, :, -2:], "lon")
    merge_third, qkv_third, left, right = lax.optimization_barrier(
        (merge_third, qkv_third, left, right)
    )

    merge_mine, qkv_mine = [
        swap_rings(lax.dynamic_slice_in_dim(table, core * (table.shape[0] // 2), table.shape[0] // 2))
        for table in (merge_third, qkv_third)
    ]

    ext_rows = tile_rows + 4
    own_window = (jnp.arange(32 * 4) % tile_cols + 2) // 4
    key_window = jnp.concatenate(
        [own_window, jnp.zeros((16,), jnp.int32), jnp.full((16,), tile_cols // 4, jnp.int32)]
    )
    same_window = (key_window[:, None] == own_window[None, :]).astype(jnp.float32)
    lat_place = lax.axis_index("lat") * tile_rows + jnp.arange(ext_rows) - 2
    valid_rows = ((lat_place >= 0) & (lat_place < tile_rows * lat_count)).astype(jnp.float32)
    valid_rows = valid_rows.reshape(ext_rows // 4, 4, 1)
    valid_keys = jnp.concatenate(
        [jnp.repeat(valid_rows, 2 * count, axis=1) for count in (tile_cols, 2, 2)], axis=1
    )
    attended = call_kernel(
        first_kernel,
        jax.ShapeDtypeStruct((tile_rows * levels * tile_cols, feat_dim), jnp.bfloat16),
        (
            cells.reshape(-1, feat_dim),
            left.reshape(-1, feat_dim),
            right.reshape(-1, feat_dim),
            norm_first[None],
            qkv_first,
            same_window,
            valid_keys,
        ),
        flops=2 * 640 * 512 * 1536,
    )
    attended = after(attended, merge_mine, qkv_mine)
    tokens = attended.shape[0]
    skip_first, merged_in = call_kernel(
        skip_kernel,
        (
            jax.ShapeDtypeStruct((tokens, feat_dim), jnp.bfloat16),
            jax.ShapeDtypeStruct((tokens // 4, 4 * feat_dim), jnp.bfloat16),
        ),
        (
            attended,
            hidden.reshape(-1, feat_dim),
            merge_weights.reshape(2, Z_RING, 160, 640),
            norm_merge2[None],
        ),
        (
            pltpu.VMEM((tokens, feat_dim), jnp.bfloat16),
            pltpu.VMEM((2, Z_RING, 32, 512), jnp.bfloat16),
            pltpu.VMEM((1, 4 * feat_dim), jnp.float32),
            pltpu.SemaphoreType.DMA((3,)),
        ),
        flops=2 * 384 * 512 * 512,
        pulled=(1, 2, 3),
        vmem_mib=58,
    )
    own_rows = merged_in.shape[0]
    half_shape = jax.ShapeDtypeStruct((own_rows, 512), jnp.bfloat16)
    second_half, second_send = call_kernel(
        merge_kernel,
        (half_shape, half_shape),
        (merged_in, swap_cores(merged_in), merge_weights),
        flops=2 * 192 * 2048 * 512,
    )
    late = after(merge_weights, second_send).reshape(2, Z_RING, 10, 16, 640)[:, :, :9, :, 512:]
    late = lax.all_gather(
        late.reshape(-1, 128),
        "lon",
        axis=0,
        axis_index_groups=[[4 * y + x for y in range(8)] for x in range(4)],
        tiled=True,
    ).reshape(-1, 16, 128)
    second_cells, coarse_in = call_kernel(
        join_kernel,
        (
            jax.ShapeDtypeStruct((own_rows, 1024), jnp.bfloat16),
            jax.ShapeDtypeStruct((own_rows // 4, 4096), jnp.bfloat16),
        ),
        (core_place, second_half, swap_cores(second_send), norm_merge3[None]),
        (pltpu.VMEM((2, own_rows, 512), jnp.bfloat16),),
        flops=2 * 96 * 96 * 1024,
    )
    own_count = coarse_in.shape[0]

    pieces, forth, back = [coarse_in], coarse_in, coarse_in
    for _ in range(3):
        forth, back = ring_shift(forth, 1), ring_shift(back, -1)
        pieces += [forth, back]
    merge_mine, qkv_mine = after(merge_mine, pieces[1]), after(qkv_mine, pieces[3])
    merge_partner, qkv_partner = swap_cores(merge_mine), swap_cores(qkv_mine)
    half_feats = coarse_in.shape[1] // 2
    forth, back = after(forth, merge_partner), after(back, qkv_partner)
    far_low, far_high = ring_shift(forth[:, :half_feats], 1), ring_shift(back[:, half_feats:], -1)
    tables = (merge_third, merge_mine, merge_partner)
    near = call_kernel(
        near_kernel,
        jax.ShapeDtypeStruct((2, len(RING_ORDER), own_count, 128), jnp.bfloat16),
        (core_place, *pieces, *tables),
        flops=2 * 168 * 4096 * 256,
    )
    column_block = call_kernel(
        far_kernel,
        jax.ShapeDtypeStruct((Z_RING, 2, own_count, 128), jnp.bfloat16),
        (core_place, near, far_low, far_high, *tables),
        flops=2 * 24 * 4096 * 256,
    )
    heads_out, own_coarse = call_kernel(
        third_kernel,
        (
            jax.ShapeDtypeStruct((Z_RING, 2, own_count, HD), jnp.bfloat16),
            jax.ShapeDtypeStruct((own_count, 2048), jnp.float32),
        ),
        (core_place, ring_gather(column_block), norm_third[None], qkv_third, qkv_mine, qkv_partner),
        (
            pltpu.VMEM((Z_RING * own_count, 2048), jnp.bfloat16),
            pltpu.VMEM(qkv_third.shape, jnp.bfloat16),
            pltpu.SemaphoreType.DMA((1,)),
        ),
        flops=2 * 192 * 2048 * 384,
        pulled=(3,),
    )

    late_swapped = swap_cores(after(late, heads_out))
    decoded = call_kernel(
        up_kernel,
        jax.ShapeDtypeStruct((tile_rows * levels * tile_cols, feat_dim), jnp.bfloat16),
        (
            core_place,
            ring_scatter(heads_out),
            own_coarse,
            late,
            late_swapped,
            second_cells,
            skip_first,
        ),
        (
            pltpu.VMEM((2, 2, own_count, 512), jnp.float32),
            pltpu.VMEM((2, own_count, 512), jnp.float32),
            pltpu.VMEM((second_cells.shape[0], 1024), jnp.bfloat16),
            pltpu.VMEM((2, second_cells.shape[0], 256), jnp.float32),
        ),
        flops=2 * (24 * 1024 * 2048 + 24 * 2048 * 1024 + 96 * 1024 * 512),
    )
    return decoded.reshape(fields.shape)


def solution(mesh):
    in_specs = (
        P("lat", None, "lon", None),
        P("lat", "lon"),
        P(),
        P(),
        P(),
        P(),
        P("lat", None),
        P(),
        P("lat", None),
        P(),
        P(None, "lat"),
        P(),
        P(None, None, "lat"),
        P("lat", None),
        P("lat", None),
        P("lat", None),
    )
    out_specs = P("lat", None, "lon", None)
    return jax.shard_map(
        on_device, mesh=mesh, in_specs=in_specs, out_specs=out_specs, check_vma=False
    )
```

```python
import jax
import jax.numpy as jnp
from jax import lax
from jax.experimental import pallas as pl
from jax.experimental.pallas import tpu as pltpu
from jax.sharding import PartitionSpec as P

HD = 64


def norm_rows(values, gain):
    row_mean = jnp.mean(values, axis=-1, keepdims=True)
    centred = values - row_mean
    spread = jnp.mean(centred * centred, axis=-1, keepdims=True)
    return centred * lax.rsqrt(spread + 1e-05) * gain


def call_kernel(body, out_shape, operands, scratch=(), flops=0, pulled=(), vmem_mib=48):
    spaces = [
        pltpu.SMEM if operand.dtype == jnp.int32 else pltpu.HBM if at in pulled else pltpu.VMEM
        for at, operand in enumerate(operands)
    ]
    return pl.pallas_call(
        body,
        out_shape=out_shape,
        in_specs=[pl.BlockSpec(memory_space=space) for space in spaces],
        out_specs=jax.tree.map(lambda _: pl.BlockSpec(memory_space=pltpu.VMEM), out_shape),
        scratch_shapes=list(scratch),
        compiler_params=pltpu.CompilerParams(vmem_limit_bytes=vmem_mib * 1024 * 1024),
        cost_estimate=pl.CostEstimate(
            flops=flops,
            bytes_accessed=sum(operand.size * operand.dtype.itemsize for operand in operands),
            transcendentals=0,
        ),
    )(*operands)


def pull(sems, *pairs):
    copies = [pltpu.make_async_copy(src, dst, sems.at[at]) for at, (src, dst) in enumerate(pairs)]
    for copy in copies:
        copy.start()
    return copies


def dot_rows(left, right):
    return lax.dot_general(left, right, (((1,), (0,)), ((), ())), preferred_element_type=jnp.float32)


def mix_tokens(query, key, value, keep):
    scores = lax.dot_general(
        key, query, (((1,), (1,)), ((), ())), preferred_element_type=jnp.float32
    )
    scores = jnp.where(keep, scores, -1e30)
    weights = jnp.exp(scores - jnp.max(scores, axis=0, keepdims=True))
    weights = (weights / jnp.sum(weights, axis=0, keepdims=True)).astype(jnp.bfloat16)
    return lax.dot_general(
        weights, value, (((0,), (0,)), ((), ())), preferred_element_type=jnp.float32
    )


def pack_kernel(
    place_ref, merge_ref, first_ref, up_third_ref, up_second_ref, out_third_ref, out_ref, sems
):
    core, column = place_ref[0], place_ref[1]
    high, low = jnp.right_shift(column, 1), jnp.bitwise_and(column, 1)

    def part(ref, row, lane, lanes=128, rows=16):
        return ref.at[pl.ds(pl.multiple_of(row, 16), rows), pl.ds(pl.multiple_of(lane, 128), lanes)]

    pairs = [
        (part(merge_ref, 0, core * 512, 512, 128), out_ref.at[:128, :512]),
        (first_ref, out_ref.at[128:, :512]),
    ]
    for tile in range(4):
        pairs.append(
            (
                part(up_third_ref, column * 16, core * 512 + tile * 128),
                out_ref.at[tile * 16 : tile * 16 + 16, 512:],
            )
        )
        pairs.append(
            (
                part(out_third_ref, high * 16, low * 1024 + core * 512 + tile * 128),
                out_ref.at[64 + tile * 16 : 80 + tile * 16, 512:],
            )
        )
    for row in (128, 144):
        pairs.append(
            (part(up_second_ref, high * 16, core * 256 + low * 128), out_ref.at[row : row + 16, 512:])
        )
    for copy in pull(sems, *pairs):
        copy.wait()


def first_kernel(x_ref, left_ref, right_ref, gain_ref, qkv_ref, window_ref, lat_ref, out_ref):
    steps = lat_ref.shape[0]
    own, side = x_ref.shape[0] // steps, left_ref.shape[0] // steps
    lane = lax.broadcasted_iota(jnp.int32, (own, 128), 1)
    key_lane = lax.broadcasted_iota(jnp.int32, (own + 2 * side, 128), 1)
    gain = gain_ref[...]
    for step in range(steps):
        rows = jnp.concatenate(
            [
                x_ref[step * own : (step + 1) * own, :],
                left_ref[step * side : (step + 1) * side, :],
                right_ref[step * side : (step + 1) * side, :],
            ],
            axis=0,
        )
        normed = norm_rows(rows.astype(jnp.float32), gain).astype(jnp.bfloat16)
        query = dot_rows(normed[:own], qkv_ref[0]).astype(jnp.bfloat16)
        query = (query * 0.125).astype(jnp.bfloat16)
        key = dot_rows(normed, qkv_ref[1]).astype(jnp.bfloat16)
        value = dot_rows(normed, qkv_ref[2]).astype(jnp.bfloat16)
        keep = window_ref[...] * lat_ref[step] > 0.0
        first = own // 2 if step == 0 else 0
        last = own // 2 if step == steps - 1 else own
        start = step * own - own // 2 + first
        for pair in range(query.shape[1] // 128):
            here = slice(pair * 128, pair * 128 + 128)
            parts = []
            for odd in range(2):
                picked = (key_lane < HD) if odd == 0 else (key_lane >= HD)
                key_side = jnp.where(picked, key[:, here], jnp.zeros_like(key[:, here]))
                parts.append(mix_tokens(query[:, here], key_side, value[:, here], keep))
            mixed = jnp.where(lane < HD, parts[0], parts[1]).astype(jnp.bfloat16)
            out_ref[start : start + last - first, here] = mixed[first:last]


def pick_matrix(lat_count, lon_count, lat_side, lon_side):
    shape = (2 * lat_count * lon_count, 8 * lat_count * lon_count)
    row = lax.broadcasted_iota(jnp.int32, shape, 0)
    column = lax.broadcasted_iota(jnp.int32, shape, 1)
    bits = lon_count.bit_length() - 1
    lon = row & (lon_count - 1)
    level = jnp.right_shift(row, bits) & 1
    lat = jnp.right_shift(row, bits + 1)
    source = ((2 * lat + lat_side) * 2 + level) * (2 * lon_count) + 2 * lon + lon_side
    return jnp.where(source == column, 1.0, 0.0).astype(jnp.bfloat16)


def join_quads(cells, lat_count, lon_count, gain_ref, out_ref):
    width = cells.shape[1]
    parts = [
        dot_rows(pick_matrix(lat_count, lon_count, lat_side, lon_side), cells)
        for lat_side in range(2)
        for lon_side in range(2)
    ]
    count = 1.0 / (4 * width)
    row_mean = sum(jnp.sum(part, axis=-1, keepdims=True) for part in parts) * count
    parts = [part - row_mean for part in parts]
    spread = sum(jnp.sum(part * part, axis=-1, keepdims=True) for part in parts) * count
    scale = lax.rsqrt(spread + 1e-05)
    for place, part in enumerate(parts):
        here = slice(place * width, place * width + width)
        out_ref[:, here] = (part * scale * gain_ref[:, here]).astype(jnp.bfloat16)


def skip_kernel(
    attended_ref, hidden_hbm, weights_hbm, gain_hbm, skip_ref, merged_ref,
    hidden_ref, weights_ref, gain_ref, sems,
):
    copies = pull(
        sems,
        (weights_hbm.at[:, :, 128:160, :512], weights_ref),
        (hidden_hbm, hidden_ref),
        (gain_hbm, gain_ref),
    )
    for copy in copies:
        copy.wait()
    total = None
    for ring in range(2):
        for z in range(0, 8, 4):
            right = jnp.concatenate(
                [weights_ref[ring, zz] for zz in range(z, z + 4)],
                axis=0,
            )
            start = (ring * 8 + z) * 32
            product = dot_rows(attended_ref[:, start : start + 128], right)
            total = product if total is None else total + product
    skip = (hidden_ref[...].astype(jnp.float32) + total).astype(jnp.bfloat16)
    skip_ref[...] = skip
    join_quads(skip, 6, 8, gain_ref, merged_ref)


def merge_kernel(own_ref, other_ref, weights_ref, own_out_ref, send_ref):
    left = jnp.concatenate([own_ref[...], other_ref[...]], axis=0)
    total = None
    for ring in range(2):
        for z in range(0, 8, 2):
            right = jnp.concatenate(
                [weights_ref[ring, zz * 160 : zz * 160 + 128, :512] for zz in (z, z + 1)], axis=0
            )
            start = (ring * 8 + z) * 128
            product = dot_rows(left[:, start : start + 256], right)
            total = product if total is None else total + product
    rows = own_ref.shape[0]
    own_out_ref[...] = total[:rows].astype(jnp.bfloat16)
    send_ref[...] = total[rows:].astype(jnp.bfloat16)


def join_kernel(core_ref, own_ref, recv_ref, gain_ref, second_ref, coarse_ref, halves_ref):
    core = core_ref[0]
    halves_ref[core] = own_ref[...]
    halves_ref[1 - core] = recv_ref[...]
    second = jnp.concatenate([halves_ref[0], halves_ref[1]], axis=1)
    second_ref[...] = second
    join_quads(second, 3, 4, gain_ref, coarse_ref)


NEAR_PLACES, FAR_PLACES = (0, -1, 1, -2, 2, 4), (-3, 3)


def halves_in_order(core, mine_ref, partner_ref):
    mine, partner = mine_ref[...], partner_ref[...]
    first = core == 0
    return jnp.concatenate(
        [jnp.where(first, mine, partner), jnp.where(first, partner, mine)], axis=0
    )


def near_kernel(place_ref, *refs):
    near, (own_ref, *halves, out_ref) = refs[:6], refs[6:]
    left = jnp.concatenate([ref[...].astype(jnp.float32) for ref in near], axis=0)
    left = left.astype(jnp.bfloat16)
    rows = near[0].shape[0]
    own, other = own_ref[...], halves_in_order(place_ref[0], *halves)
    for weights, shard in ((own, place_ref[2]), (other, 1 - place_ref[2])):
        product = dot_rows(left, weights)
        for at in range(len(near)):
            out_ref[shard, at] = product[at * rows : (at + 1) * rows].astype(jnp.bfloat16)


def far_kernel(place_ref, near_ref, back_ref, forth_ref, own_ref, mine_ref, partner_ref, out_ref):
    rows = back_ref.shape[0]
    left = jnp.concatenate([back_ref[...].astype(jnp.float32), forth_ref[...].astype(jnp.float32)], axis=0)
    left = left.astype(jnp.bfloat16)
    own, other = own_ref[...], halves_in_order(place_ref[0], mine_ref, partner_ref)
    for weights, shard in ((own, place_ref[2]), (other, 1 - place_ref[2])):
        far = dot_rows(left, weights)
        for at, offset in enumerate(FAR_PLACES):
            place = jnp.bitwise_and(place_ref[1] + (offset + 8), 7)
            out_ref[place, shard] = far[at * rows : (at + 1) * rows].astype(jnp.bfloat16)
    for shard in range(2):
        for at, offset in enumerate(NEAR_PLACES):
            place = jnp.bitwise_and(place_ref[1] + (offset + 8), 7)
            out_ref[place, shard] = near_ref[shard, at]


def third_kernel(
    place_ref, x_ref, gain_ref, own_hbm, mine_ref, partner_ref, out_ref, coarse_ref,
    normed_ref, own_ref, sems,
):
    (copy,) = pull(sems, (own_hbm, own_ref))
    blocks, places, shards, rows, width = x_ref.shape
    count = 1.0 / (blocks * shards * width)
    order = [(z, shard) for shard in range(shards) for z in range(blocks)]
    for first in range(0, places, 2):
        tiles = [
            jnp.concatenate(
                [x_ref[z, first + at, shard].astype(jnp.float32) for at in range(2)], axis=0
            )
            for z, shard in order
        ]
        row_mean = jnp.sum(sum(tiles), axis=-1, keepdims=True) * count
        tiles = [tile - row_mean for tile in tiles]
        spread = jnp.sum(sum(tile * tile for tile in tiles), axis=-1, keepdims=True)
        scale = lax.rsqrt(spread * count + 1e-05)
        for at, tile in enumerate(tiles):
            here = slice(at * width, (at + 1) * width)
            normed_ref[first * rows : (first + 2) * rows, here] = (
                tile * scale * gain_ref[:, here]
            ).astype(jnp.bfloat16)
    for at, (z, shard) in enumerate(order):
        coarse_ref[:, at * width : (at + 1) * width] = x_ref[z, place_ref[1], shard].astype(
            jnp.float32
        )
    query_token = lax.broadcasted_iota(jnp.int32, (96, 96), 0)
    key_token = lax.broadcasted_iota(jnp.int32, (96, 96), 1)
    keep = jnp.right_shift(query_token, 5) == jnp.right_shift(key_token, 5)
    ring = place_ref[2]
    other = halves_in_order(place_ref[0], mine_ref, partner_ref)
    copy.wait()
    for weights, shard in ((own_ref[...], ring), (other, 1 - ring)):
        triple = lax.dot_general(
            normed_ref[...],
            weights,
            (((1,), (1,)), ((), ())),
            preferred_element_type=jnp.float32,
        ).astype(jnp.bfloat16)
        query = (triple[:, :HD] * 0.125).astype(jnp.bfloat16)
        key = triple[:, HD : 2 * HD]
        value = triple[:, 2 * HD :]
        for group in range(places * rows // 96):
            mine = slice(group * 96, group * 96 + 96)
            mixed = mix_tokens(query[mine], key[mine], value[mine], keep)
            for at in range(96 // rows):
                out_ref[group * (96 // rows) + at, shard] = mixed[
                    at * rows : (at + 1) * rows
                ].astype(jnp.bfloat16)


def spread_matrix(lat_count, lon_count):
    fine = (2 * lat_count * lon_count, lat_count * lon_count // 2)
    row = lax.broadcasted_iota(jnp.int32, fine, 0)
    column = lax.broadcasted_iota(jnp.int32, fine, 1)
    bits = lon_count.bit_length() - 1
    lat = jnp.right_shift(row, bits + 2)
    level = jnp.right_shift(row, bits) & 1
    lon = jnp.right_shift(row & (lon_count - 1), 1)
    source = (lat * 2 + level) * (lon_count // 2) + lon
    return jnp.where(source == column, 1.0, 0.0).astype(jnp.bfloat16)


def spread_rows(values, lat_count, lon_count):
    matrix = spread_matrix(lat_count, lon_count)
    high = values.astype(jnp.bfloat16)
    rest = values - high.astype(jnp.float32)
    middle = rest.astype(jnp.bfloat16)
    low = (rest - middle.astype(jnp.float32)).astype(jnp.bfloat16)
    return dot_rows(matrix, high) + (dot_rows(matrix, middle) + dot_rows(matrix, low))


def late_tile(ref, column, ring, z, tile):
    return ref[((column * 2 + ring) * 8 + z) * 9 + tile]


def late_row(ref, column, ring, z, first):
    return jnp.concatenate([late_tile(ref, column, ring, z, first + at) for at in range(4)], axis=1)


def up_kernel(
    core_ref, heads_ref, own_coarse_ref, late_ref, swapped_ref, second_ref, skip_ref, out_ref,
    third_ref, lift_ref, level_ref, small_ref,
):
    core = core_ref[0]
    pairs = []
    for ring in range(2):
        for z in range(0, 8, 4):
            pairs.append(
                jnp.concatenate(
                    [heads_ref[zz, ring].astype(jnp.float32) for zz in range(z, z + 4)], axis=1
                ).astype(jnp.bfloat16)
            )
    for weights_ref, origin in ((swapped_ref, 1 - core), (late_ref, core)):
        for part in range(2):
            total = None
            for ring in range(2):
                for z in range(0, 8, 4):
                    right = jnp.concatenate(
                        [
                            late_row(weights_ref, 2 * row + part, ring, zz, 4)
                            for zz in range(z, z + 4)
                            for row in range(4)
                        ],
                        axis=0,
                    )
                    product = dot_rows(pairs[ring * 2 + z // 4], right)
                    total = product if total is None else total + product
            third_ref[part, origin] = total
    level_three = []
    for place in range(16):
        here = slice(place * 128, place * 128 + 128)
        quarter = place // 4
        update = third_ref[quarter // 2, quarter % 2][:, place % 4 * 128 : place % 4 * 128 + 128]
        level_three.append((own_coarse_ref[:, here] + update).astype(jnp.bfloat16))
    for weights_ref, origin in ((late_ref, core), (swapped_ref, 1 - core)):
        total = None
        for ring in range(2):
            for z in range(0, 8, 2):
                right = jnp.concatenate(
                    [late_row(weights_ref, y, ring, zz, 0) for zz in (z, z + 1) for y in range(8)],
                    axis=0,
                )
                start = ring * 8 + z
                left = jnp.concatenate(level_three[start : start + 2], axis=1)
                product = dot_rows(left, right)
                total = product if total is None else total + product
        lift_ref[origin] = total
    lat_count, lon_count = 6, 8
    for side in range(2):
        here = slice(side * 512, side * 512 + 512)
        level_ref[:, here] = (
            second_ref[:, here].astype(jnp.float32)
            + spread_rows(lift_ref[side], lat_count, lon_count)
        ).astype(jnp.bfloat16)
    for weights_ref, origin in ((late_ref, core), (swapped_ref, 1 - core)):
        total = None
        for ring in range(2):
            for z in range(0, 8, 4):
                right = jnp.concatenate(
                    [
                        jnp.concatenate(
                            [
                                late_tile(weights_ref, 2 * row + part, ring, zz, 8)
                                for zz in range(z, z + 4)
                                for row in range(4)
                            ],
                            axis=0,
                        )
                        for part in range(2)
                    ],
                    axis=1,
                )
                start = (ring * 8 + z) * 64
                product = dot_rows(level_ref[:, start : start + 256], right)
                total = product if total is None else total + product
        small_ref[origin] = total
    for side in range(2):
        here = slice(side * 256, side * 256 + 256)
        out_ref[:, here] = (
            skip_ref[:, here].astype(jnp.float32)
            + spread_rows(small_ref[side], 2 * lat_count, 2 * lon_count)
        ).astype(jnp.bfloat16)


Z_RING = 8
RINGS = [[ring * Z_RING + place for place in range(Z_RING)] for ring in range(2)]


def neighbours(first, last, axis):
    count = lax.axis_size(axis)
    before = lax.ppermute(last, axis, [(i, (i + 1) % count) for i in range(count)])
    behind = lax.ppermute(first, axis, [((i + 1) % count, i) for i in range(count)])
    return before, behind


def swap_cores(values):
    count = lax.axis_size("lon")
    return lax.ppermute(values, "lon", [(i, i ^ 1) for i in range(count)])


def swap_rings(values):
    count = lax.axis_size("lat")
    return lax.ppermute(values, "lat", [(i, (i + Z_RING) % count) for i in range(count)])


def ring_scatter(blocks):
    return lax.all_to_all(blocks, "lat", 0, 0, axis_index_groups=RINGS, tiled=True)


def ring_shift(values, step):
    pairs = [(at, at // Z_RING * Z_RING + (at + step) % Z_RING) for at in range(2 * Z_RING)]
    return lax.ppermute(values, "lat", pairs)


def ring_gather(values):
    return ring_scatter(jnp.broadcast_to(values[None], (Z_RING,) + values.shape))


def in_order(flag, own, other, axis):
    return jnp.where(
        flag == 0,
        jnp.concatenate([own, other], axis=axis),
        jnp.concatenate([other, own], axis=axis),
    )


def after(values, *before):
    return lax.optimization_barrier((values,) + before)[0]


def on_device(
    fields,
    land_ids,
    surface_table,
    level_table,
    norm_first,
    qkv_first,
    out_first,
    norm_merge2,
    merge_second,
    norm_merge3,
    merge_third,
    norm_third,
    qkv_third,
    out_third,
    up_third,
    up_second,
):
    tile_rows, levels, tile_cols, feat_dim = fields.shape
    lat_count = lax.axis_size("lat")
    ring = lax.axis_index("lat") // Z_RING
    core = lax.axis_index("lon") % 2
    column = lax.axis_index("lon") // 4

    own_merge = call_kernel(
        pack_kernel,
        jax.ShapeDtypeStruct((160, 640), jnp.bfloat16),
        (
            jnp.stack([core, column]).astype(jnp.int32),
            merge_second,
            out_first,
            up_third,
            up_second,
            out_third,
        ),
        (pltpu.SemaphoreType.DMA((12,)),),
        pulled=(1, 2, 3, 4, 5),
        vmem_mib=62,
    )
    both_merge = lax.all_gather(
        own_merge, "lat", axis_index_groups=[[z, z + Z_RING] for z in range(Z_RING)]
    )
    merge_weights = lax.all_gather(
        both_merge, "lat", axis=1, axis_index_groups=RINGS, tiled=True
    )
    core_place = jnp.stack([core, lax.axis_index("lat") % Z_RING, ring]).astype(jnp.int32)
    picks = (land_ids[:, :, None] == jnp.arange(3, dtype=jnp.int32)).astype(jnp.float32)
    surface = jnp.einsum("ijs,sc->ijc", picks, surface_table.astype(jnp.float32))
    hidden = (
        fields.astype(jnp.float32)
        + surface[:, None, :, :]
        + level_table.astype(jnp.float32)[None, :, None, :]
    ).astype(jnp.bfloat16)
    hidden = after(hidden, both_merge)
    above, below = neighbours(hidden[:2], hidden[-2:], "lat")
    cells = jnp.concatenate([above, hidden, below], axis=0)
    qkv_third = qkv_third.transpose(0, 2, 1).reshape(-1, qkv_third.shape[1])

    merge_third, cells = lax.optimization_barrier((merge_third, cells))
    left, right = neighbours(cells[:, :, :2], cells[:, :, -2:], "lon")
    qkv_third, left, right = lax.optimization_barrier((qkv_third, left, right))

    merge_mine, qkv_mine = [
        swap_rings(lax.dynamic_slice_in_dim(table, core * (table.shape[0] // 2), table.shape[0] // 2))
        for table in (merge_third, qkv_third)
    ]

    ext_rows = tile_rows + 4
    own_window = (jnp.arange(32 * 4) % tile_cols + 2) // 4
    key_window = jnp.concatenate(
        [own_window, jnp.zeros((16,), jnp.int32), jnp.full((16,), tile_cols // 4, jnp.int32)]
    )
    same_window = (key_window[:, None] == own_window[None, :]).astype(jnp.float32)
    lat_place = lax.axis_index("lat") * tile_rows + jnp.arange(ext_rows) - 2
    valid_rows = ((lat_place >= 0) & (lat_place < tile_rows * lat_count)).astype(jnp.float32)
    valid_rows = valid_rows.reshape(ext_rows // 4, 4, 1)
    valid_keys = jnp.concatenate(
        [jnp.repeat(valid_rows, 2 * count, axis=1) for count in (tile_cols, 2, 2)], axis=1
    )
    attended = call_kernel(
        first_kernel,
        jax.ShapeDtypeStruct((tile_rows * levels * tile_cols, feat_dim), jnp.bfloat16),
        (
            cells.reshape(-1, feat_dim),
            left.reshape(-1, feat_dim),
            right.reshape(-1, feat_dim),
            norm_first[None],
            qkv_first,
            same_window,
            valid_keys,
        ),
        flops=2 * 640 * 512 * 1536,
    )
    attended = after(attended, merge_mine, qkv_mine)
    tokens = attended.shape[0]
    skip_first, merged_in = call_kernel(
        skip_kernel,
        (
            jax.ShapeDtypeStruct((tokens, feat_dim), jnp.bfloat16),
            jax.ShapeDtypeStruct((tokens // 4, 4 * feat_dim), jnp.bfloat16),
        ),
        (
            attended,
            hidden.reshape(-1, feat_dim),
            merge_weights.reshape(2, Z_RING, 160, 640),
            norm_merge2[None],
        ),
        (
            pltpu.VMEM((tokens, feat_dim), jnp.bfloat16),
            pltpu.VMEM((2, Z_RING, 32, 512), jnp.bfloat16),
            pltpu.VMEM((1, 4 * feat_dim), jnp.float32),
            pltpu.SemaphoreType.DMA((3,)),
        ),
        flops=2 * 384 * 512 * 512,
        pulled=(1, 2, 3),
        vmem_mib=58,
    )
    own_rows = merged_in.shape[0]
    half_shape = jax.ShapeDtypeStruct((own_rows, 512), jnp.bfloat16)
    second_half, second_send = call_kernel(
        merge_kernel,
        (half_shape, half_shape),
        (merged_in, swap_cores(merged_in), merge_weights),
        flops=2 * 192 * 2048 * 512,
    )
    late = after(merge_weights, second_send).reshape(2, Z_RING, 10, 16, 640)[:, :, :9, :, 512:]
    late = lax.all_gather(
        late.reshape(-1, 128),
        "lon",
        axis=0,
        axis_index_groups=[[4 * y + x for y in range(8)] for x in range(4)],
        tiled=True,
    ).reshape(-1, 16, 128)
    second_cells, coarse_in = call_kernel(
        join_kernel,
        (
            jax.ShapeDtypeStruct((own_rows, 1024), jnp.bfloat16),
            jax.ShapeDtypeStruct((own_rows // 4, 4096), jnp.bfloat16),
        ),
        (core_place, second_half, swap_cores(second_send), norm_merge3[None]),
        (pltpu.VMEM((2, own_rows, 512), jnp.bfloat16),),
        flops=2 * 96 * 96 * 1024,
    )
    own_count = coarse_in.shape[0]

    pieces, forth, back = [coarse_in], coarse_in, coarse_in
    opposite = None
    for _ in range(2):
        forth, back = ring_shift(forth, 1), ring_shift(back, -1)
        opposite = ring_shift(coarse_in, 4) if opposite is None else opposite
        pieces += [forth, back]
    merge_mine = after(merge_mine, pieces[1], pieces[2])
    qkv_mine = after(qkv_mine, pieces[3])
    merge_partner, qkv_partner = swap_cores(merge_mine), swap_cores(qkv_mine)
    back, merge_partner = lax.optimization_barrier((back, merge_partner))
    pieces.append(opposite)
    far_back, far_forth = ring_shift(forth, 1), ring_shift(back, -1)
    tables = (merge_third, merge_mine, merge_partner)
    near = call_kernel(
        near_kernel,
        jax.ShapeDtypeStruct((2, len(pieces), own_count, 128), jnp.bfloat16),
        (core_place, *pieces, *tables),
        flops=2 * 144 * 4096 * 256,
    )
    column_block = call_kernel(
        far_kernel,
        jax.ShapeDtypeStruct((Z_RING, 2, own_count, 128), jnp.bfloat16),
        (core_place, near, far_back, far_forth, *tables),
        flops=2 * 48 * 4096 * 256,
    )
    column_block = after(column_block, qkv_partner)
    heads_out, own_coarse = call_kernel(
        third_kernel,
        (
            jax.ShapeDtypeStruct((Z_RING, 2, own_count, HD), jnp.bfloat16),
            jax.ShapeDtypeStruct((own_count, 2048), jnp.float32),
        ),
        (core_place, ring_gather(column_block), norm_third[None], qkv_third, qkv_mine, qkv_partner),
        (
            pltpu.VMEM((Z_RING * own_count, 2048), jnp.bfloat16),
            pltpu.VMEM(qkv_third.shape, jnp.bfloat16),
            pltpu.SemaphoreType.DMA((1,)),
        ),
        flops=2 * 192 * 2048 * 384,
        pulled=(3,),
    )

    late_swapped = swap_cores(after(late, heads_out))
    decoded = call_kernel(
        up_kernel,
        jax.ShapeDtypeStruct((tile_rows * levels * tile_cols, feat_dim), jnp.bfloat16),
        (
            core_place,
            ring_scatter(heads_out),
            own_coarse,
            late,
            late_swapped,
            second_cells,
            skip_first,
        ),
        (
            pltpu.VMEM((2, 2, own_count, 512), jnp.float32),
            pltpu.VMEM((2, own_count, 512), jnp.float32),
            pltpu.VMEM((second_cells.shape[0], 1024), jnp.bfloat16),
            pltpu.VMEM((2, second_cells.shape[0], 256), jnp.float32),
        ),
        flops=2 * (24 * 1024 * 2048 + 24 * 2048 * 1024 + 96 * 1024 * 512),
    )
    return decoded.reshape(fields.shape)


def solution(mesh):
    in_specs = (
        P("lat", None, "lon", None),
        P("lat", "lon"),
        P(),
        P(),
        P(),
        P(),
        P("lat", None),
        P(),
        P("lat", None),
        P(),
        P(None, "lat"),
        P(),
        P(None, None, "lat"),
        P("lat", None),
        P("lat", None),
        P("lat", None),
    )
    out_specs = P("lat", None, "lon", None)
    return jax.shard_map(
        on_device, mesh=mesh, in_specs=in_specs, out_specs=out_specs, check_vma=False
    )
```

```python
import jax
import jax.numpy as jnp
from jax import lax
from jax.experimental import pallas as pl
from jax.experimental.pallas import tpu as pltpu
from jax.sharding import PartitionSpec as P

HD = 64


def norm_rows(values, gain):
    row_mean = jnp.mean(values, axis=-1, keepdims=True)
    centred = values - row_mean
    spread = jnp.mean(centred * centred, axis=-1, keepdims=True)
    return centred * lax.rsqrt(spread + 1e-05) * gain


def call_kernel(body, out_shape, operands, scratch=(), flops=0, pulled=(), vmem_mib=48):
    spaces = [
        pltpu.SMEM if operand.dtype == jnp.int32 else pltpu.HBM if at in pulled else pltpu.VMEM
        for at, operand in enumerate(operands)
    ]
    return pl.pallas_call(
        body,
        out_shape=out_shape,
        in_specs=[pl.BlockSpec(memory_space=space) for space in spaces],
        out_specs=jax.tree.map(lambda _: pl.BlockSpec(memory_space=pltpu.VMEM), out_shape),
        scratch_shapes=list(scratch),
        compiler_params=pltpu.CompilerParams(vmem_limit_bytes=vmem_mib * 1024 * 1024),
        cost_estimate=pl.CostEstimate(
            flops=flops,
            bytes_accessed=sum(operand.size * operand.dtype.itemsize for operand in operands),
            transcendentals=0,
        ),
    )(*operands)


def pull(sems, *pairs):
    copies = [pltpu.make_async_copy(src, dst, sems.at[at]) for at, (src, dst) in enumerate(pairs)]
    for copy in copies:
        copy.start()
    return copies


def dot_rows(left, right):
    return lax.dot_general(left, right, (((1,), (0,)), ((), ())), preferred_element_type=jnp.float32)


def mix_tokens(query, key, value, keep):
    scores = lax.dot_general(
        key, query, (((1,), (1,)), ((), ())), preferred_element_type=jnp.float32
    )
    scores = jnp.where(keep, scores, -1e30)
    weights = jnp.exp(scores - jnp.max(scores, axis=0, keepdims=True))
    weights = (weights / jnp.sum(weights, axis=0, keepdims=True)).astype(jnp.bfloat16)
    return lax.dot_general(
        weights, value, (((0,), (0,)), ((), ())), preferred_element_type=jnp.float32
    )


def pack_kernel(
    place_ref, merge_ref, first_ref, up_third_ref, up_second_ref, out_third_ref, out_ref, sems
):
    core, column = place_ref[0], place_ref[1]
    high, low = jnp.right_shift(column, 1), jnp.bitwise_and(column, 1)

    def part(ref, row, lane, lanes=128, rows=16):
        return ref.at[pl.ds(pl.multiple_of(row, 16), rows), pl.ds(pl.multiple_of(lane, 128), lanes)]

    pairs = [
        (part(merge_ref, 0, core * 512, 512, 128), out_ref.at[:128, :512]),
        (first_ref, out_ref.at[128:, :512]),
    ]
    for tile in range(4):
        pairs.append(
            (
                part(up_third_ref, column * 16, core * 512 + tile * 128),
                out_ref.at[tile * 16 : tile * 16 + 16, 512:],
            )
        )
        pairs.append(
            (
                part(out_third_ref, high * 16, low * 1024 + core * 512 + tile * 128),
                out_ref.at[64 + tile * 16 : 80 + tile * 16, 512:],
            )
        )
    for row in (128, 144):
        pairs.append(
            (part(up_second_ref, high * 16, core * 256 + low * 128), out_ref.at[row : row + 16, 512:])
        )
    for copy in pull(sems, *pairs):
        copy.wait()


def first_kernel(x_ref, left_ref, right_ref, gain_ref, qkv_ref, window_ref, lat_ref, out_ref):
    steps = lat_ref.shape[0]
    own, side = x_ref.shape[0] // steps, left_ref.shape[0] // steps
    lane = lax.broadcasted_iota(jnp.int32, (own, 128), 1)
    key_lane = lax.broadcasted_iota(jnp.int32, (own + 2 * side, 128), 1)
    gain = gain_ref[...]
    for step in range(steps):
        rows = jnp.concatenate(
            [
                x_ref[step * own : (step + 1) * own, :],
                left_ref[step * side : (step + 1) * side, :],
                right_ref[step * side : (step + 1) * side, :],
            ],
            axis=0,
        )
        normed = norm_rows(rows.astype(jnp.float32), gain).astype(jnp.bfloat16)
        query = dot_rows(normed[:own], qkv_ref[0]).astype(jnp.bfloat16)
        query = (query * 0.125).astype(jnp.bfloat16)
        key = dot_rows(normed, qkv_ref[1]).astype(jnp.bfloat16)
        value = dot_rows(normed, qkv_ref[2]).astype(jnp.bfloat16)
        keep = window_ref[...] * lat_ref[step] > 0.0
        first = own // 2 if step == 0 else 0
        last = own // 2 if step == steps - 1 else own
        start = step * own - own // 2 + first
        for pair in range(query.shape[1] // 128):
            here = slice(pair * 128, pair * 128 + 128)
            parts = []
            for odd in range(2):
                picked = (key_lane < HD) if odd == 0 else (key_lane >= HD)
                key_side = jnp.where(picked, key[:, here], jnp.zeros_like(key[:, here]))
                parts.append(mix_tokens(query[:, here], key_side, value[:, here], keep))
            mixed = jnp.where(lane < HD, parts[0], parts[1]).astype(jnp.bfloat16)
            out_ref[start : start + last - first, here] = mixed[first:last]


def pick_matrix(lat_count, lon_count, lat_side, lon_side):
    shape = (2 * lat_count * lon_count, 8 * lat_count * lon_count)
    row = lax.broadcasted_iota(jnp.int32, shape, 0)
    column = lax.broadcasted_iota(jnp.int32, shape, 1)
    bits = lon_count.bit_length() - 1
    lon = row & (lon_count - 1)
    level = jnp.right_shift(row, bits) & 1
    lat = jnp.right_shift(row, bits + 1)
    source = ((2 * lat + lat_side) * 2 + level) * (2 * lon_count) + 2 * lon + lon_side
    return jnp.where(source == column, 1.0, 0.0).astype(jnp.bfloat16)


def join_quads(cells, lat_count, lon_count, gain_ref, out_ref):
    width = cells.shape[1]
    parts = [
        dot_rows(pick_matrix(lat_count, lon_count, lat_side, lon_side), cells)
        for lat_side in range(2)
        for lon_side in range(2)
    ]
    count = 1.0 / (4 * width)
    row_mean = sum(jnp.sum(part, axis=-1, keepdims=True) for part in parts) * count
    parts = [part - row_mean for part in parts]
    spread = sum(jnp.sum(part * part, axis=-1, keepdims=True) for part in parts) * count
    scale = lax.rsqrt(spread + 1e-05)
    for place, part in enumerate(parts):
        here = slice(place * width, place * width + width)
        out_ref[:, here] = (part * scale * gain_ref[:, here]).astype(jnp.bfloat16)


def skip_kernel(
    attended_ref, hidden_hbm, weights_hbm, gain_hbm, skip_ref, merged_ref,
    hidden_ref, weights_ref, gain_ref, sems,
):
    copies = pull(
        sems,
        (weights_hbm.at[:, :, 128:160, :512], weights_ref),
        (hidden_hbm, hidden_ref),
        (gain_hbm, gain_ref),
    )
    for copy in copies:
        copy.wait()
    total = None
    for ring in range(2):
        for z in range(0, 8, 4):
            right = jnp.concatenate(
                [weights_ref[ring, zz] for zz in range(z, z + 4)],
                axis=0,
            )
            start = (ring * 8 + z) * 32
            product = dot_rows(attended_ref[:, start : start + 128], right)
            total = product if total is None else total + product
    skip = (hidden_ref[...].astype(jnp.float32) + total).astype(jnp.bfloat16)
    skip_ref[...] = skip
    join_quads(skip, 6, 8, gain_ref, merged_ref)


def merge_kernel(own_ref, other_ref, weights_ref, own_out_ref, send_ref):
    left = jnp.concatenate([own_ref[...], other_ref[...]], axis=0)
    total = None
    for ring in range(2):
        for z in range(0, 8, 2):
            right = jnp.concatenate(
                [weights_ref[ring, zz * 160 : zz * 160 + 128, :512] for zz in (z, z + 1)], axis=0
            )
            start = (ring * 8 + z) * 128
            product = dot_rows(left[:, start : start + 256], right)
            total = product if total is None else total + product
    rows = own_ref.shape[0]
    own_out_ref[...] = total[:rows].astype(jnp.bfloat16)
    send_ref[...] = total[rows:].astype(jnp.bfloat16)


def join_kernel(core_ref, own_ref, recv_ref, gain_ref, second_ref, coarse_ref, halves_ref):
    core = core_ref[0]
    halves_ref[core] = own_ref[...]
    halves_ref[1 - core] = recv_ref[...]
    second = jnp.concatenate([halves_ref[0], halves_ref[1]], axis=1)
    second_ref[...] = second
    join_quads(second, 3, 4, gain_ref, coarse_ref)


RING_ORDER = (0, -1, 1, -2, 2, -3, 3)


def halves_in_order(core, mine_ref, partner_ref):
    mine, partner = mine_ref[...], partner_ref[...]
    first = core == 0
    return jnp.concatenate(
        [jnp.where(first, mine, partner), jnp.where(first, partner, mine)], axis=0
    )


def near_kernel(place_ref, *refs):
    near, (own_ref, *halves, out_ref) = refs[:7], refs[7:]
    left = jnp.concatenate([ref[...].astype(jnp.float32) for ref in near], axis=0)
    left = left.astype(jnp.bfloat16)
    rows = near[0].shape[0]
    own, other = own_ref[...], halves_in_order(place_ref[0], *halves)
    for weights, shard in ((own, place_ref[2]), (other, 1 - place_ref[2])):
        product = dot_rows(left, weights)
        for at in range(len(near)):
            out_ref[shard, at] = product[at * rows : (at + 1) * rows].astype(jnp.bfloat16)


def far_kernel(place_ref, near_ref, low_ref, high_ref, own_ref, mine_ref, partner_ref, out_ref):
    half = low_ref.shape[1]
    own, other = own_ref[...], halves_in_order(place_ref[0], mine_ref, partner_ref)
    for weights, shard in ((own, place_ref[2]), (other, 1 - place_ref[2])):
        far = dot_rows(low_ref[...], weights[:half]) + dot_rows(high_ref[...], weights[half:])
        out_ref[jnp.bitwise_and(place_ref[1] + 4, 7), shard] = far.astype(jnp.bfloat16)
    for shard in range(2):
        for at, offset in enumerate(RING_ORDER):
            place = jnp.bitwise_and(place_ref[1] + (offset + 8), 7)
            out_ref[place, shard] = near_ref[shard, at]


def third_kernel(
    place_ref, x_ref, gain_ref, own_hbm, mine_ref, partner_ref, out_ref, coarse_ref,
    normed_ref, own_ref, sems,
):
    (copy,) = pull(sems, (own_hbm, own_ref))
    blocks, places, shards, rows, width = x_ref.shape
    count = 1.0 / (blocks * shards * width)
    order = [(z, shard) for shard in range(shards) for z in range(blocks)]
    for first in range(0, places, 2):
        tiles = [
            jnp.concatenate(
                [x_ref[z, first + at, shard].astype(jnp.float32) for at in range(2)], axis=0
            )
            for z, shard in order
        ]
        row_mean = jnp.sum(sum(tiles), axis=-1, keepdims=True) * count
        tiles = [tile - row_mean for tile in tiles]
        spread = jnp.sum(sum(tile * tile for tile in tiles), axis=-1, keepdims=True)
        scale = lax.rsqrt(spread * count + 1e-05)
        for at, tile in enumerate(tiles):
            here = slice(at * width, (at + 1) * width)
            normed_ref[first * rows : (first + 2) * rows, here] = (
                tile * scale * gain_ref[:, here]
            ).astype(jnp.bfloat16)
    for at, (z, shard) in enumerate(order):
        coarse_ref[:, at * width : (at + 1) * width] = x_ref[z, place_ref[1], shard].astype(
            jnp.float32
        )
    query_token = lax.broadcasted_iota(jnp.int32, (96, 96), 0)
    key_token = lax.broadcasted_iota(jnp.int32, (96, 96), 1)
    keep = jnp.right_shift(query_token, 5) == jnp.right_shift(key_token, 5)
    ring = place_ref[2]
    other = halves_in_order(place_ref[0], mine_ref, partner_ref)
    copy.wait()
    for weights, shard in ((own_ref[...], ring), (other, 1 - ring)):
        triple = lax.dot_general(
            normed_ref[...],
            weights,
            (((1,), (1,)), ((), ())),
            preferred_element_type=jnp.float32,
        ).astype(jnp.bfloat16)
        query = (triple[:, :HD] * 0.125).astype(jnp.bfloat16)
        key = triple[:, HD : 2 * HD]
        value = triple[:, 2 * HD :]
        for group in range(places * rows // 96):
            mine = slice(group * 96, group * 96 + 96)
            mixed = mix_tokens(query[mine], key[mine], value[mine], keep)
            for at in range(96 // rows):
                out_ref[group * (96 // rows) + at, shard] = mixed[
                    at * rows : (at + 1) * rows
                ].astype(jnp.bfloat16)


def spread_matrix(lat_count, lon_count):
    fine = (2 * lat_count * lon_count, lat_count * lon_count // 2)
    row = lax.broadcasted_iota(jnp.int32, fine, 0)
    column = lax.broadcasted_iota(jnp.int32, fine, 1)
    bits = lon_count.bit_length() - 1
    lat = jnp.right_shift(row, bits + 2)
    level = jnp.right_shift(row, bits) & 1
    lon = jnp.right_shift(row & (lon_count - 1), 1)
    source = (lat * 2 + level) * (lon_count // 2) + lon
    return jnp.where(source == column, 1.0, 0.0).astype(jnp.bfloat16)


def spread_rows(values, lat_count, lon_count):
    matrix = spread_matrix(lat_count, lon_count)
    high = values.astype(jnp.bfloat16)
    rest = values - high.astype(jnp.float32)
    middle = rest.astype(jnp.bfloat16)
    low = (rest - middle.astype(jnp.float32)).astype(jnp.bfloat16)
    return dot_rows(matrix, high) + (dot_rows(matrix, middle) + dot_rows(matrix, low))


def late_tile(ref, column, ring, z, tile):
    return ref[((column * 2 + ring) * 8 + z) * 9 + tile]


def late_row(ref, column, ring, z, first):
    return jnp.concatenate([late_tile(ref, column, ring, z, first + at) for at in range(4)], axis=1)


def up_kernel(
    core_ref, heads_ref, own_coarse_ref, late_ref, swapped_ref, second_ref, skip_ref, out_ref,
    third_ref, lift_ref, level_ref, small_ref,
):
    core = core_ref[0]
    pairs = []
    for ring in range(2):
        for z in range(0, 8, 2):
            pairs.append(
                jnp.concatenate(
                    [heads_ref[z, ring].astype(jnp.float32), heads_ref[z + 1, ring].astype(jnp.float32)],
                    axis=1,
                ).astype(jnp.bfloat16)
            )
    for weights_ref, origin in ((swapped_ref, 1 - core), (late_ref, core)):
        for part in range(2):
            total = None
            for ring in range(2):
                for z in range(0, 8, 2):
                    right = jnp.concatenate(
                        [
                            late_row(weights_ref, 2 * row + part, ring, zz, 4)
                            for zz in (z, z + 1)
                            for row in range(4)
                        ],
                        axis=0,
                    )
                    product = dot_rows(pairs[ring * 4 + z // 2], right)
                    total = product if total is None else total + product
            third_ref[part, origin] = total
    level_three = []
    for place in range(16):
        here = slice(place * 128, place * 128 + 128)
        quarter = place // 4
        update = third_ref[quarter // 2, quarter % 2][:, place % 4 * 128 : place % 4 * 128 + 128]
        level_three.append((own_coarse_ref[:, here] + update).astype(jnp.bfloat16))
    for weights_ref, origin in ((late_ref, core), (swapped_ref, 1 - core)):
        total = None
        for ring in range(2):
            for z in range(8):
                right = jnp.concatenate(
                    [late_row(weights_ref, y, ring, z, 0) for y in range(8)],
                    axis=0,
                )
                product = dot_rows(level_three[ring * 8 + z], right)
                total = product if total is None else total + product
        lift_ref[origin] = total
    lat_count, lon_count = 6, 8
    for side in range(2):
        here = slice(side * 512, side * 512 + 512)
        level_ref[:, here] = (
            second_ref[:, here].astype(jnp.float32)
            + spread_rows(lift_ref[side], lat_count, lon_count)
        ).astype(jnp.bfloat16)
    for weights_ref, origin in ((late_ref, core), (swapped_ref, 1 - core)):
        total = None
        for ring in range(2):
            for z in range(0, 8, 2):
                right = jnp.concatenate(
                    [
                        jnp.concatenate(
                            [
                                late_tile(weights_ref, 2 * row + part, ring, zz, 8)
                                for zz in (z, z + 1)
                                for row in range(4)
                            ],
                            axis=0,
                        )
                        for part in range(2)
                    ],
                    axis=1,
                )
                start = (ring * 8 + z) * 64
                product = dot_rows(level_ref[:, start : start + 128], right)
                total = product if total is None else total + product
        small_ref[origin] = total
    for side in range(2):
        here = slice(side * 256, side * 256 + 256)
        out_ref[:, here] = (
            skip_ref[:, here].astype(jnp.float32)
            + spread_rows(small_ref[side], 2 * lat_count, 2 * lon_count)
        ).astype(jnp.bfloat16)


Z_RING = 8
RINGS = [[ring * Z_RING + place for place in range(Z_RING)] for ring in range(2)]


def neighbours(first, last, axis):
    count = lax.axis_size(axis)
    before = lax.ppermute(last, axis, [(i, (i + 1) % count) for i in range(count)])
    behind = lax.ppermute(first, axis, [((i + 1) % count, i) for i in range(count)])
    return before, behind


def swap_cores(values):
    count = lax.axis_size("lon")
    return lax.ppermute(values, "lon", [(i, i ^ 1) for i in range(count)])


def swap_rings(values):
    count = lax.axis_size("lat")
    return lax.ppermute(values, "lat", [(i, (i + Z_RING) % count) for i in range(count)])


def ring_scatter(blocks):
    return lax.all_to_all(blocks, "lat", 0, 0, axis_index_groups=RINGS, tiled=True)


def ring_shift(values, step):
    pairs = [(at, at // Z_RING * Z_RING + (at + step) % Z_RING) for at in range(2 * Z_RING)]
    return lax.ppermute(values, "lat", pairs)


def ring_gather(values):
    return ring_scatter(jnp.broadcast_to(values[None], (Z_RING,) + values.shape))


def after(values, *before):
    return lax.optimization_barrier((values,) + before)[0]


def on_device(
    fields,
    land_ids,
    surface_table,
    level_table,
    norm_first,
    qkv_first,
    out_first,
    norm_merge2,
    merge_second,
    norm_merge3,
    merge_third,
    norm_third,
    qkv_third,
    out_third,
    up_third,
    up_second,
):
    tile_rows, levels, tile_cols, feat_dim = fields.shape
    lat_count = lax.axis_size("lat")
    ring = lax.axis_index("lat") // Z_RING
    core = lax.axis_index("lon") % 2
    column = lax.axis_index("lon") // 4

    own_merge = call_kernel(
        pack_kernel,
        jax.ShapeDtypeStruct((160, 640), jnp.bfloat16),
        (
            jnp.stack([core, column]).astype(jnp.int32),
            merge_second,
            out_first,
            up_third,
            up_second,
            out_third,
        ),
        (pltpu.SemaphoreType.DMA((12,)),),
        pulled=(1, 2, 3, 4, 5),
        vmem_mib=62,
    )
    both_merge = lax.all_gather(
        own_merge, "lat", axis_index_groups=[[z, z + Z_RING] for z in range(Z_RING)]
    )
    merge_weights = lax.all_gather(
        both_merge, "lat", axis=1, axis_index_groups=RINGS, tiled=True
    )
    core_place = jnp.stack([core, lax.axis_index("lat") % Z_RING, ring]).astype(jnp.int32)
    picks = (land_ids[:, :, None] == jnp.arange(3, dtype=jnp.int32)).astype(jnp.float32)
    surface = jnp.einsum("ijs,sc->ijc", picks, surface_table.astype(jnp.float32))
    hidden = (
        fields.astype(jnp.float32)
        + surface[:, None, :, :]
        + level_table.astype(jnp.float32)[None, :, None, :]
    ).astype(jnp.bfloat16)
    hidden = after(hidden, both_merge)
    above, below = neighbours(hidden[:2], hidden[-2:], "lat")
    cells = jnp.concatenate([above, hidden, below], axis=0)
    qkv_third = qkv_third.transpose(0, 2, 1).reshape(-1, qkv_third.shape[1])

    merge_third, cells = lax.optimization_barrier((merge_third, cells))
    left, right = neighbours(cells[:, :, :2], cells[:, :, -2:], "lon")
    qkv_third, left, right = lax.optimization_barrier((qkv_third, left, right))

    merge_mine, qkv_mine = [
        swap_rings(lax.dynamic_slice_in_dim(table, core * (table.shape[0] // 2), table.shape[0] // 2))
        for table in (merge_third, qkv_third)
    ]

    ext_rows = tile_rows + 4
    own_window = (jnp.arange(32 * 4) % tile_cols + 2) // 4
    key_window = jnp.concatenate(
        [own_window, jnp.zeros((16,), jnp.int32), jnp.full((16,), tile_cols // 4, jnp.int32)]
    )
    same_window = (key_window[:, None] == own_window[None, :]).astype(jnp.float32)
    lat_place = lax.axis_index("lat") * tile_rows + jnp.arange(ext_rows) - 2
    valid_rows = ((lat_place >= 0) & (lat_place < tile_rows * lat_count)).astype(jnp.float32)
    valid_rows = valid_rows.reshape(ext_rows // 4, 4, 1)
    valid_keys = jnp.concatenate(
        [jnp.repeat(valid_rows, 2 * count, axis=1) for count in (tile_cols, 2, 2)], axis=1
    )
    attended = call_kernel(
        first_kernel,
        jax.ShapeDtypeStruct((tile_rows * levels * tile_cols, feat_dim), jnp.bfloat16),
        (
            cells.reshape(-1, feat_dim),
            left.reshape(-1, feat_dim),
            right.reshape(-1, feat_dim),
            norm_first[None],
            qkv_first,
            same_window,
            valid_keys,
        ),
        flops=2 * 640 * 512 * 1536,
    )
    attended = after(attended, merge_mine, qkv_mine)
    tokens = attended.shape[0]
    skip_first, merged_in = call_kernel(
        skip_kernel,
        (
            jax.ShapeDtypeStruct((tokens, feat_dim), jnp.bfloat16),
            jax.ShapeDtypeStruct((tokens // 4, 4 * feat_dim), jnp.bfloat16),
        ),
        (
            attended,
            hidden.reshape(-1, feat_dim),
            merge_weights.reshape(2, Z_RING, 160, 640),
            norm_merge2[None],
        ),
        (
            pltpu.VMEM((tokens, feat_dim), jnp.bfloat16),
            pltpu.VMEM((2, Z_RING, 32, 512), jnp.bfloat16),
            pltpu.VMEM((1, 4 * feat_dim), jnp.float32),
            pltpu.SemaphoreType.DMA((3,)),
        ),
        flops=2 * 384 * 512 * 512,
        pulled=(1, 2, 3),
        vmem_mib=58,
    )
    own_rows = merged_in.shape[0]
    half_shape = jax.ShapeDtypeStruct((own_rows, 512), jnp.bfloat16)
    second_half, second_send = call_kernel(
        merge_kernel,
        (half_shape, half_shape),
        (merged_in, swap_cores(merged_in), merge_weights),
        flops=2 * 192 * 2048 * 512,
    )
    late = after(merge_weights, second_send).reshape(2, Z_RING, 10, 16, 640)[:, :, :9, :, 512:]
    late = lax.all_gather(
        late.reshape(-1, 128),
        "lon",
        axis=0,
        axis_index_groups=[[4 * y + x for y in range(8)] for x in range(4)],
        tiled=True,
    ).reshape(-1, 16, 128)
    second_cells, coarse_in = call_kernel(
        join_kernel,
        (
            jax.ShapeDtypeStruct((own_rows, 1024), jnp.bfloat16),
            jax.ShapeDtypeStruct((own_rows // 4, 4096), jnp.bfloat16),
        ),
        (core_place, second_half, swap_cores(second_send), norm_merge3[None]),
        (pltpu.VMEM((2, own_rows, 512), jnp.bfloat16),),
        flops=2 * 96 * 96 * 1024,
    )
    own_count = coarse_in.shape[0]

    pieces, forth, back = [coarse_in], coarse_in, coarse_in
    for _ in range(3):
        forth, back = ring_shift(forth, 1), ring_shift(back, -1)
        pieces += [forth, back]
    merge_mine, qkv_mine = after(merge_mine, pieces[1]), after(qkv_mine, pieces[3])
    merge_partner, qkv_partner = swap_cores(merge_mine), swap_cores(qkv_mine)
    half_feats = coarse_in.shape[1] // 2
    forth, back = after(forth, merge_partner), after(back, qkv_partner)
    far_low, far_high = ring_shift(forth[:, :half_feats], 1), ring_shift(back[:, half_feats:], -1)
    tables = (merge_third, merge_mine, merge_partner)
    near = call_kernel(
        near_kernel,
        jax.ShapeDtypeStruct((2, len(RING_ORDER), own_count, 128), jnp.bfloat16),
        (core_place, *pieces, *tables),
        flops=2 * 168 * 4096 * 256,
    )
    column_block = call_kernel(
        far_kernel,
        jax.ShapeDtypeStruct((Z_RING, 2, own_count, 128), jnp.bfloat16),
        (core_place, near, far_low, far_high, *tables),
        flops=2 * 24 * 4096 * 256,
    )
    heads_out, own_coarse = call_kernel(
        third_kernel,
        (
            jax.ShapeDtypeStruct((Z_RING, 2, own_count, HD), jnp.bfloat16),
            jax.ShapeDtypeStruct((own_count, 2048), jnp.float32),
        ),
        (core_place, ring_gather(column_block), norm_third[None], qkv_third, qkv_mine, qkv_partner),
        (
            pltpu.VMEM((Z_RING * own_count, 2048), jnp.bfloat16),
            pltpu.VMEM(qkv_third.shape, jnp.bfloat16),
            pltpu.SemaphoreType.DMA((1,)),
        ),
        flops=2 * 192 * 2048 * 384,
        pulled=(3,),
    )

    late_swapped = swap_cores(after(late, heads_out))
    decoded = call_kernel(
        up_kernel,
        jax.ShapeDtypeStruct((tile_rows * levels * tile_cols, feat_dim), jnp.bfloat16),
        (
            core_place,
            ring_scatter(heads_out),
            own_coarse,
            late,
            late_swapped,
            second_cells,
            skip_first,
        ),
        (
            pltpu.VMEM((2, 2, own_count, 512), jnp.float32),
            pltpu.VMEM((2, own_count, 512), jnp.float32),
            pltpu.VMEM((second_cells.shape[0], 1024), jnp.bfloat16),
            pltpu.VMEM((2, second_cells.shape[0], 256), jnp.float32),
        ),
        flops=2 * (24 * 1024 * 2048 + 24 * 2048 * 1024 + 96 * 1024 * 512),
    )
    return decoded.reshape(fields.shape)


def solution(mesh):
    in_specs = (
        P("lat", None, "lon", None),
        P("lat", "lon"),
        P(),
        P(),
        P(),
        P(),
        P("lat", None),
        P(),
        P("lat", None),
        P(),
        P(None, "lat"),
        P(),
        P(None, None, "lat"),
        P("lat", None),
        P("lat", None),
        P("lat", None),
    )
    out_specs = P("lat", None, "lon", None)
    return jax.shard_map(
        on_device, mesh=mesh, in_specs=in_specs, out_specs=out_specs, check_vma=False
    )
```

```python
import jax
import jax.numpy as jnp
from jax import lax
from jax.experimental import pallas as pl
from jax.experimental.pallas import tpu as pltpu
from jax.sharding import PartitionSpec as P

HD = 64


def norm_rows(values, gain):
    row_mean = jnp.mean(values, axis=-1, keepdims=True)
    centred = values - row_mean
    spread = jnp.mean(centred * centred, axis=-1, keepdims=True)
    return centred * lax.rsqrt(spread + 1e-05) * gain


def call_kernel(body, out_shape, operands, scratch=(), flops=0, pulled=(), vmem_mib=48):
    spaces = [
        pltpu.SMEM if operand.dtype == jnp.int32 else pltpu.HBM if at in pulled else pltpu.VMEM
        for at, operand in enumerate(operands)
    ]
    return pl.pallas_call(
        body,
        out_shape=out_shape,
        in_specs=[pl.BlockSpec(memory_space=space) for space in spaces],
        out_specs=jax.tree.map(lambda _: pl.BlockSpec(memory_space=pltpu.VMEM), out_shape),
        scratch_shapes=list(scratch),
        compiler_params=pltpu.CompilerParams(vmem_limit_bytes=vmem_mib * 1024 * 1024),
        cost_estimate=pl.CostEstimate(
            flops=flops,
            bytes_accessed=sum(operand.size * operand.dtype.itemsize for operand in operands),
            transcendentals=0,
        ),
    )(*operands)


def pull(sems, *pairs):
    copies = [pltpu.make_async_copy(src, dst, sems.at[at]) for at, (src, dst) in enumerate(pairs)]
    for copy in copies:
        copy.start()
    return copies


def dot_rows(left, right):
    return lax.dot_general(left, right, (((1,), (0,)), ((), ())), preferred_element_type=jnp.float32)


def mix_tokens(query, key, value, keep):
    scores = lax.dot_general(
        key, query, (((1,), (1,)), ((), ())), preferred_element_type=jnp.float32
    )
    scores = jnp.where(keep, scores, -1e30)
    weights = jnp.exp(scores - jnp.max(scores, axis=0, keepdims=True))
    weights = (weights / jnp.sum(weights, axis=0, keepdims=True)).astype(jnp.bfloat16)
    return lax.dot_general(
        weights, value, (((0,), (0,)), ((), ())), preferred_element_type=jnp.float32
    )


def pack_kernel(
    place_ref, merge_ref, first_ref, up_third_ref, up_second_ref, out_third_ref, out_ref, sems
):
    core, column = place_ref[0], place_ref[1]
    high, low = jnp.right_shift(column, 1), jnp.bitwise_and(column, 1)

    def part(ref, row, lane, lanes=128, rows=16):
        return ref.at[pl.ds(pl.multiple_of(row, 16), rows), pl.ds(pl.multiple_of(lane, 128), lanes)]

    pairs = [
        (part(merge_ref, 0, core * 512, 512, 128), out_ref.at[:128, :512]),
        (first_ref, out_ref.at[128:, :512]),
    ]
    for tile in range(4):
        pairs.append(
            (
                part(up_third_ref, column * 16, core * 512 + tile * 128),
                out_ref.at[tile * 16 : tile * 16 + 16, 512:],
            )
        )
        pairs.append(
            (
                part(out_third_ref, high * 16, low * 1024 + core * 512 + tile * 128),
                out_ref.at[64 + tile * 16 : 80 + tile * 16, 512:],
            )
        )
    for row in (128, 144):
        pairs.append(
            (part(up_second_ref, high * 16, core * 256 + low * 128), out_ref.at[row : row + 16, 512:])
        )
    for copy in pull(sems, *pairs):
        copy.wait()


def first_kernel(x_ref, left_ref, right_ref, gain_ref, qkv_ref, window_ref, lat_ref, out_ref):
    steps = lat_ref.shape[0]
    own, side = x_ref.shape[0] // steps, left_ref.shape[0] // steps
    lane = lax.broadcasted_iota(jnp.int32, (own, 128), 1)
    key_lane = lax.broadcasted_iota(jnp.int32, (own + 2 * side, 128), 1)
    gain = gain_ref[...]
    for step in range(steps):
        rows = jnp.concatenate(
            [
                x_ref[step * own : (step + 1) * own, :],
                left_ref[step * side : (step + 1) * side, :],
                right_ref[step * side : (step + 1) * side, :],
            ],
            axis=0,
        )
        normed = norm_rows(rows.astype(jnp.float32), gain).astype(jnp.bfloat16)
        query = dot_rows(normed[:own], qkv_ref[0]).astype(jnp.bfloat16)
        query = (query * 0.125).astype(jnp.bfloat16)
        key = dot_rows(normed, qkv_ref[1]).astype(jnp.bfloat16)
        value = dot_rows(normed, qkv_ref[2]).astype(jnp.bfloat16)
        keep = window_ref[...] * lat_ref[step] > 0.0
        first = own // 2 if step == 0 else 0
        last = own // 2 if step == steps - 1 else own
        start = step * own - own // 2 + first
        for pair in range(query.shape[1] // 128):
            here = slice(pair * 128, pair * 128 + 128)
            parts = []
            for odd in range(2):
                picked = (key_lane < HD) if odd == 0 else (key_lane >= HD)
                key_side = jnp.where(picked, key[:, here], jnp.zeros_like(key[:, here]))
                parts.append(mix_tokens(query[:, here], key_side, value[:, here], keep))
            mixed = jnp.where(lane < HD, parts[0], parts[1]).astype(jnp.bfloat16)
            out_ref[start : start + last - first, here] = mixed[first:last]


def pick_matrix(lat_count, lon_count, lat_side, lon_side):
    shape = (2 * lat_count * lon_count, 8 * lat_count * lon_count)
    row = lax.broadcasted_iota(jnp.int32, shape, 0)
    column = lax.broadcasted_iota(jnp.int32, shape, 1)
    bits = lon_count.bit_length() - 1
    lon = row & (lon_count - 1)
    level = jnp.right_shift(row, bits) & 1
    lat = jnp.right_shift(row, bits + 1)
    source = ((2 * lat + lat_side) * 2 + level) * (2 * lon_count) + 2 * lon + lon_side
    return jnp.where(source == column, 1.0, 0.0).astype(jnp.bfloat16)


def join_quads(cells, lat_count, lon_count, gain_ref, out_ref):
    width = cells.shape[1]
    parts = [
        dot_rows(pick_matrix(lat_count, lon_count, lat_side, lon_side), cells)
        for lat_side in range(2)
        for lon_side in range(2)
    ]
    count = 1.0 / (4 * width)
    row_mean = sum(jnp.sum(part, axis=-1, keepdims=True) for part in parts) * count
    parts = [part - row_mean for part in parts]
    spread = sum(jnp.sum(part * part, axis=-1, keepdims=True) for part in parts) * count
    scale = lax.rsqrt(spread + 1e-05)
    for place, part in enumerate(parts):
        here = slice(place * width, place * width + width)
        out_ref[:, here] = (part * scale * gain_ref[:, here]).astype(jnp.bfloat16)


def skip_kernel(
    attended_ref, hidden_hbm, weights_hbm, gain_hbm, skip_ref, merged_ref,
    hidden_ref, weights_ref, gain_ref, sems,
):
    copies = pull(
        sems,
        (weights_hbm.at[:, :, 128:160, :512], weights_ref),
        (hidden_hbm, hidden_ref),
        (gain_hbm, gain_ref),
    )
    for copy in copies:
        copy.wait()
    total = None
    for ring in range(2):
        for z in range(0, 8, 4):
            right = jnp.concatenate(
                [weights_ref[ring, zz] for zz in range(z, z + 4)],
                axis=0,
            )
            start = (ring * 8 + z) * 32
            product = dot_rows(attended_ref[:, start : start + 128], right)
            total = product if total is None else total + product
    skip = (hidden_ref[...].astype(jnp.float32) + total).astype(jnp.bfloat16)
    skip_ref[...] = skip
    join_quads(skip, 6, 8, gain_ref, merged_ref)


def merge_kernel(own_ref, other_ref, weights_ref, own_out_ref, send_ref):
    left = jnp.concatenate([own_ref[...], other_ref[...]], axis=0)
    total = None
    for ring in range(2):
        for z in range(0, 8, 2):
            right = jnp.concatenate(
                [weights_ref[ring, zz * 160 : zz * 160 + 128, :512] for zz in (z, z + 1)], axis=0
            )
            start = (ring * 8 + z) * 128
            product = dot_rows(left[:, start : start + 256], right)
            total = product if total is None else total + product
    rows = own_ref.shape[0]
    own_out_ref[...] = total[:rows].astype(jnp.bfloat16)
    send_ref[...] = total[rows:].astype(jnp.bfloat16)


def join_kernel(core_ref, own_ref, recv_ref, gain_ref, second_ref, coarse_ref, halves_ref):
    core = core_ref[0]
    halves_ref[core] = own_ref[...]
    halves_ref[1 - core] = recv_ref[...]
    second = jnp.concatenate([halves_ref[0], halves_ref[1]], axis=1)
    second_ref[...] = second
    join_quads(second, 3, 4, gain_ref, coarse_ref)


RING_ORDER = (0, -1, 1, -2, 2, -3, 3)


def halves_in_order(core, mine_ref, partner_ref):
    mine, partner = mine_ref[...], partner_ref[...]
    first = core == 0
    return jnp.concatenate(
        [jnp.where(first, mine, partner), jnp.where(first, partner, mine)], axis=0
    )


def near_kernel(place_ref, *refs):
    near, (own_ref, *halves, out_ref) = refs[:7], refs[7:]
    left = jnp.concatenate([ref[...].astype(jnp.float32) for ref in near], axis=0)
    left = left.astype(jnp.bfloat16)
    rows = near[0].shape[0]
    own, other = own_ref[...], halves_in_order(place_ref[0], *halves)
    for weights, shard in ((own, place_ref[2]), (other, 1 - place_ref[2])):
        product = dot_rows(left, weights)
        for at in range(len(near)):
            out_ref[shard, at] = product[at * rows : (at + 1) * rows].astype(jnp.bfloat16)


def far_kernel(place_ref, near_ref, low_ref, high_ref, own_ref, mine_ref, partner_ref, out_ref):
    half = low_ref.shape[1]
    own, other = own_ref[...], halves_in_order(place_ref[0], mine_ref, partner_ref)
    for weights, shard in ((own, place_ref[2]), (other, 1 - place_ref[2])):
        far = dot_rows(low_ref[...], weights[:half]) + dot_rows(high_ref[...], weights[half:])
        out_ref[jnp.bitwise_and(place_ref[1] + 4, 7), shard] = far.astype(jnp.bfloat16)
    for shard in range(2):
        for at, offset in enumerate(RING_ORDER):
            place = jnp.bitwise_and(place_ref[1] + (offset + 8), 7)
            out_ref[place, shard] = near_ref[shard, at]


def third_kernel(
    place_ref, x_ref, gain_ref, own_hbm, mine_ref, partner_ref, out_ref, coarse_ref,
    normed_ref, own_ref, sems,
):
    (copy,) = pull(sems, (own_hbm, own_ref))
    blocks, places, shards, rows, width = x_ref.shape
    count = 1.0 / (blocks * shards * width)
    order = [(z, shard) for shard in range(shards) for z in range(blocks)]
    for first in range(0, places, 2):
        tiles = [
            jnp.concatenate(
                [x_ref[z, first + at, shard].astype(jnp.float32) for at in range(2)], axis=0
            )
            for z, shard in order
        ]
        row_mean = jnp.sum(sum(tiles), axis=-1, keepdims=True) * count
        tiles = [tile - row_mean for tile in tiles]
        spread = jnp.sum(sum(tile * tile for tile in tiles), axis=-1, keepdims=True)
        scale = lax.rsqrt(spread * count + 1e-05)
        for at, tile in enumerate(tiles):
            here = slice(at * width, (at + 1) * width)
            normed_ref[first * rows : (first + 2) * rows, here] = (
                tile * scale * gain_ref[:, here]
            ).astype(jnp.bfloat16)
    for at, (z, shard) in enumerate(order):
        coarse_ref[:, at * width : (at + 1) * width] = x_ref[z, place_ref[1], shard].astype(
            jnp.float32
        )
    query_token = lax.broadcasted_iota(jnp.int32, (96, 96), 0)
    key_token = lax.broadcasted_iota(jnp.int32, (96, 96), 1)
    keep = jnp.right_shift(query_token, 5) == jnp.right_shift(key_token, 5)
    ring = place_ref[2]
    other = halves_in_order(place_ref[0], mine_ref, partner_ref)
    copy.wait()
    for weights, shard in ((own_ref[...], ring), (other, 1 - ring)):
        triple = lax.dot_general(
            normed_ref[...],
            weights,
            (((1,), (1,)), ((), ())),
            preferred_element_type=jnp.float32,
        ).astype(jnp.bfloat16)
        query = (triple[:, :HD] * 0.125).astype(jnp.bfloat16)
        key = triple[:, HD : 2 * HD]
        value = triple[:, 2 * HD :]
        for group in range(places * rows // 96):
            mine = slice(group * 96, group * 96 + 96)
            mixed = mix_tokens(query[mine], key[mine], value[mine], keep)
            for at in range(96 // rows):
                out_ref[group * (96 // rows) + at, shard] = mixed[
                    at * rows : (at + 1) * rows
                ].astype(jnp.bfloat16)


def spread_matrix(lat_count, lon_count):
    fine = (2 * lat_count * lon_count, lat_count * lon_count // 2)
    row = lax.broadcasted_iota(jnp.int32, fine, 0)
    column = lax.broadcasted_iota(jnp.int32, fine, 1)
    bits = lon_count.bit_length() - 1
    lat = jnp.right_shift(row, bits + 2)
    level = jnp.right_shift(row, bits) & 1
    lon = jnp.right_shift(row & (lon_count - 1), 1)
    source = (lat * 2 + level) * (lon_count // 2) + lon
    return jnp.where(source == column, 1.0, 0.0).astype(jnp.bfloat16)


def spread_rows(values, lat_count, lon_count):
    matrix = spread_matrix(lat_count, lon_count)
    high = values.astype(jnp.bfloat16)
    rest = values - high.astype(jnp.float32)
    middle = rest.astype(jnp.bfloat16)
    low = (rest - middle.astype(jnp.float32)).astype(jnp.bfloat16)
    return dot_rows(matrix, high) + (dot_rows(matrix, middle) + dot_rows(matrix, low))


def late_tile(ref, column, ring, z, tile):
    return ref[((column * 2 + ring) * 8 + z) * 9 + tile]


def late_row(ref, column, ring, z, first):
    return jnp.concatenate([late_tile(ref, column, ring, z, first + at) for at in range(4)], axis=1)


def up_kernel(
    core_ref, heads_ref, own_coarse_ref, late_ref, swapped_ref, second_ref, skip_ref, out_ref,
    third_ref, lift_ref, level_ref, small_ref,
):
    core = core_ref[0]
    pairs = []
    for ring in range(2):
        for z in range(0, 8, 2):
            pairs.append(
                jnp.concatenate(
                    [heads_ref[z, ring].astype(jnp.float32), heads_ref[z + 1, ring].astype(jnp.float32)],
                    axis=1,
                ).astype(jnp.bfloat16)
            )
    for weights_ref, origin in ((swapped_ref, 1 - core), (late_ref, core)):
        for part in range(2):
            total = None
            for ring in range(2):
                for z in range(0, 8, 2):
                    right = jnp.concatenate(
                        [
                            late_row(weights_ref, 2 * row + part, ring, zz, 4)
                            for zz in (z, z + 1)
                            for row in range(4)
                        ],
                        axis=0,
                    )
                    product = dot_rows(pairs[ring * 4 + z // 2], right)
                    total = product if total is None else total + product
            third_ref[part, origin] = total
    level_three = []
    for place in range(16):
        here = slice(place * 128, place * 128 + 128)
        quarter = place // 4
        update = third_ref[quarter // 2, quarter % 2][:, place % 4 * 128 : place % 4 * 128 + 128]
        level_three.append((own_coarse_ref[:, here] + update).astype(jnp.bfloat16))
    for weights_ref, origin in ((late_ref, core), (swapped_ref, 1 - core)):
        total = None
        for ring in range(2):
            for z in range(8):
                right = jnp.concatenate(
                    [late_row(weights_ref, y, ring, z, 0) for y in range(8)],
                    axis=0,
                )
                product = dot_rows(level_three[ring * 8 + z], right)
                total = product if total is None else total + product
        lift_ref[origin] = total
    lat_count, lon_count = 6, 8
    for side in range(2):
        here = slice(side * 512, side * 512 + 512)
        level_ref[:, here] = (
            second_ref[:, here].astype(jnp.float32)
            + spread_rows(lift_ref[side], lat_count, lon_count)
        ).astype(jnp.bfloat16)
    for weights_ref, origin in ((late_ref, core), (swapped_ref, 1 - core)):
        total = None
        for ring in range(2):
            for z in range(0, 8, 2):
                right = jnp.concatenate(
                    [
                        jnp.concatenate(
                            [
                                late_tile(weights_ref, 2 * row + part, ring, zz, 8)
                                for zz in (z, z + 1)
                                for row in range(4)
                            ],
                            axis=0,
                        )
                        for part in range(2)
                    ],
                    axis=1,
                )
                start = (ring * 8 + z) * 64
                product = dot_rows(level_ref[:, start : start + 128], right)
                total = product if total is None else total + product
        small_ref[origin] = total
    for side in range(2):
        here = slice(side * 256, side * 256 + 256)
        out_ref[:, here] = (
            skip_ref[:, here].astype(jnp.float32)
            + spread_rows(small_ref[side], 2 * lat_count, 2 * lon_count)
        ).astype(jnp.bfloat16)


Z_RING = 8
RINGS = [[ring * Z_RING + place for place in range(Z_RING)] for ring in range(2)]


def neighbours(first, last, axis):
    count = lax.axis_size(axis)
    before = lax.ppermute(last, axis, [(i, (i + 1) % count) for i in range(count)])
    behind = lax.ppermute(first, axis, [((i + 1) % count, i) for i in range(count)])
    return before, behind


def swap_cores(values):
    count = lax.axis_size("lon")
    return lax.ppermute(values, "lon", [(i, i ^ 1) for i in range(count)])


def swap_rings(values):
    count = lax.axis_size("lat")
    return lax.ppermute(values, "lat", [(i, (i + Z_RING) % count) for i in range(count)])


def ring_scatter(blocks):
    return lax.all_to_all(blocks, "lat", 0, 0, axis_index_groups=RINGS, tiled=True)


def ring_shift(values, step):
    pairs = [(at, at // Z_RING * Z_RING + (at + step) % Z_RING) for at in range(2 * Z_RING)]
    return lax.ppermute(values, "lat", pairs)


def ring_gather(values):
    return ring_scatter(jnp.broadcast_to(values[None], (Z_RING,) + values.shape))


def after(values, *before):
    return lax.optimization_barrier((values,) + before)[0]


def on_device(
    fields,
    land_ids,
    surface_table,
    level_table,
    norm_first,
    qkv_first,
    out_first,
    norm_merge2,
    merge_second,
    norm_merge3,
    merge_third,
    norm_third,
    qkv_third,
    out_third,
    up_third,
    up_second,
):
    tile_rows, levels, tile_cols, feat_dim = fields.shape
    lat_count = lax.axis_size("lat")
    ring = lax.axis_index("lat") // Z_RING
    core = lax.axis_index("lon") % 2
    column = lax.axis_index("lon") // 4

    own_merge = call_kernel(
        pack_kernel,
        jax.ShapeDtypeStruct((160, 640), jnp.bfloat16),
        (
            jnp.stack([core, column]).astype(jnp.int32),
            merge_second,
            out_first,
            up_third,
            up_second,
            out_third,
        ),
        (pltpu.SemaphoreType.DMA((12,)),),
        pulled=(1, 2, 3, 4, 5),
        vmem_mib=62,
    )
    both_merge = lax.all_gather(
        own_merge, "lat", axis_index_groups=[[z, z + Z_RING] for z in range(Z_RING)]
    )
    merge_weights = lax.all_gather(
        both_merge, "lat", axis=1, axis_index_groups=RINGS, tiled=True
    )
    core_place = jnp.stack([core, lax.axis_index("lat") % Z_RING, ring]).astype(jnp.int32)
    picks = (land_ids[:, :, None] == jnp.arange(3, dtype=jnp.int32)).astype(jnp.float32)
    surface = jnp.einsum("ijs,sc->ijc", picks, surface_table.astype(jnp.float32))
    hidden = (
        fields.astype(jnp.float32)
        + surface[:, None, :, :]
        + level_table.astype(jnp.float32)[None, :, None, :]
    ).astype(jnp.bfloat16)
    hidden = after(hidden, both_merge)
    above, below = neighbours(hidden[:2], hidden[-2:], "lat")
    cells = jnp.concatenate([above, hidden, below], axis=0)
    qkv_third = qkv_third.transpose(0, 2, 1).reshape(-1, qkv_third.shape[1])

    merge_third, qkv_third, cells = lax.optimization_barrier((merge_third, qkv_third, cells))
    left, right = neighbours(cells[:, :, :2], cells[:, :, -2:], "lon")

    merge_mine, qkv_mine = [
        swap_rings(lax.dynamic_slice_in_dim(table, core * (table.shape[0] // 2), table.shape[0] // 2))
        for table in (merge_third, qkv_third)
    ]

    ext_rows = tile_rows + 4
    own_window = (jnp.arange(32 * 4) % tile_cols + 2) // 4
    key_window = jnp.concatenate(
        [own_window, jnp.zeros((16,), jnp.int32), jnp.full((16,), tile_cols // 4, jnp.int32)]
    )
    same_window = (key_window[:, None] == own_window[None, :]).astype(jnp.float32)
    lat_place = lax.axis_index("lat") * tile_rows + jnp.arange(ext_rows) - 2
    valid_rows = ((lat_place >= 0) & (lat_place < tile_rows * lat_count)).astype(jnp.float32)
    valid_rows = valid_rows.reshape(ext_rows // 4, 4, 1)
    valid_keys = jnp.concatenate(
        [jnp.repeat(valid_rows, 2 * count, axis=1) for count in (tile_cols, 2, 2)], axis=1
    )
    attended = call_kernel(
        first_kernel,
        jax.ShapeDtypeStruct((tile_rows * levels * tile_cols, feat_dim), jnp.bfloat16),
        (
            cells.reshape(-1, feat_dim),
            left.reshape(-1, feat_dim),
            right.reshape(-1, feat_dim),
            norm_first[None],
            qkv_first,
            same_window,
            valid_keys,
        ),
        flops=2 * 640 * 512 * 1536,
    )
    merge_partner, qkv_partner = swap_cores(merge_mine), swap_cores(qkv_mine)
    attended = after(attended, merge_partner, qkv_partner)
    tokens = attended.shape[0]
    skip_first, merged_in = call_kernel(
        skip_kernel,
        (
            jax.ShapeDtypeStruct((tokens, feat_dim), jnp.bfloat16),
            jax.ShapeDtypeStruct((tokens // 4, 4 * feat_dim), jnp.bfloat16),
        ),
        (
            attended,
            hidden.reshape(-1, feat_dim),
            merge_weights.reshape(2, Z_RING, 160, 640),
            norm_merge2[None],
        ),
        (
            pltpu.VMEM((tokens, feat_dim), jnp.bfloat16),
            pltpu.VMEM((2, Z_RING, 32, 512), jnp.bfloat16),
            pltpu.VMEM((1, 4 * feat_dim), jnp.float32),
            pltpu.SemaphoreType.DMA((3,)),
        ),
        flops=2 * 384 * 512 * 512,
        pulled=(1, 2, 3),
        vmem_mib=58,
    )
    own_rows = merged_in.shape[0]
    half_shape = jax.ShapeDtypeStruct((own_rows, 512), jnp.bfloat16)
    second_half, second_send = call_kernel(
        merge_kernel,
        (half_shape, half_shape),
        (merged_in, swap_cores(merged_in), merge_weights),
        flops=2 * 192 * 2048 * 512,
    )
    late = after(merge_weights, second_send).reshape(2, Z_RING, 10, 16, 640)[:, :, :9, :, 512:]
    late = lax.all_gather(
        late.reshape(-1, 128),
        "lon",
        axis=0,
        axis_index_groups=[[4 * y + x for y in range(8)] for x in range(4)],
        tiled=True,
    ).reshape(-1, 16, 128)
    second_cells, coarse_in = call_kernel(
        join_kernel,
        (
            jax.ShapeDtypeStruct((own_rows, 1024), jnp.bfloat16),
            jax.ShapeDtypeStruct((own_rows // 4, 4096), jnp.bfloat16),
        ),
        (core_place, second_half, swap_cores(second_send), norm_merge3[None]),
        (pltpu.VMEM((2, own_rows, 512), jnp.bfloat16),),
        flops=2 * 96 * 96 * 1024,
    )
    own_count = coarse_in.shape[0]

    pieces, forth, back = [coarse_in], coarse_in, coarse_in
    for _ in range(3):
        forth, back = ring_shift(forth, 1), ring_shift(back, -1)
        pieces += [forth, back]
    half_feats = coarse_in.shape[1] // 2
    far_low, far_high = ring_shift(forth[:, :half_feats], 1), ring_shift(back[:, half_feats:], -1)
    tables = (merge_third, merge_mine, merge_partner)
    near = call_kernel(
        near_kernel,
        jax.ShapeDtypeStruct((2, len(RING_ORDER), own_count, 128), jnp.bfloat16),
        (core_place, *pieces, *tables),
        flops=2 * 168 * 4096 * 256,
    )
    column_block = call_kernel(
        far_kernel,
        jax.ShapeDtypeStruct((Z_RING, 2, own_count, 128), jnp.bfloat16),
        (core_place, near, far_low, far_high, *tables),
        flops=2 * 24 * 4096 * 256,
    )
    heads_out, own_coarse = call_kernel(
        third_kernel,
        (
            jax.ShapeDtypeStruct((Z_RING, 2, own_count, HD), jnp.bfloat16),
            jax.ShapeDtypeStruct((own_count, 2048), jnp.float32),
        ),
        (core_place, ring_gather(column_block), norm_third[None], qkv_third, qkv_mine, qkv_partner),
        (
            pltpu.VMEM((Z_RING * own_count, 2048), jnp.bfloat16),
            pltpu.VMEM(qkv_third.shape, jnp.bfloat16),
            pltpu.SemaphoreType.DMA((1,)),
        ),
        flops=2 * 192 * 2048 * 384,
        pulled=(3,),
    )

    late_swapped = swap_cores(after(late, heads_out))
    decoded = call_kernel(
        up_kernel,
        jax.ShapeDtypeStruct((tile_rows * levels * tile_cols, feat_dim), jnp.bfloat16),
        (
            core_place,
            ring_scatter(heads_out),
            own_coarse,
            late,
            late_swapped,
            second_cells,
            skip_first,
        ),
        (
            pltpu.VMEM((2, 2, own_count, 512), jnp.float32),
            pltpu.VMEM((2, own_count, 512), jnp.float32),
            pltpu.VMEM((second_cells.shape[0], 1024), jnp.bfloat16),
            pltpu.VMEM((2, second_cells.shape[0], 256), jnp.float32),
        ),
        flops=2 * (24 * 1024 * 2048 + 24 * 2048 * 1024 + 96 * 1024 * 512),
    )
    return decoded.reshape(fields.shape)


def solution(mesh):
    in_specs = (
        P("lat", None, "lon", None),
        P("lat", "lon"),
        P(),
        P(),
        P(),
        P(),
        P("lat", None),
        P(),
        P("lat", None),
        P(),
        P(None, "lat"),
        P(),
        P(None, None, "lat"),
        P("lat", None),
        P("lat", None),
        P("lat", None),
    )
    out_specs = P("lat", None, "lon", None)
    return jax.shard_map(
        on_device, mesh=mesh, in_specs=in_specs, out_specs=out_specs, check_vma=False
    )
```
